128 devices in a mesh: ctx: 8 (over y_lo, x), wsh: 16 (over z, y_hi, core).
Axes of the slice: x: 4, y: 4 (y_hi: 2, y_lo: 2; y = y_hi * 2 + y_lo), z: 4, core: 2. Of those that a mesh axis runs over, the one named last changes fastest.
Arguments:
- tokens: bfloat16 [16, 1024, 1024], P('wsh', 'ctx'), may hold values from -6 to 6
- gain_attn: bfloat16 [1024], P('wsh'), may hold values from 0.5 to 1.5
- w_query: bfloat16 [1024, 1024], P('wsh'), may hold values from -0.1875 to 0.1875
- w_key: bfloat16 [1024, 512], P('wsh'), may hold values from -0.1875 to 0.1875
- w_value: bfloat16 [1024, 512], P('wsh'), may hold values from -0.1875 to 0.1875
- w_output: bfloat16 [1024, 1024], P('wsh'), may hold values from -1 to 1
- gain_moe: bfloat16 [1024], P('wsh'), may hold values from 0.5 to 1.5
- w_router: bfloat16 [1024, 32], P('wsh'), may hold values from -0.09375 to 0.09375
- w_in: bfloat16 [32, 1024, 1024], P('wsh'), may hold values from -0.1875 to 0.1875
- w_out: bfloat16 [32, 1024, 512], P('wsh'), may hold values from -1 to 1
- routes: int32 [16, 8, 128, 8], P('wsh', 'ctx'), may hold values from 0 to 31, all different within a row; in each aligned block of 128 rows (0 to 127, 128 to 255, ..., all dimensions but the last counted through in order) at most 64 rows name the same one
- cotangent: bfloat16 [16, 1024, 1024], P('wsh', 'ctx'), may hold values from -6 to 6
Outputs:
- output: bfloat16 [16, 1024, 1024], P('wsh', 'ctx')
- tokens_grad: bfloat16 [16, 1024, 1024], P('wsh', 'ctx')
- gain_attn_grad: float32 [1024], P('wsh')
- w_query_grad: float32 [1024, 1024], P('wsh')
- w_key_grad: float32 [1024, 512], P('wsh')
- w_value_grad: float32 [1024, 512], P('wsh')
- w_output_grad: float32 [1024, 1024], P('wsh')
- gain_moe_grad: float32 [1024], P('wsh')
- w_router_grad: float32 [1024, 32], P('wsh')
- w_in_grad: float32 [32, 1024, 1024], P('wsh', 'ctx')
- w_out_grad: float32 [32, 1024, 512], P('wsh', 'ctx')
The draws below stay inside these ranges and needn't reach their ends.
Inputs may be any that keep to these rules, and one draw needn't show every extreme that they name: `routes`: each row names 8 different experts; in the rows of one device (aligned blocks of 128 rows in array order) no expert is named more than 64 times, a bound that some block reaches.
All inputs are finite; a program needn't handle non-finite values.
Results may differ from the reference program's by a relative error of at most 0.025.
Values may be sent and summed in bfloat16 or wider, within the bound.
A program may use at most 192 MiB of HBM per device.

```python
import math
from functools import partial
import jax
import jax.numpy as jnp
import numpy as np
from jax import lax

D = 1024
HEADS = 16
KV_HEADS = 8
DH = 64
EXPERTS = 32
FF = 512
TOPK = 8
SEQ = 1024
SEQS = 1
CT = 128
TD = 128
CAP = 64
NSEQ = 16
N_CTX = 8
N_WSH = 16


def block_scale(own_key, dims, cuts, low, top_value):
    gain = 1.0
    for position, shards_of in cuts:
        steps = jax.random.uniform(jax.random.fold_in(jax.random.fold_in(own_key, 6), position), (shards_of,), jnp.float32, low / len(cuts), top_value / len(cuts))
        gain = gain * jnp.repeat(jnp.exp(steps), dims[position] // shards_of).reshape((-1,) + (1,) * (len(dims) - 1 - position))
    return gain


def assign_block(own_key, own, number, rows, number_of, top, bound, skew):
    order = jax.random.permutation(own_key, number_of)
    packed, ordinary = shares(number_of, rows * top, bound, skew, True), shares(number_of, rows * top, bound, skew, False)
    places = jnp.arange(number_of)

    def named(sizes, rotation):
        used = int((sizes > 0).sum())
        fixed = max(1, used // 4)
        passed = fixed + (places - fixed + rotation * (used - fixed)) % max(1, number_of - fixed)
        return jnp.zeros((number_of,), jnp.int32).at[order[jnp.where(places < fixed, places, passed)]].set(jnp.asarray(sizes, jnp.int32))

    sizes = jnp.where(number % 4 == 0, named(packed, number // 4), named(ordinary, number - number // 4 - 1))
    mixed = jax.random.permutation(jax.random.fold_in(own, 3), number_of)
    donor, receiver = mixed[0:number_of // 2 * 2:2], mixed[1:number_of // 2 * 2:2]
    room = jnp.minimum(sizes[donor] - 1, bound - sizes[receiver]) // 2
    room = jnp.where((donor == order[0]) | (receiver == order[0]) | (sizes[receiver] == 0), 0, jnp.maximum(room, 0))
    passed = jax.random.randint(jax.random.fold_in(own, 4), (number_of // 2,), 0, 1 << 20) % (room + 1)
    sizes = sizes.at[donor].add(-passed).at[receiver].add(passed)
    members = jnp.searchsorted(jnp.cumsum(sizes), jnp.arange(rows * top), side="right").astype(jnp.int32)
    table = members.reshape(top, rows).T
    table = table[jax.random.permutation(jax.random.fold_in(own, 1), rows)]
    rotation = jax.random.randint(jax.random.fold_in(own, 2), (rows, 1), 0, top)
    return jnp.take_along_axis(table, (jnp.arange(top)[None, :] + rotation) % top, axis=1)


def shares(count, total, limit, slope, full):
    weights = [(1 << 20) // math.isqrt(rank ** slope) + 1 for rank in range(1, count + 1)]
    largest = limit if full else min(limit, max(-(-total // count), total * weights[0] // sum(weights)))
    least = 1 if total - largest >= count - 1 else 0
    counts, rest = [largest] + [least] * (count - 1), total - largest - least * (count - 1)
    while rest > 0:
        free = [i for i in range(1, count) if counts[i] < largest] or [i for i in range(1, count) if counts[i] < limit]
        pool, remaining = sum([weights[i] for i in free]), rest
        for i in free:
            extra = min(limit - counts[i], max(1, remaining * weights[i] // pool), rest)
            counts[i] = counts[i] + extra
            rest = rest - extra
    return np.array(counts)


def gaussian(key, extent, width, limit, split=(), kind=jnp.bfloat16):
    level = block_scale(key, extent, split, -0.22, 0.18) if split else 1.0
    array = jax.random.normal(key, extent, jnp.float32) * width * level
    return jnp.minimum(jnp.maximum(array, -limit), limit).astype(kind)


def setup_inputs(seed: int = 0) -> dict:
    arg_keys = jax.random.split(jax.random.key(seed), 13)
    tokens = gaussian(arg_keys[0], (NSEQ, SEQ, D), 1.0, 6.0, ((0, 16), (1, 8)))
    gain_attn = jnp.clip(1.0 + 0.1 * jax.random.normal(arg_keys[1], (D,), jnp.float32), 0.5, 1.5).astype(jnp.bfloat16)
    w_query = gaussian(arg_keys[2], (D, HEADS * DH), D ** -0.5, 0.1875, ((0, 16),))
    w_key = gaussian(arg_keys[3], (D, KV_HEADS * DH), D ** -0.5, 0.1875, ((0, 16),))
    w_value = gaussian(arg_keys[4], (D, KV_HEADS * DH), D ** -0.5, 0.1875, ((0, 16),))
    w_output = gaussian(arg_keys[5], (HEADS * DH, D), (HEADS * DH // 32) ** -0.5, 1.0, ((0, 16),))
    gain_moe = jnp.clip(1.0 + 0.1 * jax.random.normal(arg_keys[6], (D,), jnp.float32), 0.5, 1.5).astype(jnp.bfloat16)
    w_router = gaussian(arg_keys[7], (D, EXPERTS), (4 * D) ** -0.5, 0.09375, ((0, 16),))
    w_in = gaussian(arg_keys[8], (EXPERTS, 2 * FF, D), D ** -0.5, 0.1875, ((0, 16),))
    w_out = gaussian(arg_keys[9], (EXPERTS, D, FF), (FF // 16) ** -0.5, 1.0, ((0, 16),))
    routes_keys = jax.random.split(jax.random.fold_in(arg_keys[10], 1), N_WSH * N_CTX * TD // TD)
    routes_turns = jax.random.permutation(jax.random.fold_in(arg_keys[10], 3), N_WSH * N_CTX * TD // TD)
    routes = jax.vmap(lambda own, number: assign_block(jax.random.fold_in(arg_keys[10], 2), own, number, TD, EXPERTS, TOPK, CAP, 1))(routes_keys, routes_turns).reshape((N_WSH, N_CTX, TD, TOPK))
    cotangent = gaussian(arg_keys[11], (NSEQ, SEQ, D), 1.0, 6.0, ((0, 16), (1, 8)))
    return {"tokens": tokens, "gain_attn": gain_attn, "w_query": w_query, "w_key": w_key, "w_value": w_value, "w_output": w_output, "gain_moe": gain_moe, "w_router": w_router, "w_in": w_in, "w_out": w_out, "routes": routes, "cotangent": cotangent}


@jax.custom_vjp
def low(v):
    return lax.optimization_barrier(v.astype(jnp.bfloat16)).astype(jnp.float32)

@jax.custom_vjp
def low_back(v):
    return v

def low_keep(v):
    return (low(v), None)

def low_pass(kept, grad):
    return (grad,)

def back_keep(v):
    return (v, None)

def back_low(kept, grad):
    return (low(grad),)
low.defvjp(low_keep, low_pass)
low_back.defvjp(back_keep, back_low)
epsilon = 1e-05
rope_base = 10000.0
masked_score = -1e+30
full_precision = lax.Precision.HIGHEST

def product(left, right):
    return jnp.dot(left, right, precision=full_precision, preferred_element_type=jnp.float32)

def rms_scale(token_rows):
    return lax.rsqrt(lax.optimization_barrier(jnp.mean(token_rows * token_rows, -1, keepdims=True)) + epsilon)

def rope_tables(positions, head_width):
    half_width = head_width // 2
    frequencies = rope_base ** (-jnp.arange(half_width, dtype=jnp.float32) * 2.0 / head_width)
    angles = positions[:, None] * frequencies[None, :]
    cosine_table = jnp.cos(angles)
    sine_table = jnp.sin(angles)
    return (jnp.concatenate([cosine_table, cosine_table], -1), jnp.concatenate([sine_table, sine_table], -1))

def rotate(values, cosine_table, sine_table):
    half_width = values.shape[-1] // 2
    turned = jnp.concatenate([-values[..., half_width:], values[..., :half_width]], -1)
    return values * cosine_table[:, None, :] + turned * sine_table[:, None, :]

def attend(operand):
    queries, key_rows, value_rows = operand
    raw_scores = low_back(jnp.einsum('tgrd,jgd->grtj', queries, key_rows, precision=full_precision))
    scores = raw_scores * DH ** (-0.5)
    positions = jnp.arange(SEQ, dtype=jnp.int32)
    visible = positions[None, :] <= positions[:, None]
    scores = jnp.where(visible, scores, masked_score)
    row_max = lax.optimization_barrier(jnp.max(scores, -1, keepdims=True))
    logsum = row_max + jnp.log(lax.optimization_barrier(jnp.sum(jnp.exp(scores - row_max), -1, keepdims=True)))
    attention = low(jnp.exp(scores - logsum))
    return jnp.einsum('grtj,jgd->tgrd', attention, value_rows, precision=full_precision)

def slot_of(chosen_ids):
    flat_ids = chosen_ids.reshape(-1)
    matches = (flat_ids[:, None] == jnp.arange(EXPERTS, dtype=jnp.int32)[None, :]).astype(jnp.int32)
    earlier = jnp.cumsum(matches, 0) - matches
    return flat_ids * CAP + lax.optimization_barrier(jnp.sum(earlier * matches, 1))

def expert_block(w_in, w_out, operand):
    token_rows, logits, chosen_ids = operand
    chosen = jnp.take_along_axis(logits, chosen_ids, 1)
    row_max = lax.optimization_barrier(jnp.max(chosen, -1, keepdims=True))
    raised = jnp.exp(chosen - row_max)
    gate_weights = raised / lax.optimization_barrier(jnp.sum(raised, -1, keepdims=True))
    slot_index = slot_of(chosen_ids)
    copies = low_back(jnp.repeat(token_rows, TOPK, axis=0))
    buffer = jnp.zeros((EXPERTS * CAP, D), token_rows.dtype).at[slot_index].set(copies).reshape(EXPERTS, CAP, D)
    projected = low_back(jnp.einsum('ecd,efd->ecf', buffer, w_in, precision=full_precision))
    hidden = low(jax.nn.silu(projected[..., :FF]) * projected[..., FF:])
    produced = low(low_back(jnp.einsum('ecf,edf->ecd', hidden, w_out, precision=full_precision)))
    picked = produced.reshape(EXPERTS * CAP, D)[slot_index].reshape(TD, TOPK, D)
    return lax.optimization_barrier(jnp.sum(gate_weights[..., None] * picked, 1))

def to_blocks(token_rows):
    model_width = token_rows.shape[-1]
    arranged = token_rows.reshape(N_WSH, SEQS, N_CTX, CT, model_width)
    return arranged.transpose(0, 2, 1, 3, 4).reshape(N_WSH * N_CTX, TD, model_width)

def from_blocks(blocks):
    model_width = blocks.shape[-1]
    arranged = blocks.reshape(N_WSH, N_CTX, SEQS, CT, model_width)
    return arranged.transpose(0, 2, 1, 3, 4).reshape(NSEQ * SEQ, model_width)

def forward(chosen_ids, tokens, gain_attn, w_query, w_key, w_value, w_output, gain_moe, w_router, w_in, w_out):
    token_rows = tokens.reshape(NSEQ * SEQ, D)
    normed_attn = low(token_rows * rms_scale(token_rows) * gain_attn)
    query_pre = low_back(product(normed_attn, w_query))
    key_pre = low_back(product(normed_attn, w_key))
    value_pre = low_back(product(normed_attn, w_value))
    cosine_table, sine_table = rope_tables(jnp.arange(SEQ).astype(tokens.dtype), DH)
    queries = low(rotate(query_pre.reshape(NSEQ, SEQ, HEADS, DH), cosine_table, sine_table))
    key_rows = low(rotate(key_pre.reshape(NSEQ, SEQ, KV_HEADS, DH), cosine_table, sine_table))
    value_rows = low(value_pre.reshape(NSEQ, SEQ, KV_HEADS, DH))
    grouped = queries.reshape(NSEQ, SEQ, KV_HEADS, HEADS // KV_HEADS, DH)
    attended = lax.map(jax.checkpoint(attend), (grouped, key_rows, value_rows))
    merged = low(low_back(attended.reshape(NSEQ * SEQ, HEADS * DH)))
    residual = token_rows + low_back(product(merged, w_output))
    normed_moe = low(residual * rms_scale(residual) * gain_moe)
    logits = product(normed_moe, w_router)
    expert_sum = lax.map(jax.checkpoint(partial(expert_block, w_in, w_out)), (to_blocks(normed_moe), to_blocks(logits), chosen_ids))
    return (residual + from_blocks(expert_sum)).reshape(NSEQ, SEQ, D)

def reference(tokens, gain_attn, w_query, w_key, w_value, w_output, gain_moe, w_router, w_in, w_out, routes, cotangent):
    primals = [operand.astype(jnp.float32) for operand in (tokens, gain_attn, w_query, w_key, w_value, w_output, gain_moe, w_router, w_in, w_out)]
    chosen_ids = routes.reshape(N_WSH * N_CTX, TD, TOPK)
    output, pullback = jax.vjp(partial(forward, chosen_ids), *primals)
    gradients = pullback(cotangent.astype(jnp.float32))
    return (output.astype(jnp.bfloat16), gradients[0].astype(jnp.bfloat16), gradients[1], gradients[2], gradients[3], gradients[4], gradients[5], gradients[6], gradients[7], gradients[8], gradients[9])
```

```python
import functools

import jax
import jax.numpy as jnp
from jax import lax
from jax.experimental import pallas as pl
from jax.experimental.pallas import tpu as pltpu
from jax.sharding import PartitionSpec as P

MESH = pl.DeviceIdType.MESH
F32 = jnp.float32
BF16 = jnp.bfloat16
DH = 64
EPS = 1e-05
ROPE_BASE = 10000.0
MASKED = -1e30
VMEM = pl.BlockSpec(memory_space=pltpu.VMEM)
NT = (((1,), (1,)), ((), ()))
TN = (((0,), (0,)), ((), ()))


def dot(a, b, dims=(((1,), (0,)), ((), ()))):
    return lax.dot_general(a, b, dims, preferred_element_type=F32)


def wsh_place():
    w = lax.axis_index("wsh")
    return w // 4, (w // 2) % 2, w % 2


def wsh_slot(a, b, core):
    return (a * 2 + b) * 2 + core


def wsh_device(a, b, core):
    return (lax.axis_index("ctx"), wsh_slot(a, b, core))


def ctx_place():
    c = lax.axis_index("ctx")
    return c % 4, c // 4


def ctx_slot(a, b):
    return b * 4 + a


def ctx_device(a, b):
    return (ctx_slot(a, b), lax.axis_index("wsh"))


def around(a, step):
    return lax.rem(a + step, 4)


def greet(peers):
    barrier = pltpu.get_barrier_semaphore()
    for peer in peers:
        pl.semaphore_signal(barrier, inc=1, device_id=peer, device_id_type=MESH)
    pl.semaphore_wait(barrier, len(peers))


def remote(src, dst, send, recv, k, device):
    return pltpu.make_async_remote_copy(
        src_ref=src,
        dst_ref=dst,
        send_sem=send.at[k],
        recv_sem=recv.at[k],
        device_id=device,
        device_id_type=MESH,
    )


def wsh_peers():
    a, b, core = wsh_place()
    return [
        wsh_device(around(a, 1), b, core),
        wsh_device(around(a, 3), b, core),
        wsh_device(around(a, 2), b, core),
        wsh_device(a, 1 - b, core),
        wsh_device(a, b, 1 - core),
    ]


def ctx_peers():
    a, b = ctx_place()
    return [
        ctx_device(around(a, 1), b),
        ctx_device(around(a, 3), b),
        ctx_device(around(a, 2), b),
        ctx_device(a, 1 - b),
    ]


def gather_steps(full, slot, device, a, b, send, recv, arrived):
    up, down, far = around(a, 1), around(a, 3), around(a, 2)
    other = 1 - b

    def push(k, sa, sb, to):
        at = full.at[slot(sa, sb)]
        copy = remote(at, at, send, recv, k, to)
        copy.start()
        return copy

    def landed(k, sa, sb):
        at = full.at[slot(sa, sb)]
        remote(at, at, send, recv, k, device(a, b)).wait_recv()
        arrived(k, sa, sb)

    sent = [
        push(3, a, b, device(a, other)),
        push(0, a, b, device(up, b)),
        push(1, a, b, device(down, b)),
        push(2, a, b, device(far, b)),
    ]
    landed(3, a, other)
    sent.append(push(4, a, other, device(up, b)))
    sent.append(push(5, a, other, device(down, b)))
    landed(0, down, b)
    landed(1, up, b)
    landed(2, far, b)
    sent.append(push(6, far, b, device(a, other)))
    landed(4, down, other)
    landed(5, up, other)
    landed(6, far, other)
    for copy in sent:
        copy.wait_send()


def gather_wsh(x, cid):
    rows, cols = x.shape

    def kernel(x_ref, full, send, recv, send_c, recv_c):
        a, b, core = wsh_place()
        greet(wsh_peers())
        full[wsh_slot(a, b, core)] = x_ref[...]
        slot = lambda sa, sb: wsh_slot(sa, sb, core)
        handed = []

        def hand(k, sa, sb):
            at = full.at[wsh_slot(sa, sb, core)]
            copy = remote(at, at, send_c, recv_c, k, wsh_device(a, b, 1 - core))
            copy.start()
            handed.append((copy, k, sa, sb))

        hand(7, a, b)
        gather_steps(full, slot, lambda sa, sb: wsh_device(sa, sb, core), a, b, send, recv, hand)
        for copy, k, sa, sb in handed:
            copy.wait_send()
            at = full.at[wsh_slot(sa, sb, 1 - core)]
            remote(at, at, send_c, recv_c, k, wsh_device(a, b, 1 - core)).wait_recv()

    return pl.pallas_call(
        kernel,
        out_shape=jax.ShapeDtypeStruct((16, rows, cols), x.dtype),
        in_specs=[VMEM],
        out_specs=VMEM,
        scratch_shapes=[pltpu.SemaphoreType.DMA((7,))] * 2 + [pltpu.SemaphoreType.DMA((8,))] * 2,
        compiler_params=pltpu.CompilerParams(
            collective_id=cid, has_side_effects=True, vmem_limit_bytes=32 << 20
        ),
        name="gather_wsh",
    )(x)


def gather_ctx(x, cid):
    rows, cols = x.shape

    def kernel(x_ref, full, send, recv):
        a, b = ctx_place()
        greet(ctx_peers())
        full[ctx_slot(a, b)] = x_ref[...]
        gather_steps(full, ctx_slot, ctx_device, a, b, send, recv, lambda *_: None)

    return pl.pallas_call(
        kernel,
        out_shape=jax.ShapeDtypeStruct((8, rows, cols), x.dtype),
        in_specs=[VMEM],
        out_specs=VMEM,
        scratch_shapes=[pltpu.SemaphoreType.DMA((7,))] * 2,
        compiler_params=pltpu.CompilerParams(
            collective_id=cid, has_side_effects=True, vmem_limit_bytes=32 << 20
        ),
        name="gather_ctx",
    )(x)


def scatter_steps(acc, land, slot, device, a, b, send, recv, ready, add):
    up, down, far = around(a, 1), around(a, 3), around(a, 2)
    other = 1 - b

    def push(k, sa, sb, to):
        copy = remote(acc.at[slot(sa, sb)], land.at[k], send, recv, k, to)
        copy.start()
        return copy

    def landed(k, sa, sb):
        remote(acc.at[slot(sa, sb)], land.at[k], send, recv, k, device(a, b)).wait_recv()
        add(sa, sb, k)

    sent = []
    ready(far, other)
    sent.append(push(0, far, other, device(a, other)))
    ready(up, other)
    sent.append(push(1, up, other, device(up, b)))
    ready(down, other)
    sent.append(push(2, down, other, device(down, b)))
    ready(up, b)
    sent.append(push(3, up, b, device(up, b)))
    ready(down, b)
    sent.append(push(4, down, b, device(down, b)))
    ready(far, b)
    landed(0, far, b)
    sent.append(push(5, far, b, device(far, b)))
    ready(a, other)
    landed(1, a, other)
    landed(2, a, other)
    sent.append(push(6, a, other, device(a, other)))
    ready(a, b)
    landed(3, a, b)
    landed(4, a, b)
    landed(5, a, b)
    landed(6, a, b)
    for copy in sent:
        copy.wait_send()


def wsh_sum_body(p_ref, acc, land, land_c, send, recv, send_c, recv_c):
    a, b, core = wsh_place()
    slot = lambda sa, sb: sa * 2 + sb
    far, up, down = around(a, 2), around(a, 1), around(a, 3)
    order = [(far, 1 - b), (up, 1 - b), (down, 1 - b), (up, b), (down, b), (far, b), (a, 1 - b), (a, b)]
    handed = []
    for k, (sa, sb) in enumerate(order):
        copy = remote(
            p_ref.at[slot(sa, sb), 1 - core],
            land_c.at[k],
            send_c,
            recv_c,
            k,
            wsh_device(a, b, 1 - core),
        )
        copy.start()
        handed.append(copy)
    count = [0]

    def ready(sa, sb):
        k = count[0]
        count[0] += 1
        handed[k].wait_recv()
        at = slot(sa, sb)
        acc[at] = (p_ref[at, core].astype(F32) + land_c[k].astype(F32)).astype(acc.dtype)

    def add(sa, sb, k):
        at = slot(sa, sb)
        acc[at] = (acc[at].astype(F32) + land[k].astype(F32)).astype(acc.dtype)

    scatter_steps(acc, land, slot, lambda sa, sb: wsh_device(sa, sb, core), a, b, send, recv, ready, add)
    for copy in handed:
        copy.wait_send()
    return slot(a, b)


def sum_wsh(p, cid):
    _, rows, cols = p.shape

    def kernel(p_ref, o_ref, acc, land, land_c, send, recv, send_c, recv_c):
        greet(wsh_peers())
        own = wsh_sum_body(p_ref, acc, land, land_c, send, recv, send_c, recv_c)
        o_ref[...] = acc[own]

    return pl.pallas_call(
        kernel,
        out_shape=jax.ShapeDtypeStruct((rows, cols), BF16),
        in_specs=[VMEM],
        out_specs=VMEM,
        scratch_shapes=[
            pltpu.VMEM((8, rows, cols), BF16),
            pltpu.VMEM((7, rows, cols), BF16),
            pltpu.VMEM((8, rows, cols), BF16),
        ]
        + [pltpu.SemaphoreType.DMA((7,))] * 2
        + [pltpu.SemaphoreType.DMA((8,))] * 2,
        compiler_params=pltpu.CompilerParams(
            collective_id=cid, has_side_effects=True, vmem_limit_bytes=48 << 20
        ),
        name="sum_wsh",
    )(p.reshape(8, 2, rows, cols))


def sum_ctx(p, cid):
    _, rows, cols = p.shape

    def kernel(p_ref, o_ref, acc, land, send, recv):
        a, b = ctx_place()
        greet(ctx_peers())

        def ready(sa, sb):
            at = ctx_slot(sa, sb)
            acc[at] = p_ref[at]

        def add(sa, sb, k):
            at = ctx_slot(sa, sb)
            acc[at] = (acc[at].astype(F32) + land[k].astype(F32)).astype(acc.dtype)

        scatter_steps(acc, land, ctx_slot, ctx_device, a, b, send, recv, ready, add)
        o_ref[...] = acc[ctx_slot(a, b)]

    return pl.pallas_call(
        kernel,
        out_shape=jax.ShapeDtypeStruct((rows, cols), p.dtype),
        in_specs=[VMEM],
        out_specs=VMEM,
        scratch_shapes=[
            pltpu.VMEM((8, rows, cols), p.dtype),
            pltpu.VMEM((7, rows, cols), p.dtype),
        ]
        + [pltpu.SemaphoreType.DMA((7,))] * 2,
        compiler_params=pltpu.CompilerParams(
            collective_id=cid, has_side_effects=True, vmem_limit_bytes=32 << 20
        ),
        name="sum_ctx",
    )(p)


def sum_all(p, cid):
    _, rows, cols = p.shape
    part = rows // 8

    def kernel(p_ref, o_ref, acc, land, land_c, acc2, land2, *sems):
        send, recv, send_c, recv_c, send2, recv2, send3, recv3 = sems
        greet(wsh_peers() + ctx_peers())
        own = wsh_sum_body(p_ref, acc, land, land_c, send, recv, send_c, recv_c)
        a, b = ctx_place()
        acc2[...] = acc[own].astype(F32).reshape(8, part, cols)

        def add(sa, sb, k):
            acc2[ctx_slot(sa, sb)] += land2[k]

        scatter_steps(
            acc2, land2, ctx_slot, ctx_device, a, b, send2, recv2, lambda *_: None, add
        )
        o_ref[ctx_slot(a, b)] = acc2[ctx_slot(a, b)]
        gather_steps(o_ref, ctx_slot, ctx_device, a, b, send3, recv3, lambda *_: None)

    out = pl.pallas_call(
        kernel,
        out_shape=jax.ShapeDtypeStruct((8, part, cols), F32),
        in_specs=[VMEM],
        out_specs=VMEM,
        scratch_shapes=[
            pltpu.VMEM((8, rows, cols), BF16),
            pltpu.VMEM((7, rows, cols), BF16),
            pltpu.VMEM((8, rows, cols), BF16),
            pltpu.VMEM((8, part, cols), F32),
            pltpu.VMEM((7, part, cols), F32),
        ]
        + [pltpu.SemaphoreType.DMA((7,))] * 2
        + [pltpu.SemaphoreType.DMA((8,))] * 2
        + [pltpu.SemaphoreType.DMA((7,))] * 4,
        compiler_params=pltpu.CompilerParams(
            collective_id=cid, has_side_effects=True, vmem_limit_bytes=48 << 20
        ),
        name="sum_all",
    )(p.reshape(8, 2, rows, cols))
    return out.reshape(rows, cols)


def compute(kernel, outs, scratch=(), limit=48, name=None):
    return pl.pallas_call(
        kernel,
        out_shape=[jax.ShapeDtypeStruct(s, d) for s, d in outs],
        scratch_shapes=list(scratch),
        compiler_params=pltpu.CompilerParams(vmem_limit_bytes=limit << 20),
        name=name,
    )


def rms_scale(x):
    return lax.rsqrt(jnp.mean(x * x, -1, keepdims=True) + EPS)


def norm_back(u, x, scale):
    return scale * u - x * scale * scale * scale * jnp.mean(u * x, -1, keepdims=True)


def low_half(shape):
    return lax.broadcasted_iota(jnp.int32, shape, len(shape) - 1) % DH < DH // 2


def rotate(v, cos, sin):
    width = v.shape[-1]
    turned = jnp.where(
        low_half(v.shape), -pltpu.roll(v, width - DH // 2, 1), pltpu.roll(v, DH // 2, 1)
    )
    return v * cos + turned * sin


def unrotate(v, cos, sin):
    width = v.shape[-1]
    scaled = v * sin
    turned = jnp.where(
        low_half(v.shape), pltpu.roll(scaled, width - DH // 2, 1), -pltpu.roll(scaled, DH // 2, 1)
    )
    return v * cos + turned


def project_kernel(tok, w, cos, sin, normed_o, q_o, kv_o, misc_o):
    x = tok[...].astype(F32)
    misc = w[:, 2048:2176].astype(F32).T
    misc_o[...] = misc
    normed = (x * rms_scale(x) * misc[96:97]).astype(BF16)
    normed_o[...] = normed
    c, s = cos[...], sin[...]
    q = dot(normed, w[:, :1024])
    q_o[...] = rotate(q, c, s).astype(BF16)
    k = dot(normed, w[:, 1024:1536])
    kv_o[:, :512] = rotate(k, c[:, :512], s[:, :512]).astype(BF16)
    kv_o[:, 512:] = dot(normed, w[:, 1536:2048]).astype(BF16)


def two_heads(ref, g):
    return jnp.concatenate(
        [ref[:, g * 128 : g * 128 + 64], ref[:, g * 128 + 64 : g * 128 + 128]], 0
    )


def side_by_side(rows):
    return jnp.concatenate([rows[:128], rows[128:]], 1)


def visible_mask():
    row = lax.broadcasted_iota(jnp.int32, (256, 1024), 0) % 128
    col = lax.broadcasted_iota(jnp.int32, (256, 1024), 1)
    return col <= row + lax.axis_index("ctx") * 128


def attend_kernel(q, kv, tok, wo, misc, merged_o, mid_o, normed_o, lse_o):
    visible = visible_mask()
    for g in range(8):
        keys = kv[:, g * 64 : g * 64 + 64]
        values = kv[:, 512 + g * 64 : 512 + g * 64 + 64]
        scores = jnp.where(visible, dot(two_heads(q, g), keys, NT) * DH**-0.5, MASKED)
        top = jnp.max(scores, -1, keepdims=True)
        raised = jnp.exp(scores - top)
        total = jnp.sum(raised, -1, keepdims=True)
        lse_o[g] = top + jnp.log(total)
        probs = (raised * (1.0 / total)).astype(BF16)
        merged_o[:, g * 128 : g * 128 + 128] = side_by_side(dot(probs, values)).astype(BF16)
    mid = tok[...].astype(F32) + dot(merged_o[...], wo[...])
    mid_o[...] = mid
    normed_o[...] = (mid * rms_scale(mid) * misc[97:98, :]).astype(BF16)


def parts_of(v):
    high = v.astype(BF16)
    rest = v - high.astype(F32)
    middle = rest.astype(BF16)
    return high, middle, (rest - middle.astype(F32)).astype(BF16)


def experts_kernel(
    x, g, w_in, w_out, misc, mask, pay, wg, sel, buf, gbuf, gcol, ggcol, gp, hidden, gact, gcopy
):
    own = lax.axis_index("wsh") * 2
    tri = (
        lax.broadcasted_iota(jnp.int32, (128, 128), 0)
        < lax.broadcasted_iota(jnp.int32, (128, 128), 1)
    ).astype(BF16)
    router = misc[0:32, :].astype(BF16)
    experts = lax.broadcasted_iota(jnp.int32, (32, 128), 0)
    slots = lax.broadcasted_iota(jnp.int32, (64, 128), 0).astype(F32)

    def pick(s, _):
        rows = pl.ds(pl.multiple_of(s * 128, 128), 128)
        chosen = mask[s]
        logits = jnp.where(chosen > 0, dot(router, x[rows, :], NT), MASKED)
        raised = jnp.exp(logits - jnp.max(logits, 0, keepdims=True)) * chosen
        gates = raised / jnp.sum(raised, 0, keepdims=True)
        earlier = dot(chosen.astype(BF16), tri)
        place, gate = [], []
        for j in range(2):
            is_own = experts == own + j
            row = lambda v: jnp.sum(jnp.where(is_own, v, 0.0), 0, keepdims=True)
            hit = (slots == row(earlier)) & (row(chosen) > 0)
            place.append(hit.astype(F32))
            gate.append(jnp.sum(jnp.where(hit, row(gates), 0.0), 1, keepdims=True))
        both = jnp.concatenate(place, 0).astype(BF16)
        sel[s] = both
        xb = dot(both, x[rows, :]).astype(BF16)
        gb = dot(both, g[rows, :]).astype(BF16)
        at = pl.ds(pl.multiple_of(s * 64, 64), 64)
        for j in range(2):
            buf[j, at, :] = xb[j * 64 : j * 64 + 64]
            gbuf[j, at, :] = gb[j * 64 : j * 64 + 64]
            gcol[j, at, :] = gate[j]
        return _

    lax.fori_loop(0, 16, pick, 0)

    def tile(i, _):
        j = i // 4
        at = pl.ds(pl.multiple_of((i % 4) * 256, 256), 256)
        act = dot(buf[j, at, :], w_in[j], NT)
        gate, up = act[:, :512], act[:, 512:]
        s = jax.nn.sigmoid(gate)
        h = (gate * s * up).astype(BF16)
        hidden[j, at, :] = h
        produced = dot(h, w_out[j], NT).astype(BF16).astype(F32)
        gate_col = gcol[j, at, :]
        gr = gbuf[j, at, :].astype(F32)
        ggcol[j, at, :] = jnp.sum(gr * produced, 1, keepdims=True)
        gbuf[j, at, :] = (produced * gate_col).astype(BF16)
        gpt = (gr * gate_col).astype(BF16)
        gp[j, at, :] = gpt
        gh = dot(gpt, w_out[j])
        ga_gate = (gh * up * s * (1.0 + gate * (1.0 - s))).astype(BF16)
        ga_up = (gh * gate * s).astype(BF16)
        ga = jnp.concatenate([ga_gate, ga_up], 1)
        gact[j, at, :] = ga
        gcopy[j, at, :] = dot(ga, w_in[j]).astype(BF16)
        return _

    lax.fori_loop(0, 8, tile, 0)

    def weights(i, _):
        j = i // 4
        at = pl.ds(pl.multiple_of((i % 4) * 256, 256), 256)
        gi = dot(gact[j, :, at], buf[j], TN).astype(BF16)
        go = dot(gp[j, :, at], hidden[j], TN).astype(BF16)
        c = (i % 4) * 2
        for h in range(2):
            wg[c + h, j, :, :1024] = gi[h * 128 : h * 128 + 128]
            wg[c + h, j, :, 1024:] = go[h * 128 : h * 128 + 128]
        return _

    lax.fori_loop(0, 8, weights, 0)
    lane = lax.broadcasted_iota(jnp.int32, (64, 128), 1)

    def combine(s, _):
        at = pl.ds(pl.multiple_of(s * 64, 64), 64)
        both = sel[s]
        rows = lambda ref: jnp.concatenate([ref[0, at, :], ref[1, at, :]], 0)
        pay[s, :, :1024] = dot(both, rows(gbuf), TN).astype(BF16)
        pay[s, :, 1024:2048] = dot(both, rows(gcopy), TN).astype(BF16)
        cells = []
        for j in range(2):
            parts = parts_of(ggcol[j, at, :])
            cell = jnp.zeros((64, 128), F32)
            for n, part in enumerate(parts):
                cell = jnp.where(lane == own + j + 32 * n, part.astype(F32), cell)
            cells.append(cell.astype(BF16))
        pay[s, :, 2048:] = dot(both, jnp.concatenate(cells, 0), TN).astype(BF16)
        return _

    lax.fori_loop(0, 16, combine, 0)


def split_dot(a, b, dims):
    high = a.astype(BF16)
    rest = (a - high.astype(F32)).astype(BF16)
    return dot(high, b, dims) + dot(rest, b, dims)


def back_kernel(
    back, mid_r, cot, misc, mask, normed, merged, q, kv, lse, wo, cos, sin,
    out_o, gmid_o, gkv_o, gq_o, gwo_o, gmisc_o, gm, dkv,
):
    mid = mid_r[...]
    out_o[...] = (mid + back[:, :1024].astype(F32)).astype(BF16)
    cells = back[:, 2048:].astype(F32)
    ggates = cells[:, :32] + cells[:, 32:64] + cells[:, 64:96]
    router = misc[0:32, :].astype(BF16)
    chosen = mask[...]
    logits = jnp.where(chosen > 0, dot(normed[...], router, NT), MASKED)
    raised = jnp.exp(logits - jnp.max(logits, 1, keepdims=True)) * chosen
    gates = raised / jnp.sum(raised, 1, keepdims=True)
    glogits = gates * (ggates - jnp.sum(gates * ggates, 1, keepdims=True))
    scale = rms_scale(mid)
    gnormed = back[:, 1024:2048].astype(F32) + split_dot(glogits, router, (((1,), (0,)), ((), ())))
    gmisc_o[0:32, :] = split_dot(glogits, normed[...], TN)
    gmisc_o[32:33, :] = jnp.sum(gnormed * mid * scale, 0, keepdims=True)
    gmid = cot[...].astype(F32) + norm_back(gnormed * misc[97:98, :], mid, scale)
    gmid_o[...] = gmid
    branch = gmid.astype(BF16)
    gwo_o[...] = dot(merged[...], branch, TN).astype(BF16)
    gm[...] = dot(branch, wo[...], NT).astype(BF16)
    visible = visible_mask()
    gq = []
    for g in range(8):
        keys = kv[:, g * 64 : g * 64 + 64]
        values = kv[:, 512 + g * 64 : 512 + g * 64 + 64]
        queries, grads = two_heads(q, g), two_heads(gm, g)
        scores = jnp.where(visible, dot(queries, keys, NT) * DH**-0.5, MASKED)
        probs = jnp.exp(scores - lse[g])
        gprobs = dot(grads, values, NT)
        inner = jnp.sum(probs * gprobs, -1, keepdims=True)
        graw = (probs * (gprobs - inner) * DH**-0.5).astype(BF16)
        gq.append(side_by_side(dot(graw, keys)))
        dkv[g * 64 : g * 64 + 64, :] = dot(queries, graw, TN)
        dkv[512 + g * 64 : 512 + g * 64 + 64, :] = dot(grads, probs.astype(BF16), TN)
    gq_o[...] = unrotate(jnp.concatenate(gq, 1), cos[...], sin[...]).astype(BF16)
    for c in range(8):
        gkv_o[c] = dkv[:, c * 128 : c * 128 + 128].T.astype(BF16)


def finish_kernel(gkv, gq, normed, w, tok, gmid, cos, sin, misc, gwo, gmisc, tgrad_o, pack_o, gall):
    c, s = cos[:, :512], sin[:, :512]
    gall[:, :1024] = gq[...]
    gall[:, 1024:1536] = unrotate(gkv[:, :512].astype(F32), c, s).astype(BF16)
    gall[:, 1536:] = gkv[:, 512:]
    x = tok[...].astype(F32)
    scale = rms_scale(x)
    gnormed = dot(gall[...], w[:, :2048], NT)
    pack_o[:, :2048] = dot(normed[...], gall[...], TN).astype(BF16)
    pack_o[:, 2048:3072] = gwo[...]
    gain = jnp.sum(gnormed * x * scale, 0, keepdims=True)
    rows = jnp.concatenate([gmisc[0:33, :], gain, jnp.zeros((94, 1024), F32)], 0)
    pack_o[:, 3072:] = rows.T.astype(BF16)
    tgrad_o[...] = (gmid[...] + norm_back(gnormed * misc[96:97, :], x, scale)).astype(BF16)


def local(
    tokens, gain_attn, w_query, w_key, w_value, w_output, gain_moe, w_router, w_in, w_out, routes,
    cotangent,
):
    tok = tokens.reshape(128, 1024)
    cot = cotangent.reshape(128, 1024)
    chosen = routes.reshape(128, 8)
    own_mask = jnp.sum(
        (chosen[:, :, None] == jnp.arange(32, dtype=jnp.int32)).astype(F32), 1
    )
    low_mask = own_mask.astype(BF16)
    pack = jnp.concatenate(
        [
            w_query, w_key, w_value, w_router, low_mask[:64], low_mask[64:],
            gain_attn[:, None], gain_moe[:, None], jnp.zeros((64, 30), BF16),
        ],
        1,
    )
    wo = lax.all_gather(w_output, "wsh", axis=0, tiled=True)
    cot_all = lax.all_gather(cot, "wsh", axis=0, tiled=True)
    positions = (lax.axis_index("ctx") * 128 + jnp.arange(128, dtype=jnp.int32)).astype(F32)
    frequencies = ROPE_BASE ** (-jnp.arange(DH // 2, dtype=F32) * 2.0 / DH)
    angles = positions[:, None] * frequencies[None, :]
    cos = jnp.tile(jnp.cos(angles), (1, 32))
    sin = jnp.tile(jnp.sin(angles), (1, 32))

    w = gather_wsh(pack, 0).reshape(1024, 2176)
    t, d = 128, 1024
    normed, q, kv, misc = compute(
        project_kernel,
        [((t, d), BF16), ((t, d), BF16), ((t, d), BF16), ((128, d), F32)],
        name="project",
    )(tok, w, cos, sin)
    kv_all = gather_ctx(kv, 1).reshape(1024, 1024)
    merged, mid, normed_moe, lse = compute(
        attend_kernel,
        [((t, d), BF16), ((t, d), F32), ((t, d), BF16), ((8, 256, 1), F32)],
        name="attend",
    )(q, kv_all, tok, wo, misc)
    x_all = gather_wsh(normed_moe, 2).reshape(2048, 1024)
    mask = misc[32:96].reshape(2, 32, 16, 64).transpose(2, 1, 0, 3).reshape(16, 32, 128)
    e = 1024
    pay, wg = compute(
        experts_kernel,
        [((16, t, 2176), BF16), ((8, 2, 128, 1536), BF16)],
        [
            pltpu.VMEM((16, 128, 128), BF16),
            pltpu.VMEM((2, e, d), BF16),
            pltpu.VMEM((2, e, d), BF16),
            pltpu.VMEM((2, e, 1), F32),
            pltpu.VMEM((2, e, 1), F32),
            pltpu.VMEM((2, e, d), BF16),
            pltpu.VMEM((2, e, 512), BF16),
            pltpu.VMEM((2, e, d), BF16),
            pltpu.VMEM((2, e, d), BF16),
        ],
        limit=62,
        name="experts",
    )(x_all, cot_all, w_in, w_out, misc, mask)
    expert_grads = lax.psum_scatter(wg, "ctx", scatter_dimension=0, tiled=False).astype(F32)
    back = sum_wsh(pay, 3)
    output, gmid, gkv, gq, gwo, gmisc = compute(
        back_kernel,
        [
            ((t, d), BF16), ((t, d), F32), ((8, t, d), BF16), ((t, d), BF16), ((d, d), BF16),
            ((40, d), F32),
        ],
        [pltpu.VMEM((t, d), BF16), pltpu.VMEM((d, d), F32)],
        name="back",
    )(back, mid, cot, misc, own_mask, normed_moe, merged, q, kv_all, lse, wo, cos, sin)
    gkv_own = sum_ctx(gkv, 4)
    tokens_grad, packed = compute(
        finish_kernel,
        [((t, d), BF16), ((d, 3200), BF16)],
        [pltpu.VMEM((t, 2048), BF16)],
        name="finish",
    )(gkv_own, gq, normed, w, tok, gmid, cos, sin, misc, gwo, gmisc)
    sums = sum_all(packed.reshape(16, 64, 3200), 5)
    return (
        output.reshape(1, 128, 1024),
        tokens_grad.reshape(1, 128, 1024),
        sums[:, 3105],
        sums[:, :1024],
        sums[:, 1024:1536],
        sums[:, 1536:2048],
        sums[:, 2048:3072],
        sums[:, 3104],
        sums[:, 3072:3104],
        expert_grads[:, :, :1024],
        expert_grads[:, :, 1024:],
    )


def solution(mesh):
    return jax.shard_map(
        local,
        mesh=mesh,
        in_specs=(
            P("wsh", "ctx", None),
            P("wsh"),
            P("wsh", None),
            P("wsh", None),
            P("wsh", None),
            P("wsh", None),
            P("wsh"),
            P("wsh", None),
            P("wsh", None, None),
            P("wsh", None, None),
            P("wsh", "ctx", None, None),
            P("wsh", "ctx", None),
        ),
        out_specs=(
            P("wsh", "ctx", None),
            P("wsh", "ctx", None),
            P("wsh"),
            P("wsh", None),
            P("wsh", None),
            P("wsh", None),
            P("wsh", None),
            P("wsh"),
            P("wsh", None),
            P("wsh", "ctx", None),
            P("wsh", "ctx", None),
        ),
        check_vma=False,
    )
```

```python
import jax
import jax.numpy as jnp
from jax import lax
from jax.experimental import pallas as pl
from jax.experimental.pallas import tpu as pltpu
from jax.sharding import PartitionSpec as P

MESH = pl.DeviceIdType.MESH
F32 = jnp.float32
BF16 = jnp.bfloat16
DH = 64
EPS = 1e-05
ROPE_BASE = 10000.0
MASKED = -1e30
VMEM = pl.BlockSpec(memory_space=pltpu.VMEM)
NT = (((1,), (1,)), ((), ()))
TN = (((0,), (0,)), ((), ()))


def dot(a, b, dims=(((1,), (0,)), ((), ()))):
    return lax.dot_general(a, b, dims, preferred_element_type=F32)


def wsh_place():
    w = lax.axis_index("wsh")
    return w // 4, (w // 2) % 2, w % 2


def wsh_slot(a, b, core):
    return (a * 2 + b) * 2 + core


def wsh_device(a, b, core):
    return (lax.axis_index("ctx"), wsh_slot(a, b, core))


def ctx_place():
    c = lax.axis_index("ctx")
    return c % 4, c // 4


def ctx_slot(a, b):
    return b * 4 + a


def ctx_device(a, b):
    return (ctx_slot(a, b), lax.axis_index("wsh"))


def around(a, step):
    return lax.rem(a + step, 4)


def greet(peers):
    barrier = pltpu.get_barrier_semaphore()
    for peer in peers:
        pl.semaphore_signal(barrier, inc=1, device_id=peer, device_id_type=MESH)
    pl.semaphore_wait(barrier, len(peers))


def remote(src, dst, send, recv, k, device):
    return pltpu.make_async_remote_copy(
        src_ref=src,
        dst_ref=dst,
        send_sem=send.at[k],
        recv_sem=recv.at[k],
        device_id=device,
        device_id_type=MESH,
    )


def wsh_peers():
    a, b, core = wsh_place()
    return [
        wsh_device(around(a, 1), b, core),
        wsh_device(around(a, 3), b, core),
        wsh_device(around(a, 2), b, core),
        wsh_device(a, 1 - b, core),
        wsh_device(a, b, 1 - core),
    ]


def ctx_peers():
    a, b = ctx_place()
    return [
        ctx_device(around(a, 1), b),
        ctx_device(around(a, 3), b),
        ctx_device(around(a, 2), b),
        ctx_device(a, 1 - b),
    ]


def run(*plans):
    plans = list(plans)
    while plans:
        plans = [p for p in plans if next(p, "end") != "end"]


def gather_plan(full, slot, device, a, b, send, recv, arrived=lambda *_: None):
    up, down, far = around(a, 1), around(a, 3), around(a, 2)
    other = 1 - b

    def push(k, sa, sb, to):
        at = full.at[slot(sa, sb)]
        copy = remote(at, at, send, recv, k, to)
        copy.start()
        return copy

    def landed(k, sa, sb):
        at = full.at[slot(sa, sb)]
        remote(at, at, send, recv, k, device(a, b)).wait_recv()
        arrived(k, sa, sb)

    sent = [
        push(3, a, b, device(a, other)),
        push(0, a, b, device(up, b)),
        push(1, a, b, device(down, b)),
        push(2, a, b, device(far, b)),
    ]
    yield
    landed(3, a, other)
    sent.append(push(4, a, other, device(up, b)))
    sent.append(push(5, a, other, device(down, b)))
    yield
    landed(0, down, b)
    landed(1, up, b)
    yield
    landed(2, far, b)
    sent.append(push(6, far, b, device(a, other)))
    yield
    landed(4, down, other)
    landed(5, up, other)
    yield
    landed(6, far, other)
    for copy in sent:
        copy.wait_send()


def gather_wsh_plan(full, sems, after_same=lambda: None):
    send, recv, send_c, recv_c = sems
    a, b, core = wsh_place()
    handed = []

    def hand(k, sa, sb):
        at = full.at[wsh_slot(sa, sb, core)]
        copy = remote(at, at, send_c, recv_c, k, wsh_device(a, b, 1 - core))
        copy.start()
        handed.append((copy, k, sa, sb))

    def take(k, sa, sb):
        at = full.at[wsh_slot(sa, sb, 1 - core)]
        remote(at, at, send_c, recv_c, k, wsh_device(a, b, 1 - core)).wait_recv()

    hand(7, a, b)
    slot = lambda sa, sb: wsh_slot(sa, sb, core)
    steps = gather_plan(full, slot, lambda sa, sb: wsh_device(sa, sb, core), a, b, send, recv, hand)
    for count, _ in enumerate(steps):
        if count == 3:
            near = [h for h in handed if h[1] in (7, 0, 1, 2)]
            for _, k, sa, sb in near:
                take(k, sa, sb)
            after_same()
        yield
    for copy, k, sa, sb in handed:
        if k not in (7, 0, 1, 2):
            take(k, sa, sb)
        copy.wait_send()


WSH_SEMS = [pltpu.SemaphoreType.DMA((7,))] * 2 + [pltpu.SemaphoreType.DMA((8,))] * 2
CTX_SEMS = [pltpu.SemaphoreType.DMA((7,))] * 2


def talk(kernel, outs, scratch, cid, name, in_specs, out_specs=None, limit=48, flops=0):
    return pl.pallas_call(
        kernel,
        out_shape=[jax.ShapeDtypeStruct(s, d) for s, d in outs],
        in_specs=in_specs,
        out_specs=out_specs or [VMEM] * len(outs),
        scratch_shapes=list(scratch),
        compiler_params=pltpu.CompilerParams(
            collective_id=cid, has_side_effects=True, vmem_limit_bytes=limit << 20
        ),
        cost_estimate=pl.CostEstimate(
            flops=flops, bytes_accessed=1 << 20, transcendentals=0
        ),
        name=name,
    )


def gather_weights(x, cid):
    rows, cols = x.shape

    def kernel(x_ref, full, *sems):
        a, b, core = wsh_place()
        greet(wsh_peers())
        full[wsh_slot(a, b, core)] = x_ref[...]
        run(gather_wsh_plan(full, sems))

    return talk(
        kernel, [((16, rows, cols), BF16)], WSH_SEMS, cid, "gather_weights", [VMEM], flops=20 << 30
    )(x)[0]


def gather_sequence(kv, cot, wo, cid):
    def kernel(kv_r, cot_r, wo_r, kv_full, cot_full, wo_full, *sems):
        a, b, core = wsh_place()
        ca, cb = ctx_place()
        greet(wsh_peers() + ctx_peers())
        kv_full[ctx_slot(ca, cb)] = kv_r[...]
        wo_full[wsh_slot(a, b, core)] = wo_r[...]
        cot_full[wsh_slot(a, b, core)] = cot_r[...]
        run(
            gather_plan(kv_full, ctx_slot, ctx_device, ca, cb, *sems[:2]),
            gather_wsh_plan(wo_full, sems[2:6]),
            gather_wsh_plan(cot_full, sems[6:10]),
        )

    return talk(
        kernel,
        [((8, 128, 1024), BF16), ((16, 128, 1024), BF16), ((16, 64, 1024), BF16)],
        CTX_SEMS + WSH_SEMS * 2,
        cid,
        "gather_sequence",
        [VMEM] * 3,
        flops=25 << 30,
    )(kv, cot, wo)


def scatter_plan(acc, land, slot, device, a, b, send, recv, ready, add):
    up, down, far = around(a, 1), around(a, 3), around(a, 2)
    other = 1 - b

    def push(k, sa, sb, to):
        copy = remote(acc.at[slot(sa, sb)], land.at[k], send, recv, k, to)
        copy.start()
        return copy

    def landed(k, sa, sb):
        remote(acc.at[slot(sa, sb)], land.at[k], send, recv, k, device(a, b)).wait_recv()
        add(sa, sb, k)

    sent = []
    ready(up, other)
    sent.append(push(1, up, other, device(up, b)))
    ready(far, other)
    sent.append(push(0, far, other, device(a, other)))
    ready(down, other)
    sent.append(push(2, down, other, device(down, b)))
    ready(a, other)
    ready(up, b)
    sent.append(push(3, up, b, device(up, b)))
    ready(far, b)
    ready(down, b)
    sent.append(push(4, down, b, device(down, b)))
    ready(a, b)
    yield
    landed(0, far, b)
    sent.append(push(5, far, b, device(far, b)))
    yield
    landed(1, a, other)
    landed(2, a, other)
    sent.append(push(6, a, other, device(a, other)))
    yield
    landed(3, a, b)
    landed(4, a, b)
    yield
    landed(5, a, b)
    landed(6, a, b)
    for copy in sent:
        copy.wait_send()


def pair_slot(sa, sb):
    return sa * 2 + sb


def hand_step(k):
    a, b, _ = wsh_place()
    return lax.rem(a + k + 1, 4), lax.rem(b + 1 + k // 4, 2)


def hand_over(p_ref, land_c, send_c, recv_c, k):
    a, b, core = wsh_place()
    return remote(
        p_ref.at[pair_slot(*hand_step(k)), 1 - core],
        land_c.at[k],
        send_c,
        recv_c,
        k,
        wsh_device(a, b, 1 - core),
    )


def scatter_wsh_plan(p_ref, acc, land, land_c, sems, handed=False):
    send, recv, send_c, recv_c = sems
    a, b, core = wsh_place()
    copies = [hand_over(p_ref, land_c, send_c, recv_c, k) for k in range(8)]
    if not handed:
        for copy in copies:
            copy.start()
    count = [0]

    def ready(sa, sb):
        k = count[0]
        count[0] += 1
        copies[k].wait_recv()
        at = pair_slot(sa, sb)
        acc[at] = (p_ref[at, core].astype(F32) + land_c[k].astype(F32)).astype(acc.dtype)

    def add(sa, sb, k):
        at = pair_slot(sa, sb)
        acc[at] = (acc[at].astype(F32) + land[k].astype(F32)).astype(acc.dtype)

    device = lambda sa, sb: wsh_device(sa, sb, core)
    yield from scatter_plan(acc, land, pair_slot, device, a, b, send, recv, ready, add)
    for copy in copies:
        copy.wait_send()


def scatter_ctx_plan(p_ref, acc, land, sems):
    a, b = ctx_place()

    def ready(sa, sb):
        at = ctx_slot(sa, sb)
        acc[at] = p_ref[at]

    def add(sa, sb, k):
        at = ctx_slot(sa, sb)
        acc[at] = (acc[at].astype(F32) + land[k].astype(F32)).astype(acc.dtype)

    yield from scatter_plan(acc, land, ctx_slot, ctx_device, a, b, *sems, ready, add)


def wsh_land(rows, cols):
    return [
        pltpu.VMEM((8, rows, cols), BF16),
        pltpu.VMEM((7, rows, cols), BF16),
        pltpu.VMEM((8, rows, cols), BF16),
    ]


def sum_sequence(gkv, pay, cid):
    def kernel(gkv_r, pay_r, gkv_o, pay_o, kacc, kland, acc, land, land_c, *sems):
        greet(wsh_peers() + ctx_peers())
        run(
            scatter_ctx_plan(gkv_r, kacc, kland, sems[:2]),
            scatter_wsh_plan(pay_r, acc, land, land_c, sems[2:]),
        )
        a, b, _ = wsh_place()
        pay_o[...] = acc[pair_slot(a, b)]
        gkv_o[...] = kacc[lax.axis_index("ctx")]

    return talk(
        kernel,
        [((128, 1024), BF16), ((128, 1024), BF16)],
        [pltpu.VMEM((8, 128, 1024), BF16), pltpu.VMEM((7, 128, 1024), BF16)]
        + wsh_land(128, 1024)
        + CTX_SEMS
        + WSH_SEMS,
        cid,
        "sum_sequence",
        [VMEM] * 2,
        flops=25 << 30,
    )(gkv, pay.reshape(8, 2, 128, 1024))


def sum_all(p, cid):
    _, rows, cols = p.shape
    part = rows // 8

    def kernel(p_ref, o_ref, acc, land, land_c, acc2, land2, *sems):
        greet(wsh_peers() + ctx_peers())
        run(scatter_wsh_plan(p_ref, acc, land, land_c, sems[:4]))
        wa, wb, _ = wsh_place()
        acc2[...] = acc[pair_slot(wa, wb)].astype(F32).reshape(8, part, cols)
        a, b = ctx_place()

        def add(sa, sb, k):
            acc2[ctx_slot(sa, sb)] += land2[k]

        none = lambda *_: None
        run(scatter_plan(acc2, land2, ctx_slot, ctx_device, a, b, *sems[4:6], none, add))
        o_ref[ctx_slot(a, b)] = acc2[ctx_slot(a, b)]
        run(gather_plan(o_ref, ctx_slot, ctx_device, a, b, *sems[6:8]))

    return talk(
        kernel,
        [((8, part, cols), F32)],
        wsh_land(rows, cols)
        + [pltpu.VMEM((8, part, cols), F32), pltpu.VMEM((7, part, cols), F32)]
        + WSH_SEMS
        + CTX_SEMS * 2,
        cid,
        "sum_all",
        [VMEM],
        flops=50 << 30,
    )(p.reshape(8, 2, rows, cols))[0].reshape(rows, cols)


def compute(kernel, outs, scratch=(), limit=48, name=None):
    return pl.pallas_call(
        kernel,
        out_shape=[jax.ShapeDtypeStruct(s, d) for s, d in outs],
        scratch_shapes=list(scratch),
        compiler_params=pltpu.CompilerParams(vmem_limit_bytes=limit << 20),
        cost_estimate=pl.CostEstimate(flops=10 << 30, bytes_accessed=1 << 20, transcendentals=0),
        name=name,
    )


def rms_scale(x):
    return lax.rsqrt(jnp.mean(x * x, -1, keepdims=True) + EPS)


def norm_back(u, x, scale):
    return scale * u - x * scale * scale * scale * jnp.mean(u * x, -1, keepdims=True)


def low_half(shape):
    return lax.broadcasted_iota(jnp.int32, shape, len(shape) - 1) % DH < DH // 2


def rotate(v, cos, sin):
    width = v.shape[-1]
    turned = jnp.where(
        low_half(v.shape), -pltpu.roll(v, width - DH // 2, 1), pltpu.roll(v, DH // 2, 1)
    )
    return v * cos + turned * sin


def unrotate(v, cos, sin):
    width = v.shape[-1]
    scaled = v * sin
    turned = jnp.where(
        low_half(v.shape), pltpu.roll(scaled, width - DH // 2, 1), -pltpu.roll(scaled, DH // 2, 1)
    )
    return v * cos + turned


def project_kernel(tok, w, cos, sin, normed_o, q_o, kv_o, misc_o):
    x = tok[...].astype(F32)
    misc = w[:, 2048:2176].astype(F32).T
    misc_o[...] = misc
    normed = (x * rms_scale(x) * misc[96:97]).astype(BF16)
    normed_o[...] = normed
    c, s = cos[...], sin[...]
    q = dot(normed, w[:, :1024])
    q_o[...] = rotate(q, c, s).astype(BF16)
    k = dot(normed, w[:, 1024:1536])
    kv_o[:, :512] = rotate(k, c[:, :512], s[:, :512]).astype(BF16)
    kv_o[:, 512:] = dot(normed, w[:, 1536:2048]).astype(BF16)


def two_heads(ref, g):
    return jnp.concatenate(
        [ref[:, g * 128 : g * 128 + 64], ref[:, g * 128 + 64 : g * 128 + 128]], 0
    )


def side_by_side(rows):
    return jnp.concatenate([rows[:128], rows[128:]], 1)


def visible_mask():
    row = lax.broadcasted_iota(jnp.int32, (256, 1024), 0) % 128
    col = lax.broadcasted_iota(jnp.int32, (256, 1024), 1)
    return col <= row + lax.axis_index("ctx") * 128


def attend_kernel(q, kv, tok, wo, misc, merged_o, mid_o, normed_o, lse_o):
    visible = visible_mask()
    for g in range(8):
        keys = kv[:, g * 64 : g * 64 + 64]
        values = kv[:, 512 + g * 64 : 512 + g * 64 + 64]
        scores = jnp.where(visible, dot(two_heads(q, g), keys, NT) * DH**-0.5, MASKED)
        top = jnp.max(scores, -1, keepdims=True)
        raised = jnp.exp(scores - top)
        total = jnp.sum(raised, -1, keepdims=True)
        lse_o[g] = top + jnp.log(total)
        probs = (raised * (1.0 / total)).astype(BF16)
        merged_o[:, g * 128 : g * 128 + 128] = side_by_side(dot(probs, values)).astype(BF16)
    mid = tok[...].astype(F32) + dot(merged_o[...], wo[...])
    mid_o[...] = mid
    normed_o[...] = (mid * rms_scale(mid) * misc[97:98, :]).astype(BF16)


def parts_of(v):
    high = v.astype(BF16)
    rest = v - high.astype(F32)
    middle = rest.astype(BF16)
    return high, middle, (rest - middle.astype(F32)).astype(BF16)


def experts_kernel(
    x_r, cot, w_in_r, w_out_r, misc, mask, full, back_o, wg0, wg1, wg2, wg3,
    w_in, w_out, sel, buf, gbuf, gcol, ggcol, gp, hidden, gact, gcopy, pay, wg,
    acc, land, land_c, load, store, *sems,
):
    loads = [
        pltpu.make_async_copy(cot, gp, load.at[0]),
        pltpu.make_async_copy(w_in_r, w_in, load.at[1]),
        pltpu.make_async_copy(w_out_r, w_out, load.at[2]),
    ]
    for copy in loads:
        copy.start()
    wa, wb, core = wsh_place()
    ca, cb = ctx_place()
    own = lax.axis_index("wsh") * 2
    tri = (
        lax.broadcasted_iota(jnp.int32, (128, 128), 0)
        < lax.broadcasted_iota(jnp.int32, (128, 128), 1)
    ).astype(BF16)
    router = misc[0:32, :].astype(BF16)
    experts = lax.broadcasted_iota(jnp.int32, (32, 128), 0)
    slots = lax.broadcasted_iota(jnp.int32, (64, 128), 0).astype(F32)

    def pick(b):
        def one(i, _):
            s = wsh_slot(lax.rem(wa + i // 2, 4), b, i % 2)
            chosen = mask[s]
            x = full[s]
            logits = jnp.where(chosen > 0, dot(router, x, NT), MASKED)
            raised = jnp.exp(logits - jnp.max(logits, 0, keepdims=True)) * chosen
            gates = raised / jnp.sum(raised, 0, keepdims=True)
            earlier = dot(chosen.astype(BF16), tri)
            place, gate = [], []
            for j in range(2):
                is_own = experts == own + j
                row = lambda v: jnp.sum(jnp.where(is_own, v, 0.0), 0, keepdims=True)
                hit = (slots == row(earlier)) & (row(chosen) > 0)
                place.append(hit.astype(F32))
                gate.append(jnp.sum(jnp.where(hit, row(gates), 0.0), 1, keepdims=True))
            both = jnp.concatenate(place, 0).astype(BF16)
            sel[s] = both
            xb = dot(both, x).astype(BF16)
            gb = dot(both, gp[pl.ds(pl.multiple_of(s * 128, 128), 128), :]).astype(BF16)
            at = pl.ds(pl.multiple_of(s * 64, 64), 64)
            for j in range(2):
                buf[j, at, :] = xb[j * 64 : j * 64 + 64]
                gbuf[j, at, :] = gb[j * 64 : j * 64 + 64]
                gcol[j, at, :] = gate[j]
            return _

        lax.fori_loop(0, 8, one, 0)

    greet(wsh_peers())
    full[wsh_slot(wa, wb, core)] = x_r[...]

    def pick_same():
        loads[0].wait()
        pick(wb)

    run(gather_wsh_plan(full, sems[:4], pick_same))
    pick(1 - wb)
    loads[1].wait()
    loads[2].wait()

    def tile(i, _):
        j = i // 4
        at = pl.ds(pl.multiple_of((i % 4) * 256, 256), 256)
        flat = pl.ds(pl.multiple_of(i * 256, 256), 256)
        act = dot(buf[j, at, :], w_in[j], NT)
        gate, up = act[:, :512], act[:, 512:]
        s = jax.nn.sigmoid(gate)
        h = (gate * s * up).astype(BF16)
        hidden[j, at, :] = h
        produced = dot(h, w_out[j], NT).astype(BF16).astype(F32)
        gate_col = gcol[j, at, :]
        gr = gbuf[j, at, :].astype(F32)
        ggcol[j, at, :] = jnp.sum(gr * produced, 1, keepdims=True)
        gbuf[j, at, :] = (produced * gate_col).astype(BF16)
        gpt = (gr * gate_col).astype(BF16)
        gp[flat, :] = gpt
        gh = dot(gpt, w_out[j])
        ga_gate = (gh * up * s * (1.0 + gate * (1.0 - s))).astype(BF16)
        ga_up = (gh * gate * s).astype(BF16)
        ga = jnp.concatenate([ga_gate, ga_up], 1)
        gact[j, at, :] = ga
        gcopy[j, at, :] = dot(ga, w_in[j]).astype(BF16)
        return _

    lax.fori_loop(0, 8, tile, 0)
    lane = lax.broadcasted_iota(jnp.int32, (64, 128), 1)

    def rows(ref, s):
        at = pl.ds(pl.multiple_of(s * 64, 64), 64)
        return jnp.concatenate([ref[0, at, :], ref[1, at, :]], 0)

    def combine(k, _):
        sa, sb = hand_step(k)
        for c in range(2):
            s = wsh_slot(sa, sb, c)
            at = pl.ds(pl.multiple_of(s * 64, 64), 64)
            both = sel[s]
            pay[pair_slot(sa, sb), c, :, :1024] = dot(both, rows(gcopy, s), TN).astype(BF16)
            cells = []
            for j in range(2):
                cell = jnp.zeros((64, 128), F32)
                for n, part in enumerate(parts_of(ggcol[j, at, :])):
                    cell = jnp.where(lane == own + j + 32 * n, part.astype(F32), cell)
                cells.append(cell.astype(BF16))
            pay[pair_slot(sa, sb), c, :, 1024:] = dot(both, jnp.concatenate(cells, 0), TN).astype(
                BF16
            )
        hand_over(pay, land_c, sems[6], sems[7], k).start()
        return _

    lax.fori_loop(0, 8, combine, 0)

    stores = [
        pltpu.make_async_copy(wg.at[d], out, store.at[d])
        for d, out in enumerate((wg0, wg1, wg2, wg3))
    ]

    def weights(i, _):
        d, j = i // 2, i % 2
        blocks = [
            pl.ds(pl.multiple_of(ctx_slot(lax.rem(ca + d, 4), lax.rem(cb + e, 2)) * 128, 128), 128)
            for e in range(2)
        ]
        lhs = jnp.concatenate([gact[j, :, blk] for blk in blocks], 1)
        gi = dot(lhs, buf[j], TN).astype(BF16)
        here = pl.ds(pl.multiple_of(j * 1024, 1024), 1024)
        lhs = jnp.concatenate([gp[here, blk] for blk in blocks], 1)
        go = dot(lhs, hidden[j], TN).astype(BF16)
        for e in range(2):
            wg[d, e, j, :, :1024] = gi[e * 128 : e * 128 + 128]
            wg[d, e, j, :, 1024:] = go[e * 128 : e * 128 + 128]
        return _

    def out_rows(s, _):
        full[s] = dot(sel[s], rows(gbuf, s), TN).astype(BF16)
        return _

    steps = scatter_wsh_plan(pay, acc, land, land_c, sems[4:8], handed=True)
    next(steps)
    lax.fori_loop(0, 4, weights, 0)
    stores[0].start()
    stores[1].start()
    next(steps)
    next(steps)
    lax.fori_loop(4, 8, weights, 0)
    stores[2].start()
    stores[3].start()
    next(steps)
    lax.fori_loop(0, 16, out_rows, 0)
    run(steps)
    back_o[...] = acc[pair_slot(wa, wb)]
    for copy in stores:
        copy.wait()


def experts(x, cot, w_in, w_out, misc, mask, cid):
    t, d, e = 128, 1024, 1024
    wg = ((2, 2, t, 1536), BF16)
    return talk(
        experts_kernel,
        [((16, t, d), BF16), ((t, 1152), BF16), wg, wg, wg, wg],
        [
            pltpu.VMEM((2, e, d), BF16),
            pltpu.VMEM((2, d, 512), BF16),
            pltpu.VMEM((16, 128, 128), BF16),
            pltpu.VMEM((2, e, d), BF16),
            pltpu.VMEM((2, e, d), BF16),
            pltpu.VMEM((2, e, 1), F32),
            pltpu.VMEM((2, e, 1), F32),
            pltpu.VMEM((2 * e, d), BF16),
            pltpu.VMEM((2, e, 512), BF16),
            pltpu.VMEM((2, e, d), BF16),
            pltpu.VMEM((2, e, d), BF16),
            pltpu.VMEM((8, 2, t, 1152), BF16),
            pltpu.VMEM((4, 2, 2, t, 1536), BF16),
        ]
        + wsh_land(t, 1152)
        + [pltpu.SemaphoreType.DMA((3,)), pltpu.SemaphoreType.DMA((4,))]
        + WSH_SEMS * 2,
        cid,
        "experts",
        [VMEM] + [pl.BlockSpec(memory_space=pl.ANY)] * 3 + [VMEM] * 2,
        [VMEM] * 2 + [pl.BlockSpec(memory_space=pl.ANY)] * 4,
        limit=63,
        flops=80 << 30,
    )(x, cot, w_in, w_out, misc, mask)


def split_dot(a, b, dims):
    high = a.astype(BF16)
    rest = (a - high.astype(F32)).astype(BF16)
    return dot(high, b, dims) + dot(rest, b, dims)


def back_kernel(
    back, mid_r, cot, misc, mask, normed, merged, q, kv, lse, wo, cos, sin,
    gmid_o, gkv_o, gq_o, gwo_o, gmisc_o, gm, dkv,
):
    mid = mid_r[...]
    cells = back[:, 1024:].astype(F32)
    ggates = cells[:, :32] + cells[:, 32:64] + cells[:, 64:96]
    router = misc[0:32, :].astype(BF16)
    chosen = mask[...]
    logits = jnp.where(chosen > 0, dot(normed[...], router, NT), MASKED)
    raised = jnp.exp(logits - jnp.max(logits, 1, keepdims=True)) * chosen
    gates = raised / jnp.sum(raised, 1, keepdims=True)
    glogits = gates * (ggates - jnp.sum(gates * ggates, 1, keepdims=True))
    scale = rms_scale(mid)
    gnormed = back[:, :1024].astype(F32) + split_dot(glogits, router, (((1,), (0,)), ((), ())))
    gmisc_o[0:32, :] = split_dot(glogits, normed[...], TN)
    gmisc_o[32:33, :] = jnp.sum(gnormed * mid * scale, 0, keepdims=True)
    gmid = cot[...].astype(F32) + norm_back(gnormed * misc[97:98, :], mid, scale)
    gmid_o[...] = gmid
    branch = gmid.astype(BF16)
    gwo_o[...] = dot(merged[...], branch, TN).astype(BF16)
    gm[...] = dot(branch, wo[...], NT).astype(BF16)
    visible = visible_mask()
    gq = []
    for g in range(8):
        keys = kv[:, g * 64 : g * 64 + 64]
        values = kv[:, 512 + g * 64 : 512 + g * 64 + 64]
        queries, grads = two_heads(q, g), two_heads(gm, g)
        scores = jnp.where(visible, dot(queries, keys, NT) * DH**-0.5, MASKED)
        probs = jnp.exp(scores - lse[g])
        gprobs = dot(grads, values, NT)
        inner = jnp.sum(probs * gprobs, -1, keepdims=True)
        graw = (probs * (gprobs - inner) * DH**-0.5).astype(BF16)
        gq.append(side_by_side(dot(graw, keys)))
        dkv[g * 64 : g * 64 + 64, :] = dot(queries, graw, TN)
        dkv[512 + g * 64 : 512 + g * 64 + 64, :] = dot(grads, probs.astype(BF16), TN)
    gq_o[...] = unrotate(jnp.concatenate(gq, 1), cos[...], sin[...]).astype(BF16)
    for c in range(8):
        gkv_o[c] = dkv[:, c * 128 : c * 128 + 128].T.astype(BF16)


def finish_kernel(
    gkv, gq, normed, w, tok, gmid, cos, sin, misc, gwo, gmisc, mid, extra,
    tgrad_o, pack_o, out_o, gall,
):
    out_o[...] = (mid[...] + extra[...].astype(F32)).astype(BF16)
    c, s = cos[:, :512], sin[:, :512]
    gall[:, :1024] = gq[...]
    gall[:, 1024:1536] = unrotate(gkv[:, :512].astype(F32), c, s).astype(BF16)
    gall[:, 1536:] = gkv[:, 512:]
    x = tok[...].astype(F32)
    scale = rms_scale(x)
    gnormed = dot(gall[...], w[:, :2048], NT)
    pack_o[:, :2048] = dot(normed[...], gall[...], TN).astype(BF16)
    pack_o[:, 2048:3072] = gwo[...]
    gain = jnp.sum(gnormed * x * scale, 0, keepdims=True)
    rows = jnp.concatenate([gmisc[0:33, :], gain, jnp.zeros((94, 1024), F32)], 0)
    pack_o[:, 3072:] = rows.T.astype(BF16)
    tgrad_o[...] = (gmid[...] + norm_back(gnormed * misc[96:97, :], x, scale)).astype(BF16)


def local(
    tokens, gain_attn, w_query, w_key, w_value, w_output, gain_moe, w_router, w_in, w_out, routes,
    cotangent,
):
    tok = tokens.reshape(128, 1024)
    cot = cotangent.reshape(128, 1024)
    chosen = routes.reshape(128, 8)
    own_mask = jnp.sum(
        (chosen[:, :, None] == jnp.arange(32, dtype=jnp.int32)).astype(F32), 1
    )
    low_mask = own_mask.astype(BF16)
    pack = jnp.concatenate(
        [
            w_query, w_key, w_value, w_router, low_mask[:64], low_mask[64:],
            gain_attn[:, None], gain_moe[:, None], jnp.zeros((64, 30), BF16),
        ],
        1,
    )
    positions = (lax.axis_index("ctx") * 128 + jnp.arange(128, dtype=jnp.int32)).astype(F32)
    frequencies = ROPE_BASE ** (-jnp.arange(DH // 2, dtype=F32) * 2.0 / DH)
    angles = positions[:, None] * frequencies[None, :]
    cos = jnp.tile(jnp.cos(angles), (1, 32))
    sin = jnp.tile(jnp.sin(angles), (1, 32))

    w = gather_weights(pack, 0).reshape(1024, 2176)
    t, d = 128, 1024
    normed, q, kv, misc = compute(
        project_kernel,
        [((t, d), BF16), ((t, d), BF16), ((t, d), BF16), ((128, d), F32)],
        name="project",
    )(tok, w, cos, sin)
    kv_all, cot_all, wo = gather_sequence(kv, cot, w_output, 1)
    kv_all, cot_all, wo = kv_all.reshape(d, d), cot_all.reshape(2048, d), wo.reshape(d, d)
    merged, mid, normed_moe, lse = compute(
        attend_kernel,
        [((t, d), BF16), ((t, d), F32), ((t, d), BF16), ((8, 256, 1), F32)],
        name="attend",
    )(q, kv_all, tok, wo, misc)
    mask = misc[32:96].reshape(2, 32, 16, 64).transpose(2, 1, 0, 3).reshape(16, 32, 128)
    pay, back, *wg = experts(normed_moe, cot_all, w_in, w_out, misc, mask, 2)

    def along_x(step):
        return [(c, c // 4 * 4 + (c + step) % 4) for c in range(8)]

    met = [lax.ppermute(wg[step], "ctx", along_x(step)) for step in (1, 2, 3)]
    chip_sum = wg[0].astype(F32) + met[0].astype(F32) + met[1].astype(F32) + met[2].astype(F32)
    across = lax.ppermute(chip_sum[1].astype(BF16), "ctx", [(c, (c + 4) % 8) for c in range(8)])
    expert_grads = chip_sum[0] + across.astype(F32)

    gmid, gkv, gq, gwo, gmisc = compute(
        back_kernel,
        [((t, d), F32), ((8, t, d), BF16), ((t, d), BF16), ((d, d), BF16), ((40, d), F32)],
        [pltpu.VMEM((t, d), BF16), pltpu.VMEM((d, d), F32)],
        name="back",
    )(back, mid, cot, misc, own_mask, normed_moe, merged, q, kv_all, lse, wo, cos, sin)
    gkv_own, extra = sum_sequence(gkv, pay, 3)
    tokens_grad, packed, output = compute(
        finish_kernel,
        [((t, d), BF16), ((d, 3200), BF16), ((t, d), BF16)],
        [pltpu.VMEM((t, 2048), BF16)],
        name="finish",
    )(gkv_own, gq, normed, w, tok, gmid, cos, sin, misc, gwo, gmisc, mid, extra)
    sums = sum_all(packed.reshape(16, 64, 3200), 4)
    return (
        output.reshape(1, 128, 1024),
        tokens_grad.reshape(1, 128, 1024),
        sums[:, 3105],
        sums[:, :1024],
        sums[:, 1024:1536],
        sums[:, 1536:2048],
        sums[:, 2048:3072],
        sums[:, 3104],
        sums[:, 3072:3104],
        expert_grads[:, :, :1024],
        expert_grads[:, :, 1024:],
    )


def solution(mesh):
    return jax.shard_map(
        local,
        mesh=mesh,
        in_specs=(
            P("wsh", "ctx", None),
            P("wsh"),
            P("wsh", None),
            P("wsh", None),
            P("wsh", None),
            P("wsh", None),
            P("wsh"),
            P("wsh", None),
            P("wsh", None, None),
            P("wsh", None, None),
            P("wsh", "ctx", None, None),
            P("wsh", "ctx", None),
        ),
        out_specs=(
            P("wsh", "ctx", None),
            P("wsh", "ctx", None),
            P("wsh"),
            P("wsh", None),
            P("wsh", None),
            P("wsh", None),
            P("wsh", None),
            P("wsh"),
            P("wsh", None),
            P("wsh", "ctx", None),
            P("wsh", "ctx", None),
        ),
        check_vma=False,
    )
```

```python
import jax
import jax.numpy as jnp
from jax import lax
from jax.experimental import pallas as pl
from jax.experimental.pallas import tpu as pltpu
from jax.sharding import PartitionSpec as P

MESH = pl.DeviceIdType.MESH
F32 = jnp.float32
BF16 = jnp.bfloat16
DH = 64
EPS = 1e-05
ROPE_BASE = 10000.0
MASKED = -1e30
VMEM = pl.BlockSpec(memory_space=pltpu.VMEM)
NT = (((1,), (1,)), ((), ()))
TN = (((0,), (0,)), ((), ()))


def dot(a, b, dims=(((1,), (0,)), ((), ()))):
    return lax.dot_general(a, b, dims, preferred_element_type=F32)


def wsh_place():
    w = lax.axis_index("wsh")
    return w // 4, (w // 2) % 2, w % 2


def wsh_slot(a, b, core):
    return (a * 2 + b) * 2 + core


def wsh_device(a, b, core):
    return (lax.axis_index("ctx"), wsh_slot(a, b, core))


def ctx_place():
    c = lax.axis_index("ctx")
    return c % 4, c // 4


def ctx_slot(a, b):
    return b * 4 + a


def ctx_device(a, b):
    return (ctx_slot(a, b), lax.axis_index("wsh"))


def around(a, step):
    return lax.rem(a + step, 4)


def greet(peers):
    barrier = pltpu.get_barrier_semaphore()
    for peer in peers:
        pl.semaphore_signal(barrier, inc=1, device_id=peer, device_id_type=MESH)
    pl.semaphore_wait(barrier, len(peers))


def remote(src, dst, send, recv, k, device):
    return pltpu.make_async_remote_copy(
        src_ref=src,
        dst_ref=dst,
        send_sem=send.at[k],
        recv_sem=recv.at[k],
        device_id=device,
        device_id_type=MESH,
    )


def wsh_peers():
    a, b, core = wsh_place()
    return [
        wsh_device(around(a, 1), b, core),
        wsh_device(around(a, 3), b, core),
        wsh_device(around(a, 2), b, core),
        wsh_device(a, 1 - b, core),
        wsh_device(a, b, 1 - core),
    ]


def ctx_peers():
    a, b = ctx_place()
    return [
        ctx_device(around(a, 1), b),
        ctx_device(around(a, 3), b),
        ctx_device(around(a, 2), b),
        ctx_device(a, 1 - b),
    ]


def run(*plans):
    plans = list(plans)
    while plans:
        plans = [p for p in plans if next(p, "end") != "end"]


def gather_plan(at, device, a, b, send, recv, arrived=lambda *_: None):
    up, down, far = around(a, 1), around(a, 3), around(a, 2)
    other = 1 - b

    def push(k, sa, sb, to):
        copy = remote(at(sa, sb), at(sa, sb), send, recv, k, to)
        copy.start()
        return copy

    def landed(k, sa, sb):
        remote(at(sa, sb), at(sa, sb), send, recv, k, device(a, b)).wait_recv()
        arrived(k, sa, sb)

    sent = [
        push(3, a, b, device(a, other)),
        push(0, a, b, device(up, b)),
        push(1, a, b, device(down, b)),
        push(2, a, b, device(far, b)),
    ]
    yield
    landed(3, a, other)
    sent.append(push(4, a, other, device(up, b)))
    sent.append(push(5, a, other, device(down, b)))
    yield
    landed(0, down, b)
    landed(1, up, b)
    yield
    landed(2, far, b)
    sent.append(push(6, far, b, device(a, other)))
    yield
    landed(4, down, other)
    landed(5, up, other)
    yield
    landed(6, far, other)
    for copy in sent:
        copy.wait_send()


def gather_wsh_plan(at, sems, after_same=lambda: None):
    send, recv, send_c, recv_c = sems
    a, b, core = wsh_place()
    mine = lambda sa, sb: at(wsh_slot(sa, sb, core))
    handed = []

    def hand(k, sa, sb):
        sibling = wsh_device(a, b, 1 - core)
        copy = remote(mine(sa, sb), mine(sa, sb), send_c, recv_c, k, sibling)
        copy.start()
        handed.append((copy, k, sa, sb))

    def take(k, sa, sb):
        block = at(wsh_slot(sa, sb, 1 - core))
        remote(block, block, send_c, recv_c, k, wsh_device(a, b, 1 - core)).wait_recv()

    hand(7, a, b)
    device = lambda sa, sb: wsh_device(sa, sb, core)
    steps = gather_plan(mine, device, a, b, send, recv, hand)
    for count, _ in enumerate(steps):
        if count == 3:
            for _, k, sa, sb in handed:
                if k in (7, 0, 1, 2):
                    take(k, sa, sb)
            after_same()
        yield
    for copy, k, sa, sb in handed:
        if k not in (7, 0, 1, 2):
            take(k, sa, sb)
        copy.wait_send()


def wsh_moves(at, sems):
    send, recv, send_c, recv_c = sems
    a, b, core = wsh_place()
    sibling = wsh_device(a, b, 1 - core)
    mine = lambda sa, sb: at(wsh_slot(sa, sb, core))
    sent = []

    def push(k, sa, sb, to):
        sent.append(remote(mine(sa, sb), mine(sa, sb), send, recv, k, wsh_device(*to, core)))
        sent[-1].start()

    def hand(k, sa, sb):
        sent.append(remote(mine(sa, sb), mine(sa, sb), send_c, recv_c, k, sibling))
        sent[-1].start()

    def landed(k, sa, sb):
        remote(mine(sa, sb), mine(sa, sb), send, recv, k, sibling).wait_recv()
        hand(k, sa, sb)

    def finish(*blocks):
        for k, sa, sb in blocks:
            block = at(wsh_slot(sa, sb, 1 - core))
            remote(block, block, send_c, recv_c, k, sibling).wait_recv()
        for copy in sent:
            copy.wait_send()

    return push, hand, landed, finish


def near_plan(at, sems):
    a, b, _ = wsh_place()
    up, down, far, other = around(a, 1), around(a, 3), around(a, 2), 1 - b
    push, hand, landed, finish = wsh_moves(at, sems)
    hand(7, a, b)
    push(3, a, b, (a, other))
    push(0, a, b, (up, b))
    push(1, a, b, (down, b))
    push(2, a, b, (far, b))
    yield
    landed(3, a, other)
    yield
    landed(0, down, b)
    landed(1, up, b)
    yield
    landed(2, far, b)
    yield
    finish((7, a, b), (3, a, other), (0, down, b), (1, up, b), (2, far, b))


def far_plan(at, sems):
    a, b, _ = wsh_place()
    up, down, far, other = around(a, 1), around(a, 3), around(a, 2), 1 - b
    push, _, landed, finish = wsh_moves(at, sems)
    push(4, a, other, (up, b))
    push(5, a, other, (down, b))
    push(6, far, b, (a, other))
    yield
    landed(4, down, other)
    landed(5, up, other)
    yield
    landed(6, far, other)
    yield
    finish((4, down, other), (5, up, other), (6, far, other))


def shared_plan(ref, sems):
    send, recv, send_c, recv_c = sems[4:]
    a, b, core = wsh_place()
    ca, cb = ctx_place()
    sibling = wsh_device(a, b, 1 - core)
    yield from gather_wsh_plan(lambda slot: ref.at[slot // 2, slot % 2, ca], sems[:4])
    part = lambda c, which: ref.at[:, c, which]
    sent = []

    def move(c, which, sem, k, to):
        sent.append(remote(part(c, which), part(c, which), *sem, k, to))
        sent[-1].start()

    for k, step in ((0, 1), (1, 3), (2, 2)):
        move(core, ca, (send, recv), k, ctx_device(around(ca, step), cb))
    for k, step in ((0, 1), (1, 3), (2, 2)):
        yield
        here = around(ca, 4 - step)
        remote(part(core, here), part(core, here), send, recv, k, sibling).wait_recv()
        move(core, here, (send_c, recv_c), k, sibling)
    for k, step in ((0, 1), (1, 3), (2, 2)):
        here = part(1 - core, around(ca, 4 - step))
        remote(here, here, send_c, recv_c, k, sibling).wait_recv()
    for copy in sent:
        copy.wait_send()


def some(plan, count):
    for _ in range(count):
        next(plan)
        yield


def rows_of(ref, rows):
    return lambda slot: ref.at[pl.ds(pl.multiple_of(slot * rows, rows), rows)]


WSH_SEMS = [pltpu.SemaphoreType.DMA((7,))] * 2 + [pltpu.SemaphoreType.DMA((8,))] * 2
CTX_SEMS = [pltpu.SemaphoreType.DMA((7,))] * 2
X_SEMS = [pltpu.SemaphoreType.DMA((3,))] * 4
ANY = pl.BlockSpec(memory_space=pl.ANY)


def talk(kernel, outs, scratch, cid, name, in_specs, out_specs=None, limit=48, flops=0):
    return pl.pallas_call(
        kernel,
        out_shape=[jax.ShapeDtypeStruct(s, d) for s, d in outs],
        in_specs=in_specs,
        out_specs=out_specs or [VMEM] * len(outs),
        scratch_shapes=list(scratch),
        compiler_params=pltpu.CompilerParams(
            collective_id=cid, has_side_effects=True, vmem_limit_bytes=limit << 20
        ),
        cost_estimate=pl.CostEstimate(
            flops=flops, bytes_accessed=1 << 20, transcendentals=0
        ),
        name=name,
    )


def scatter_plan(at, land, device, a, b, send, recv, ready, add):
    up, down, far = around(a, 1), around(a, 3), around(a, 2)
    other = 1 - b

    def push(k, sa, sb, to):
        copy = remote(at(sa, sb), land.at[k], send, recv, k, to)
        copy.start()
        return copy

    def landed(k, sa, sb):
        remote(at(sa, sb), land.at[k], send, recv, k, device(a, b)).wait_recv()
        add(sa, sb, k)

    sent = []
    ready(up, other)
    sent.append(push(1, up, other, device(up, b)))
    ready(far, other)
    sent.append(push(0, far, other, device(a, other)))
    ready(down, other)
    sent.append(push(2, down, other, device(down, b)))
    ready(a, other)
    ready(up, b)
    sent.append(push(3, up, b, device(up, b)))
    ready(far, b)
    ready(down, b)
    sent.append(push(4, down, b, device(down, b)))
    ready(a, b)
    yield
    landed(0, far, b)
    sent.append(push(5, far, b, device(far, b)))
    yield
    landed(1, a, other)
    landed(2, a, other)
    sent.append(push(6, a, other, device(a, other)))
    yield
    landed(3, a, b)
    landed(4, a, b)
    yield
    landed(5, a, b)
    landed(6, a, b)
    for copy in sent:
        copy.wait_send()


def pair_slot(sa, sb):
    return sa * 2 + sb


def hand_step(k):
    a, b, _ = wsh_place()
    return lax.rem(a + k + 1, 4), lax.rem(b + 1 + k // 4, 2)


def hand_over(p_ref, land_c, send_c, recv_c, k):
    a, b, core = wsh_place()
    return remote(
        p_ref.at[pair_slot(*hand_step(k)), 1 - core],
        land_c.at[k],
        send_c,
        recv_c,
        k,
        wsh_device(a, b, 1 - core),
    )


def scatter_wsh_plan(p_ref, land, land_c, sems, handed=False):
    send, recv, send_c, recv_c = sems
    a, b, core = wsh_place()
    copies = [hand_over(p_ref, land_c, send_c, recv_c, k) for k in range(8)]
    if not handed:
        for copy in copies:
            copy.start()
    count = [0]

    def ready(sa, sb):
        k = count[0]
        count[0] += 1
        copies[k].wait_recv()
        at = pair_slot(sa, sb)
        p_ref[at, core] = (p_ref[at, core].astype(F32) + land_c[k].astype(F32)).astype(BF16)

    def add(sa, sb, k):
        at = pair_slot(sa, sb)
        p_ref[at, core] = (p_ref[at, core].astype(F32) + land[k].astype(F32)).astype(BF16)

    device = lambda sa, sb: wsh_device(sa, sb, core)
    block = lambda sa, sb: p_ref.at[pair_slot(sa, sb), core]
    yield from scatter_plan(block, land, device, a, b, send, recv, ready, add)
    for copy in copies:
        copy.wait_send()


def scatter_ctx_plan(p_ref, land, sems):
    a, b = ctx_place()

    def add(sa, sb, k):
        at = ctx_slot(sa, sb)
        p_ref[at] = (p_ref[at].astype(F32) + land[k].astype(F32)).astype(BF16)

    none = lambda *_: None
    block = lambda sa, sb: p_ref.at[ctx_slot(sa, sb)]
    yield from scatter_plan(block, land, ctx_device, a, b, *sems, none, add)


def sum_ctx_plan(p_ref, land, full, sems):
    a, b = ctx_place()
    yield from scatter_ctx_plan(p_ref, land, sems[:2])
    full[ctx_slot(a, b)] = p_ref[ctx_slot(a, b)]
    block = lambda sa, sb: full.at[ctx_slot(sa, sb)]
    yield from gather_plan(block, ctx_device, a, b, *sems[2:])


def wsh_land(rows, cols):
    return [pltpu.VMEM((7, rows, cols), BF16), pltpu.VMEM((8, rows, cols), BF16)]


def own_pair():
    a, b, core = wsh_place()
    return pair_slot(a, b), core


class Loads:
    def __init__(self, refs, places, sems):
        self.copies = [
            pltpu.make_async_copy(ref, place, sems.at[k])
            for k, (ref, place) in enumerate(zip(refs, places))
        ]
        for copy in self.copies:
            copy.start()

    def wait(self, *which):
        for k in which:
            self.copies[k].wait()


def rms_scale(x):
    return lax.rsqrt(jnp.mean(x * x, -1, keepdims=True) + EPS)


def norm_back(u, x, scale):
    return scale * u - x * scale * scale * scale * jnp.mean(u * x, -1, keepdims=True)


def low_half(shape):
    return lax.broadcasted_iota(jnp.int32, shape, len(shape) - 1) % DH < DH // 2


def rotate(v, cos, sin):
    width = v.shape[-1]
    turned = jnp.where(
        low_half(v.shape), -pltpu.roll(v, width - DH // 2, 1), pltpu.roll(v, DH // 2, 1)
    )
    return v * cos + turned * sin


def unrotate(v, cos, sin):
    width = v.shape[-1]
    scaled = v * sin
    turned = jnp.where(
        low_half(v.shape), pltpu.roll(scaled, width - DH // 2, 1), -pltpu.roll(scaled, DH // 2, 1)
    )
    return v * cos + turned


def two_heads(ref, g):
    return jnp.concatenate(
        [ref[:, g * 128 : g * 128 + 64], ref[:, g * 128 + 64 : g * 128 + 128]], 0
    )


def side_by_side(rows):
    return jnp.concatenate([rows[:128], rows[128:]], 1)


def visible_mask():
    row = lax.broadcasted_iota(jnp.int32, (256, 1024), 0) % 128
    col = lax.broadcasted_iota(jnp.int32, (256, 1024), 1)
    return col <= row + lax.axis_index("ctx") * 128


def wide(table, width):
    return jnp.concatenate([table] * (width // 128), 1)


def block_of(ref):
    return lambda slot: ref.at[slot // 4, slot // 2 % 2, slot % 2]


def front_kernel(
    tok, wq, wk, wv, small, cos_r, sin_r, cot, wo_r,
    w, kv, cot_all, wo, normed_all, q, misc, mask_o, merged_o, mid_o, normed_moe_o, lse_o, tok_all,
    cos, sin, load, *sems,
):
    own = lax.axis_index("wsh")
    here = pl.ds(pl.multiple_of(own * 64, 64), 64)
    ca, cb = ctx_place()
    rows = pl.ds(pl.multiple_of(ctx_slot(ca, cb) * 128, 128), 128)
    cot_at = block_of(cot_all)
    loads = Loads(
        [wq, wk, wv, small, tok, cos_r, sin_r, wo_r.at[ca], cot],
        [
            w.at[here, :1024],
            w.at[here, 1024:1536],
            w.at[here, 1536:2048],
            w.at[here, 2048:],
            tok_all.at[rows],
            cos,
            sin,
            wo.at[own // 2, own % 2, ca],
            cot_at(own),
        ],
        load,
    )
    greet(wsh_peers() + ctx_peers())
    loads.wait(0, 1, 2, 3)
    w_plan = gather_wsh_plan(rows_of(w, 64), sems[:4])
    tok_at = lambda sa, sb: rows_of(tok_all, 128)(ctx_slot(sa, sb))
    tok_plan = gather_plan(tok_at, ctx_device, ca, cb, *sems[4:6])
    next(w_plan)
    loads.wait(4, 7)
    next(tok_plan)
    wo_plan = shared_plan(wo, sems[6:14])
    next(wo_plan)
    loads.wait(5, 6, 8)
    run(w_plan, tok_plan, some(wo_plan, 4))
    next(wo_plan)
    cot_plan = near_plan(cot_at, sems[14:18])
    next(cot_plan)
    misc[...] = w[:, 2048:2176].astype(F32).T
    gain = misc[96:97, :]

    def sequence(i, _):
        at = pl.ds(pl.multiple_of(i * 256, 256), 256)
        x = tok_all[at, :].astype(F32)
        normed = (x * rms_scale(x) * gain).astype(BF16)
        normed_all[at, :] = normed
        c, s = wide(cos[at, :], 512), wide(sin[at, :], 512)
        kv[at, :512] = rotate(dot(normed, w[:, 1024:1536]), c, s).astype(BF16)
        kv[at, 512:] = dot(normed, w[:, 1536:2048]).astype(BF16)
        return _

    lax.fori_loop(0, 4, sequence, 0)
    c, s = wide(cos[rows, :], 1024), wide(sin[rows, :], 1024)
    q[...] = rotate(dot(normed_all[rows, :], w[:, :1024]), c, s).astype(BF16)
    for n in range(16):
        lanes = slice(n * 64, n * 64 + 64)
        mask_o[n] = jnp.concatenate([misc[32:64, lanes], misc[64:96, lanes]], 1)
    visible = visible_mask()
    for g in range(8):
        keys = kv[:, g * 64 : g * 64 + 64]
        values = kv[:, 512 + g * 64 : 512 + g * 64 + 64]
        scores = jnp.where(visible, dot(two_heads(q, g), keys, NT) * DH**-0.5, MASKED)
        top = jnp.max(scores, -1, keepdims=True)
        raised = jnp.exp(scores - top)
        total = jnp.sum(raised, -1, keepdims=True)
        lse_o[g] = top + jnp.log(total)
        probs = (raised * (1.0 / total)).astype(BF16)
        merged_o[:, g * 128 : g * 128 + 128] = side_by_side(dot(probs, values)).astype(BF16)
        if g in (3, 6):
            next(wo_plan)
        if g in (2, 4, 7):
            next(cot_plan)
    run(wo_plan)
    mid = tok_all[rows, :].astype(F32) + dot(merged_o[...], wo[...].reshape(1024, 1024))
    mid_o[...] = mid
    normed_moe_o[...] = (mid * rms_scale(mid) * misc[97:98, :]).astype(BF16)
    run(cot_plan)


def front(*args, cid):
    t, d = 128, 1024
    return talk(
        front_kernel,
        [
            ((d, 2176), BF16), ((d, d), BF16), ((4, 2, 2, t, d), BF16), ((8, 2, 4, 16, d), BF16),
            ((d, d), BF16), ((t, d), BF16), ((128, d), F32), ((16, 32, 128), F32),
            ((t, d), BF16), ((t, d), F32), ((t, d), BF16), ((8, 256, 1), F32),
        ],
        [
            pltpu.VMEM((d, d), BF16),
            pltpu.VMEM((d, 128), F32),
            pltpu.VMEM((d, 128), F32),
            pltpu.SemaphoreType.DMA((9,)),
        ]
        + WSH_SEMS
        + CTX_SEMS
        + WSH_SEMS
        + X_SEMS
        + WSH_SEMS,
        cid,
        "front",
        [ANY] * 9,
        limit=56,
        flops=60 << 30,
    )(*args)


def parts_of(v):
    high = v.astype(BF16)
    rest = v - high.astype(F32)
    middle = rest.astype(BF16)
    return high, middle, (rest - middle.astype(F32)).astype(BF16)


def experts_kernel(
    x_r, cot, w_in_r, w_out_r, misc_r, mask_r, full, back_o, *rest,
):
    first, second, rest = rest[:4], rest[4:8], rest[8:]
    misc, mask, rest = rest[0], rest[1], rest[2:]
    cotv, w_in, w_out, sel, buf, gbuf, gcol, ggcol, gp, hidden, gact, gcopy, pay, wg = rest[:14]
    land, land_c, load, store, send_x, recv_x, *sems = rest[14:]
    wa, wb, core = wsh_place()
    ca, cb = ctx_place()
    loads = Loads(
        [x_r, misc_r, mask_r, cot.at[:, wb], cot.at[wa, 1 - wb], w_in_r, w_out_r],
        [
            full.at[wsh_slot(wa, wb, core)],
            misc,
            mask,
            cotv.at[:, wb],
            cotv.at[wa, 1 - wb],
            w_in,
            w_out,
        ],
        load,
    )
    own = lax.axis_index("wsh") * 2
    tri = (
        lax.broadcasted_iota(jnp.int32, (128, 128), 0)
        < lax.broadcasted_iota(jnp.int32, (128, 128), 1)
    ).astype(BF16)
    across_x = [ctx_device(around(ca, step), cb) for step in (1, 3, 2)]
    greet(wsh_peers() + across_x)
    loads.wait(0)
    cot_plan = far_plan(block_of(cotv), sems[8:12])
    plan = gather_wsh_plan(lambda slot: full.at[slot], sems[:4], lambda: next(cot_plan))
    next(plan)
    loads.wait(1, 2, 3, 4)
    router = misc[0:32, :].astype(BF16)
    experts = lax.broadcasted_iota(jnp.int32, (32, 128), 0)
    slots = lax.broadcasted_iota(jnp.int32, (64, 128), 0).astype(F32)

    def pick(group):
        def one(i, _):
            sa, sb = lax.rem(wa + i // 2, 4), lax.rem(wb + group, 2)
            s = wsh_slot(sa, sb, i % 2)
            chosen = mask[s]
            x = full[s]
            logits = jnp.where(chosen > 0, dot(router, x, NT), MASKED)
            raised = jnp.exp(logits - jnp.max(logits, 0, keepdims=True)) * chosen
            gates = raised / jnp.sum(raised, 0, keepdims=True)
            earlier = dot(chosen.astype(BF16), tri)
            place, gate = [], []
            for j in range(2):
                is_own = experts == own + j
                row = lambda v: jnp.sum(jnp.where(is_own, v, 0.0), 0, keepdims=True)
                hit = (slots == row(earlier)) & (row(chosen) > 0)
                place.append(hit.astype(F32))
                gate.append(jnp.sum(jnp.where(hit, row(gates), 0.0), 1, keepdims=True))
            both = jnp.concatenate(place, 0).astype(BF16)
            sel[s] = both
            xb = dot(both, x).astype(BF16)
            gb = dot(both, cotv[sa, sb, i % 2]).astype(BF16)
            at = pl.ds(pl.multiple_of(group * 512 + i * 64, 64), 64)
            for j in range(2):
                buf[j, at, :] = xb[j * 64 : j * 64 + 64]
                gbuf[j, at, :] = gb[j * 64 : j * 64 + 64]
                gcol[j, at, :] = gate[j]
            return _

        lax.fori_loop(0, 8, one, 0)


    def tile(i, _):
        j = i // 2 % 2
        row = (i // 4) * 512 + (i % 2) * 256
        at = pl.ds(pl.multiple_of(row, 256), 256)
        flat = pl.ds(pl.multiple_of(j * 1024 + row, 256), 256)
        act = dot(buf[j, at, :], w_in[j], NT)
        gate, up = act[:, :512], act[:, 512:]
        s = jax.nn.sigmoid(gate)
        h = (gate * s * up).astype(BF16)
        hidden[j, at, :] = h
        produced = dot(h, w_out[j], NT).astype(BF16).astype(F32)
        gate_col = gcol[j, at, :]
        gr = gbuf[j, at, :].astype(F32)
        ggcol[j, at, :] = jnp.sum(gr * produced, 1, keepdims=True)
        gbuf[j, at, :] = (produced * gate_col).astype(BF16)
        gpt = (gr * gate_col).astype(BF16)
        gp[flat, :] = gpt
        gh = dot(gpt, w_out[j])
        ga_gate = (gh * up * s * (1.0 + gate * (1.0 - s))).astype(BF16)
        ga_up = (gh * gate * s).astype(BF16)
        ga = jnp.concatenate([ga_gate, ga_up], 1)
        gact[j, at, :] = ga
        gcopy[j, at, :] = dot(ga, w_in[j]).astype(BF16)
        return _

    def weights(i, _):
        j, d = i // 4, i % 4
        blocks = [
            pl.ds(pl.multiple_of(ctx_slot(lax.rem(ca + d, 4), lax.rem(cb + e, 2)) * 128, 128), 128)
            for e in range(2)
        ]
        lhs = jnp.concatenate([gact[j, :, blk] for blk in blocks], 1)
        gi = dot(lhs, buf[j], TN).astype(BF16)
        here = pl.ds(pl.multiple_of(j * 1024, 1024), 1024)
        lhs = jnp.concatenate([gp[here, blk] for blk in blocks], 1)
        go = dot(lhs, hidden[j], TN).astype(BF16)
        for e in range(2):
            wg[j, d, e, :, :1024] = gi[e * 128 : e * 128 + 128]
            wg[j, d, e, :, 1024:] = go[e * 128 : e * 128 + 128]
        return _

    for _ in range(3):
        next(plan)
    loads.wait(5, 6)
    pick(0)
    lax.fori_loop(0, 4, tile, 0)
    run(plan, cot_plan)
    pick(1)
    lax.fori_loop(4, 6, tile, 0)
    lax.fori_loop(0, 4, weights, 0)
    stores = [pltpu.make_async_copy(wg.at[0, 0], first[0], store.at[0])]
    sent = [
        remote(wg.at[0, step], first[step], send_x, recv_x, step - 1, ctx_device(around(ca, step), cb))
        for step in (1, 3, 2)
    ]
    for copy in stores + sent:
        copy.start()
    lax.fori_loop(6, 8, tile, 0)
    lane = lax.broadcasted_iota(jnp.int32, (64, 128), 1)

    def place_of(sa, sb, c):
        place = lax.rem(sb + wb, 2) * 8 + lax.rem(sa - wa + 4, 4) * 2 + c
        return pl.ds(pl.multiple_of(place * 64, 64), 64)

    def rows(ref, at):
        return jnp.concatenate([ref[0, at, :], ref[1, at, :]], 0)

    def combine(k, _):
        sa, sb = hand_step(k)
        for c in range(2):
            at = place_of(sa, sb, c)
            both = sel[wsh_slot(sa, sb, c)]
            pay[pair_slot(sa, sb), c, :, :1024] = dot(both, rows(gcopy, at), TN).astype(BF16)
            cells = []
            for j in range(2):
                cell = jnp.zeros((64, 128), F32)
                for n, part in enumerate(parts_of(ggcol[j, at, :])):
                    cell = jnp.where(lane == own + j + 32 * n, part.astype(F32), cell)
                cells.append(cell.astype(BF16))
            pay[pair_slot(sa, sb), c, :, 1024:] = dot(both, jnp.concatenate(cells, 0), TN).astype(
                BF16
            )
        hand_over(pay, land_c, sems[6], sems[7], k).start()
        return _

    lax.fori_loop(0, 8, combine, 0)

    def out_rows(s, _):
        at = place_of(s // 4, s // 2 % 2, s % 2)
        full[s] = dot(sel[s], rows(gbuf, at), TN).astype(BF16)
        return _

    steps = scatter_wsh_plan(pay, land, land_c, sems[4:8], handed=True)
    next(steps)
    lax.fori_loop(4, 6, weights, 0)
    next(steps)
    lax.fori_loop(6, 8, weights, 0)
    for d, out in enumerate(second):
        stores.append(pltpu.make_async_copy(wg.at[1, d], out, store.at[1 + d]))
        stores[-1].start()
    next(steps)
    next(steps)
    lax.fori_loop(0, 16, out_rows, 0)
    run(steps)
    pair, c = own_pair()
    back_o[...] = pay[pair, c]
    for copy in stores + sent:
        copy.wait()


def experts(x, cot, w_in, w_out, misc, mask, cid):
    t, d, e = 128, 1024, 1024
    wg = ((2, t, 1536), BF16)
    out = talk(
        experts_kernel,
        [((16, t, d), BF16), ((t, 1152), BF16)] + [wg] * 8,
        [
            pltpu.VMEM((128, d), F32),
            pltpu.VMEM((16, 32, t), F32),
            pltpu.VMEM((4, 2, 2, t, d), BF16),
            pltpu.VMEM((2, e, d), BF16),
            pltpu.VMEM((2, d, 512), BF16),
            pltpu.VMEM((16, 128, 128), BF16),
            pltpu.VMEM((2, e, d), BF16),
            pltpu.VMEM((2, e, d), BF16),
            pltpu.VMEM((2, e, 1), F32),
            pltpu.VMEM((2, e, 1), F32),
            pltpu.VMEM((2 * e, d), BF16),
            pltpu.VMEM((2, e, 512), BF16),
            pltpu.VMEM((2, e, d), BF16),
            pltpu.VMEM((2, e, d), BF16),
            pltpu.VMEM((8, 2, t, 1152), BF16),
            pltpu.VMEM((2, 4, 2, t, 1536), BF16),
        ]
        + wsh_land(t, 1152)
        + [pltpu.SemaphoreType.DMA((n,)) for n in (7, 5, 3, 3)]
        + WSH_SEMS * 3,
        cid,
        "experts",
        [ANY] * 6,
        [VMEM] * 2 + [ANY] * 8,
        limit=63,
        flops=80 << 30,
    )(x, cot, w_in, w_out, misc, mask)
    return out[0], out[1], out[2:6], out[6:]


def split_dot(a, b, dims):
    high = a.astype(BF16)
    rest = (a - high.astype(F32)).astype(BF16)
    return dot(high, b, dims) + dot(rest, b, dims)


BACK_PLACES = [
    pltpu.VMEM((8, 2, 128, 1024), BF16),
    pltpu.VMEM((128, 1152), BF16),
    pltpu.VMEM((128, 1024), F32),
    pltpu.VMEM((128, 1024), BF16),
    pltpu.VMEM((128, 1024), F32),
    pltpu.VMEM((128, 1024), BF16),
    pltpu.VMEM((128, 1024), BF16),
    pltpu.VMEM((1024, 1024), BF16),
    pltpu.VMEM((128, 1024), BF16),
    pltpu.VMEM((1024, 1024), BF16),
    pltpu.VMEM((8, 256, 1), F32),
    pltpu.VMEM((1024, 128), F32),
    pltpu.VMEM((1024, 128), F32),
    pltpu.VMEM((1024, 1024), BF16),
    pltpu.VMEM((128, 1024), BF16),
    pltpu.VMEM((1024, 2176), BF16),
]


def back_kernel(chosen_r, *rest):
    count = len(BACK_PLACES)
    loaded, rest = rest[:count], rest[count:]
    experts, rest = rest[:8], rest[8:]
    out_o, tgrad_o, gwq_o, gwk_o, gwv_o, gwo_o, grouter_o, gains_o, gin_o, gout_o = rest[:10]
    rest = rest[10:]
    places, rest = rest[:count], rest[count:]
    load, gm, dkv, gkv, gall, p, pieces, sums, rest = *rest[:8], rest[8:]
    kland, sland, oland, oland_c, wland, wland_c, gland, gland_c, *rest = rest
    metx, sendy, landy, eload, send_e, recv_e, send_y, recv_y, *sems = rest
    pay, back, mid_r, cot, misc, normed_moe, merged, wo, q, kv, lse, cos, sin = places[:13]
    normed_all, tok, w = places[13:]
    own = lax.axis_index("ctx")
    own_rows = pl.ds(pl.multiple_of(own * 128, 128), 128)
    loads = Loads(loaded, places, load)
    ea, eb = ctx_place()
    eloads = Loads(experts[:5], [metx.at[0, d] for d in range(4)] + [metx.at[1, 0]], eload)
    greet(wsh_peers() + ctx_peers())
    alongx = {
        step: remote(
            experts[4 + step], metx.at[1, step], send_e, recv_e, step - 1,
            ctx_device(around(ea, step), eb),
        )
        for step in (1, 2, 3)
    }
    for step in (1, 3, 2):
        alongx[step].start()
    acrossy = [
        remote(sendy.at[j], landy.at[j], send_y, recv_y, j, ctx_device(ea, 1 - eb)) for j in range(2)
    ]

    def total(j):
        def part(e):
            return sum(metx[j, d, e].astype(F32) for d in range(4))

        sendy[j] = part(1).astype(BF16)
        acrossy[j].start()
        kept = part(0)
        gin_o[j] = kept[:, :1024]
        gout_o[j] = kept[:, 1024:]

    loads.wait(0)
    out_plan = scatter_wsh_plan(pay, oland, oland_c, sems[:4])
    next(out_plan)
    eloads.wait(0, 1, 2, 3)
    total(0)
    loads.wait(1, 2, 3, 4, 5, 6, 7)
    mid = mid_r[...]
    cells = back[:, 1024:].astype(F32)
    ggates = cells[:, :32] + cells[:, 32:64] + cells[:, 64:96]
    router = misc[0:32, :].astype(BF16)
    chosen = chosen_r[...]
    logits = jnp.where(chosen > 0, dot(normed_moe[...], router, NT), MASKED)
    raised = jnp.exp(logits - jnp.max(logits, 1, keepdims=True)) * chosen
    gates = raised / jnp.sum(raised, 1, keepdims=True)
    glogits = gates * (ggates - jnp.sum(gates * ggates, 1, keepdims=True))
    scale = rms_scale(mid)
    gnormed = back[:, :1024].astype(F32) + split_dot(glogits, router, (((1,), (0,)), ((), ())))
    grouter = split_dot(glogits, normed_moe[...], TN)
    ggain = jnp.sum(gnormed * mid * scale, 0, keepdims=True)
    gmid = cot[...].astype(F32) + norm_back(gnormed * misc[97:98, :], mid, scale)
    branch = gmid.astype(BF16)
    blocks = lambda v: v.astype(BF16).reshape(8, 2, 64, v.shape[1])
    spare = jnp.zeros((95, 1024), F32)
    p[:, :, :, 1536:1664] = blocks(jnp.concatenate([grouter, ggain, spare], 0).T)
    p[:, :, :, 1664:2688] = blocks(dot(merged[...], branch, TN))
    gm[...] = dot(branch, wo[...], NT).astype(BF16)
    next(out_plan)
    loads.wait(*range(8, count))
    visible = visible_mask()
    turned = []
    for g in range(8):
        keys = kv[:, g * 64 : g * 64 + 64]
        values = kv[:, 512 + g * 64 : 512 + g * 64 + 64]
        queries, grads = two_heads(q, g), two_heads(gm, g)
        scores = jnp.where(visible, dot(queries, keys, NT) * DH**-0.5, MASKED)
        probs = jnp.exp(scores - lse[g])
        gprobs = dot(grads, values, NT)
        inner = jnp.sum(probs * gprobs, -1, keepdims=True)
        graw = (probs * (gprobs - inner) * DH**-0.5).astype(BF16)
        turned.append(side_by_side(dot(graw, keys)))
        dkv[g * 64 : g * 64 + 64, :] = dot(queries, graw, TN)
        dkv[512 + g * 64 : 512 + g * 64 + 64, :] = dot(grads, probs.astype(BF16), TN)
        if g == 3:
            next(out_plan)
    for n in range(8):
        at = slice(n * 128, n * 128 + 128)
        gkeys = dkv[:512, at].T
        gkv[n, :, :512] = unrotate(gkeys, wide(cos[at, :], 512), wide(sin[at, :], 512)).astype(BF16)
        gkv[n, :, 512:] = dkv[512:, at].T.astype(BF16)
    partial = gkv[...].reshape(1024, 1024)
    p[:, :, :, 1024:1536] = blocks(dot(normed_all[...], partial[:, :512], TN))
    p[:, :, :, 2688:3200] = blocks(dot(normed_all[...], partial[:, 512:], TN))
    kv_plan = scatter_ctx_plan(gkv, kland, sems[4:6])
    next(kv_plan)
    c, s = wide(cos[own_rows, :], 1024), wide(sin[own_rows, :], 1024)
    gall[:, :1024] = unrotate(jnp.concatenate(turned, 1), c, s).astype(BF16)
    p[:, :, :, :1024] = blocks(dot(normed_all[own_rows, :], gall[:, :1024], TN))
    w_plan = scatter_wsh_plan(p.at[:, :, :, :3200], wland, wland_c, sems[6:10])
    next(w_plan)
    run(kv_plan, some(w_plan, 2), out_plan)
    pair, core = own_pair()
    out_o[...] = (mid + pay[pair, core].astype(F32)).astype(BF16)
    gall[:, 1024:] = gkv[own]
    x = tok[...].astype(F32)
    scale = rms_scale(x)
    gnormed = dot(gall[...], w[:, :2048], NT)
    ggain = jnp.sum(gnormed * x * scale, 0, keepdims=True)
    p[:, :, :, 3200:] = blocks(jnp.concatenate([ggain, jnp.zeros((127, 1024), F32)], 0).T)
    gain_plan = scatter_wsh_plan(p.at[:, :, :, 3200:], gland, gland_c, sems[10:14])
    next(gain_plan)
    tgrad_o[...] = (gmid + norm_back(gnormed * misc[96:97, :], x, scale)).astype(BF16)
    eloads.wait(4)
    for step in (1, 3, 2):
        alongx[step].wait()
    total(1)
    run(w_plan, gain_plan)
    mine = p[pair, core]
    for r in range(4):
        for h in range(2):
            pieces[2 * r + h] = mine[r * 16 : r * 16 + 16, h * 1664 : h * 1664 + 1664]
    run(sum_ctx_plan(pieces, sland, sums, sems[14:18]))
    for r in range(4):
        at = slice(r * 16, r * 16 + 16)
        first, second = sums[2 * r].astype(F32), sums[2 * r + 1].astype(F32)
        gwq_o[at, :] = first[:, :1024]
        gwk_o[at, :] = first[:, 1024:1536]
        grouter_o[at, :] = first[:, 1536:1568]
        gwo_o[at, :] = second[:, :1024]
        gwv_o[at, :] = second[:, 1024:1536]
    for h, lane in ((0, 32), (1, 0)):
        column = jnp.concatenate([sums[2 * r + h, :, 1536:] for r in range(4)], 0).astype(F32)
        gains_o[h : h + 1, :] = column.T[lane : lane + 1, :]
    for j in range(2):
        acrossy[j].wait()
        gin_o[j] += landy[j, :, :1024].astype(F32)
        gout_o[j] += landy[j, :, 1024:].astype(F32)


def back_half(*args, cid):
    t, d = 128, 1024
    return talk(
        back_kernel,
        [
            ((t, d), BF16), ((t, d), BF16), ((64, d), F32), ((64, 512), F32), ((64, 512), F32),
            ((64, d), F32), ((64, 32), F32), ((8, 64), F32), ((2, t, d), F32), ((2, t, 512), F32),
        ],
        BACK_PLACES
        + [
            pltpu.SemaphoreType.DMA((len(BACK_PLACES),)),
            pltpu.VMEM((t, d), BF16),
            pltpu.VMEM((d, d), F32),
            pltpu.VMEM((8, t, d), BF16),
            pltpu.VMEM((t, 2048), BF16),
            pltpu.VMEM((8, 2, 64, 3328), BF16),
            pltpu.VMEM((8, 16, 1664), BF16),
            pltpu.VMEM((8, 16, 1664), BF16),
            pltpu.VMEM((7, t, d), BF16),
            pltpu.VMEM((7, 16, 1664), BF16),
        ]
        + wsh_land(t, d)
        + wsh_land(64, 3200)
        + wsh_land(64, 128)
        + [
            pltpu.VMEM((2, 4, 2, t, 1536), BF16),
            pltpu.VMEM((2, t, 1536), BF16),
            pltpu.VMEM((2, t, 1536), BF16),
        ]
        + [pltpu.SemaphoreType.DMA((n,)) for n in (5, 3, 3, 2, 2)]
        + WSH_SEMS
        + CTX_SEMS
        + WSH_SEMS * 2
        + CTX_SEMS * 2,
        cid,
        "back",
        [VMEM] + [ANY] * (len(BACK_PLACES) + 8),
        limit=63,
        flops=80 << 30,
    )(*args)


def settle(arrays):
    count = len(arrays)

    def kernel(*refs):
        sources, places, held = refs[:count], refs[count : 2 * count], refs[2 * count : 3 * count]
        loads = Loads(sources, held, refs[-2])
        stores = []
        for k in range(count):
            loads.wait(k)
            stores.append(pltpu.make_async_copy(held[k], places[k], refs[-1].at[k]))
            stores[k].start()
        for copy in stores:
            copy.wait()

    return pl.pallas_call(
        kernel,
        out_shape=[jax.ShapeDtypeStruct(v.shape, v.dtype) for v in arrays],
        in_specs=[ANY] * count,
        out_specs=[ANY] * count,
        scratch_shapes=[pltpu.VMEM(v.shape, v.dtype) for v in arrays]
        + [pltpu.SemaphoreType.DMA((count,))] * 2,
        compiler_params=pltpu.CompilerParams(vmem_limit_bytes=16 << 20),
        name="settle",
    )(*arrays)


def local(
    tokens, gain_attn, w_query, w_key, w_value, w_output, gain_moe, w_router, w_in, w_out, routes,
    cotangent,
):
    tok = tokens.reshape(128, 1024)
    cot = cotangent.reshape(128, 1024)
    chosen = routes.reshape(128, 8)
    own_mask = jnp.sum(
        (chosen[:, :, None] == jnp.arange(32, dtype=jnp.int32)).astype(F32), 1
    )
    low_mask = own_mask.astype(BF16)
    small = jnp.concatenate(
        [
            w_router, low_mask[:64], low_mask[64:], gain_attn[:, None], gain_moe[:, None],
            jnp.zeros((64, 30), BF16),
        ],
        1,
    )
    positions = jnp.arange(1024, dtype=jnp.int32).astype(F32)
    frequencies = ROPE_BASE ** (-jnp.arange(DH // 2, dtype=F32) * 2.0 / DH)
    angles = positions[:, None] * frequencies[None, :]
    cos = jnp.tile(jnp.cos(angles), (1, 4))
    sin = jnp.tile(jnp.sin(angles), (1, 4))

    w, kv, cot_all, wo, normed_all, q, misc, mask, merged, mid, normed_moe, lse = front(
        tok, w_query, w_key, w_value, small, cos, sin, cot, w_output.reshape(4, 16, 1024), cid=0
    )
    pay, back, first, second = experts(normed_moe, cot_all, w_in, w_out, misc, mask, 1)

    results = back_half(
        own_mask, pay.reshape(8, 2, 128, 1024), back, mid, cot, misc, normed_moe, merged, wo.reshape(1024, 1024), q,
        kv, lse, cos, sin, normed_all, tok, w, *first, *second, cid=2,
    )
    output, tokens_grad, gwq, gwk, gwv, gwo, grouter, gains, gin, gout = settle(results)
    return (
        output.reshape(1, 128, 1024),
        tokens_grad.reshape(1, 128, 1024),
        gains[1],
        gwq,
        gwk,
        gwv,
        gwo,
        gains[0],
        grouter,
        gin,
        gout,
    )


def solution(mesh):
    return jax.shard_map(
        local,
        mesh=mesh,
        in_specs=(
            P("wsh", "ctx", None),
            P("wsh"),
            P("wsh", None),
            P("wsh", None),
            P("wsh", None),
            P("wsh", None),
            P("wsh"),
            P("wsh", None),
            P("wsh", None, None),
            P("wsh", None, None),
            P("wsh", "ctx", None, None),
            P("wsh", "ctx", None),
        ),
        out_specs=(
            P("wsh", "ctx", None),
            P("wsh", "ctx", None),
            P("wsh"),
            P("wsh", None),
            P("wsh", None),
            P("wsh", None),
            P("wsh", None),
            P("wsh"),
            P("wsh", None),
            P("wsh", "ctx", None),
            P("wsh", "ctx", None),
        ),
        check_vma=False,
    )
```

```python
import jax
import jax.numpy as jnp
import numpy as np
from jax import lax
from jax.experimental import pallas as pl
from jax.experimental.pallas import tpu as pltpu
from jax.sharding import PartitionSpec as P

MESH = pl.DeviceIdType.MESH
F32 = jnp.float32
BF16 = jnp.bfloat16
DH = 64
EPS = 1e-05
ROPE_BASE = 10000.0
MASKED = -1e30
VMEM = pl.BlockSpec(memory_space=pltpu.VMEM)
NT = (((1,), (1,)), ((), ()))
TN = (((0,), (0,)), ((), ()))


def dot(a, b, dims=(((1,), (0,)), ((), ()))):
    return lax.dot_general(a, b, dims, preferred_element_type=F32)


def wsh_place():
    w = lax.axis_index("wsh")
    return w // 4, (w // 2) % 2, w % 2


def wsh_slot(a, b, core):
    return (a * 2 + b) * 2 + core


def wsh_device(a, b, core):
    return (lax.axis_index("ctx"), wsh_slot(a, b, core))


def ctx_place():
    c = lax.axis_index("ctx")
    return c % 4, c // 4


def ctx_slot(a, b):
    return b * 4 + a


def ctx_device(a, b):
    return (ctx_slot(a, b), lax.axis_index("wsh"))


def around(a, step):
    return lax.rem(a + step, 4)


def greet(peers):
    barrier = pltpu.get_barrier_semaphore()
    for peer in peers:
        pl.semaphore_signal(barrier, inc=1, device_id=peer, device_id_type=MESH)
    pl.semaphore_wait(barrier, len(peers))


def remote(src, dst, send, recv, k, device):
    return pltpu.make_async_remote_copy(
        src_ref=src,
        dst_ref=dst,
        send_sem=send.at[k],
        recv_sem=recv.at[k],
        device_id=device,
        device_id_type=MESH,
    )


def wsh_peers():
    a, b, core = wsh_place()
    return [
        wsh_device(around(a, 1), b, core),
        wsh_device(around(a, 3), b, core),
        wsh_device(around(a, 2), b, core),
        wsh_device(a, 1 - b, core),
        wsh_device(a, b, 1 - core),
    ]


def ctx_peers():
    a, b = ctx_place()
    return [
        ctx_device(around(a, 1), b),
        ctx_device(around(a, 3), b),
        ctx_device(around(a, 2), b),
        ctx_device(a, 1 - b),
    ]


def run(*plans):
    plans = list(plans)
    while plans:
        plans = [p for p in plans if next(p, "end") != "end"]


def gather_plan(at, device, a, b, send, recv, arrived=lambda *_: None):
    up, down, far = around(a, 1), around(a, 3), around(a, 2)
    other = 1 - b

    def push(k, sa, sb, to):
        copy = remote(at(sa, sb), at(sa, sb), send, recv, k, to)
        copy.start()
        return copy

    def landed(k, sa, sb):
        remote(at(sa, sb), at(sa, sb), send, recv, k, device(a, b)).wait_recv()
        arrived(k, sa, sb)

    sent = [
        push(3, a, b, device(a, other)),
        push(0, a, b, device(up, b)),
        push(1, a, b, device(down, b)),
        push(2, a, b, device(far, b)),
    ]
    yield
    landed(3, a, other)
    sent.append(push(4, a, other, device(up, b)))
    sent.append(push(5, a, other, device(down, b)))
    yield
    landed(0, down, b)
    landed(1, up, b)
    yield
    landed(2, far, b)
    sent.append(push(6, far, b, device(a, other)))
    yield
    landed(4, down, other)
    landed(5, up, other)
    yield
    landed(6, far, other)
    for copy in sent:
        copy.wait_send()


def gather_wsh_plan(at, sems, after_same=lambda: None):
    send, recv, send_c, recv_c = sems
    a, b, core = wsh_place()
    mine = lambda sa, sb: at(wsh_slot(sa, sb, core))
    handed = []

    def hand(k, sa, sb):
        sibling = wsh_device(a, b, 1 - core)
        copy = remote(mine(sa, sb), mine(sa, sb), send_c, recv_c, k, sibling)
        copy.start()
        handed.append((copy, k, sa, sb))

    def take(k, sa, sb):
        block = at(wsh_slot(sa, sb, 1 - core))
        remote(block, block, send_c, recv_c, k, wsh_device(a, b, 1 - core)).wait_recv()

    hand(7, a, b)
    device = lambda sa, sb: wsh_device(sa, sb, core)
    steps = gather_plan(mine, device, a, b, send, recv, hand)
    for count, _ in enumerate(steps):
        if count == 3:
            for _, k, sa, sb in handed:
                if k in (7, 0, 1, 2):
                    take(k, sa, sb)
            after_same()
        yield
    for copy, k, sa, sb in handed:
        if k not in (7, 0, 1, 2):
            take(k, sa, sb)
        copy.wait_send()


def wsh_moves(at, sems):
    send, recv, send_c, recv_c = sems
    a, b, core = wsh_place()
    sibling = wsh_device(a, b, 1 - core)
    mine = lambda sa, sb: at(wsh_slot(sa, sb, core))
    sent = []

    def push(k, sa, sb, to):
        sent.append(remote(mine(sa, sb), mine(sa, sb), send, recv, k, wsh_device(*to, core)))
        sent[-1].start()

    def hand(k, sa, sb):
        sent.append(remote(mine(sa, sb), mine(sa, sb), send_c, recv_c, k, sibling))
        sent[-1].start()

    def landed(k, sa, sb):
        remote(mine(sa, sb), mine(sa, sb), send, recv, k, sibling).wait_recv()
        hand(k, sa, sb)

    def finish(*blocks):
        for k, sa, sb in blocks:
            block = at(wsh_slot(sa, sb, 1 - core))
            remote(block, block, send_c, recv_c, k, sibling).wait_recv()
        for copy in sent:
            copy.wait_send()

    return push, hand, landed, finish


def near_plan(at, sems):
    a, b, _ = wsh_place()
    up, down, far, other = around(a, 1), around(a, 3), around(a, 2), 1 - b
    push, hand, landed, finish = wsh_moves(at, sems)
    hand(7, a, b)
    push(3, a, b, (a, other))
    push(0, a, b, (up, b))
    push(1, a, b, (down, b))
    push(2, a, b, (far, b))
    yield
    landed(3, a, other)
    yield
    landed(0, down, b)
    landed(1, up, b)
    yield
    landed(2, far, b)
    yield
    finish((7, a, b), (3, a, other), (0, down, b), (1, up, b), (2, far, b))


def far_plan(at, sems):
    a, b, _ = wsh_place()
    up, down, far, other = around(a, 1), around(a, 3), around(a, 2), 1 - b
    push, _, landed, finish = wsh_moves(at, sems)
    push(4, a, other, (up, b))
    push(5, a, other, (down, b))
    push(6, far, b, (a, other))
    yield
    landed(4, down, other)
    landed(5, up, other)
    yield
    landed(6, far, other)
    yield
    finish((4, down, other), (5, up, other), (6, far, other))


def shared_plan(ref, sems):
    send, recv, send_c, recv_c = sems[4:]
    a, b, core = wsh_place()
    ca, cb = ctx_place()
    sibling = wsh_device(a, b, 1 - core)
    yield from gather_wsh_plan(lambda slot: ref.at[slot // 2, slot % 2, ca], sems[:4])
    part = lambda c, which: ref.at[:, c, which]
    sent = []

    def move(c, which, sem, k, to):
        sent.append(remote(part(c, which), part(c, which), *sem, k, to))
        sent[-1].start()

    for k, step in ((0, 1), (1, 3), (2, 2)):
        move(core, ca, (send, recv), k, ctx_device(around(ca, step), cb))
    for k, step in ((0, 1), (1, 3), (2, 2)):
        yield
        here = around(ca, 4 - step)
        remote(part(core, here), part(core, here), send, recv, k, sibling).wait_recv()
        move(core, here, (send_c, recv_c), k, sibling)
    for k, step in ((0, 1), (1, 3), (2, 2)):
        here = part(1 - core, around(ca, 4 - step))
        remote(here, here, send_c, recv_c, k, sibling).wait_recv()
    for copy in sent:
        copy.wait_send()


def some(plan, count):
    for _ in range(count):
        next(plan)
        yield


def rows_of(ref, rows):
    return lambda slot: ref.at[pl.ds(pl.multiple_of(slot * rows, rows), rows)]


WSH_SEMS = [pltpu.SemaphoreType.DMA((7,))] * 2 + [pltpu.SemaphoreType.DMA((8,))] * 2
CTX_SEMS = [pltpu.SemaphoreType.DMA((7,))] * 2
X_SEMS = [pltpu.SemaphoreType.DMA((3,))] * 4
ANY = pl.BlockSpec(memory_space=pl.ANY)


def talk(kernel, outs, scratch, cid, name, in_specs, out_specs=None, limit=48, flops=0):
    return pl.pallas_call(
        kernel,
        out_shape=[jax.ShapeDtypeStruct(s, d) for s, d in outs],
        in_specs=in_specs,
        out_specs=out_specs or [VMEM] * len(outs),
        scratch_shapes=list(scratch),
        compiler_params=pltpu.CompilerParams(
            collective_id=cid, has_side_effects=True, vmem_limit_bytes=limit << 20
        ),
        cost_estimate=pl.CostEstimate(
            flops=flops, bytes_accessed=1 << 20, transcendentals=0
        ),
        name=name,
    )


def scatter_plan(at, land, device, a, b, send, recv, ready, add, wide=False):
    up, down, far = around(a, 1), around(a, 3), around(a, 2)
    other = 1 - b

    def push(k, sa, sb, to):
        copy = remote(at(sa, sb), land.at[k], send, recv, k, to)
        copy.start()
        return copy

    def landed(k, sa, sb):
        remote(at(sa, sb), land.at[k], send, recv, k, device(a, b)).wait_recv()
        add(sa, sb, k)

    sent = []
    ready(up, other)
    sent.append(push(1, up, other, device(up, b)))
    ready(far, other)
    sent.append(push(0, far, other, device(far, b) if wide else device(a, other)))
    ready(down, other)
    sent.append(push(2, down, other, device(down, b)))
    ready(a, other)
    ready(up, b)
    sent.append(push(3, up, b, device(up, b)))
    ready(far, b)
    ready(down, b)
    sent.append(push(4, down, b, device(down, b)))
    ready(a, b)
    if wide:
        sent.append(push(5, far, b, device(far, b)))
    yield
    if not wide:
        landed(0, far, b)
        sent.append(push(5, far, b, device(far, b)))
    yield
    landed(1, a, other)
    landed(2, a, other)
    if wide:
        landed(0, a, other)
    sent.append(push(6, a, other, device(a, other)))
    yield
    landed(3, a, b)
    landed(4, a, b)
    yield
    landed(5, a, b)
    landed(6, a, b)
    for copy in sent:
        copy.wait_send()


def pair_slot(sa, sb):
    return sa * 2 + sb


def hand_step(k):
    a, b, _ = wsh_place()
    return lax.rem(a + k + 1, 4), lax.rem(b + 1 + k // 4, 2)


def hand_over(p_ref, land_c, send_c, recv_c, k):
    a, b, core = wsh_place()
    return remote(
        p_ref.at[pair_slot(*hand_step(k)), 1 - core],
        land_c.at[k],
        send_c,
        recv_c,
        k,
        wsh_device(a, b, 1 - core),
    )


def scatter_wsh_plan(p_ref, land, land_c, sems, handed=False, wide=False):
    send, recv, send_c, recv_c = sems
    a, b, core = wsh_place()
    copies = [hand_over(p_ref, land_c, send_c, recv_c, k) for k in range(8)]
    if not handed:
        for copy in copies:
            copy.start()
    count = [0]

    def ready(sa, sb):
        k = count[0]
        count[0] += 1
        copies[k].wait_recv()
        at = pair_slot(sa, sb)
        p_ref[at, core] = (p_ref[at, core].astype(F32) + land_c[k].astype(F32)).astype(BF16)

    def add(sa, sb, k):
        at = pair_slot(sa, sb)
        p_ref[at, core] = (p_ref[at, core].astype(F32) + land[k].astype(F32)).astype(BF16)

    device = lambda sa, sb: wsh_device(sa, sb, core)
    block = lambda sa, sb: p_ref.at[pair_slot(sa, sb), core]
    yield from scatter_plan(block, land, device, a, b, send, recv, ready, add, wide)
    for copy in copies:
        copy.wait_send()


def scatter_ctx_plan(p_ref, land, sems):
    a, b = ctx_place()

    def add(sa, sb, k):
        at = ctx_slot(sa, sb)
        p_ref[at] = (p_ref[at].astype(F32) + land[k].astype(F32)).astype(BF16)

    none = lambda *_: None
    block = lambda sa, sb: p_ref.at[ctx_slot(sa, sb)]
    yield from scatter_plan(block, land, ctx_device, a, b, *sems, none, add)


def sum_ctx_plan(p_ref, land, full, sems):
    send, recv, send_f, recv_f = sems
    me = lax.axis_index("ctx")
    peer = lambda d: lax.rem(me + d, 8)
    device = lambda d: (peer(d), lax.axis_index("wsh"))
    near = (4, 1, 7, 5, 3, 2, 6)
    sent = [
        remote(p_ref.at[peer(d)], land.at[d - 1], send, recv, d - 1, device(d)) for d in near
    ]
    for copy in sent:
        copy.start()
    yield
    total = p_ref[me].astype(F32)
    for d in near:
        remote(p_ref.at[me], land.at[d - 1], send, recv, d - 1, device(d)).wait_recv()
        total = total + land[d - 1].astype(F32)
    full[me] = total.astype(BF16)
    for d in near:
        sent.append(remote(full.at[me], full.at[me], send_f, recv_f, d - 1, device(d)))
        sent[-1].start()
    yield
    for d in near:
        here = full.at[peer(8 - d)]
        remote(here, here, send_f, recv_f, d - 1, device(d)).wait_recv()
    for copy in sent:
        copy.wait_send()


def ctx_others():
    me = lax.axis_index("ctx")
    return [(lax.rem(me + d, 8), lax.axis_index("wsh")) for d in range(1, 8)]


def wsh_land(rows, cols):
    return [pltpu.VMEM((7, rows, cols), BF16), pltpu.VMEM((8, rows, cols), BF16)]


def own_pair():
    a, b, core = wsh_place()
    return pair_slot(a, b), core


class Loads:
    def __init__(self, refs, places, sems):
        self.copies = [
            pltpu.make_async_copy(ref, place, sems.at[k])
            for k, (ref, place) in enumerate(zip(refs, places))
        ]
        for copy in self.copies:
            copy.start()

    def wait(self, *which):
        for k in which:
            self.copies[k].wait()


def rms_scale(x):
    return lax.rsqrt(jnp.mean(x * x, -1, keepdims=True) + EPS)


def norm_back(u, x, scale):
    return scale * u - x * scale * scale * scale * jnp.mean(u * x, -1, keepdims=True)


def low_half(shape):
    return lax.broadcasted_iota(jnp.int32, shape, len(shape) - 1) % DH < DH // 2


def rotate(v, cos, sin):
    width = v.shape[-1]
    turned = jnp.where(
        low_half(v.shape), -pltpu.roll(v, width - DH // 2, 1), pltpu.roll(v, DH // 2, 1)
    )
    return v * cos + turned * sin


def unrotate(v, cos, sin):
    width = v.shape[-1]
    scaled = v * sin
    turned = jnp.where(
        low_half(v.shape), pltpu.roll(scaled, width - DH // 2, 1), -pltpu.roll(scaled, DH // 2, 1)
    )
    return v * cos + turned


def two_heads(ref, g):
    return jnp.concatenate(
        [ref[:, g * 128 : g * 128 + 64], ref[:, g * 128 + 64 : g * 128 + 128]], 0
    )


def side_by_side(rows):
    return jnp.concatenate([rows[:128], rows[128:]], 1)


def visible_mask():
    row = lax.broadcasted_iota(jnp.int32, (256, 1024), 0) % 128
    col = lax.broadcasted_iota(jnp.int32, (256, 1024), 1)
    return col <= row + lax.axis_index("ctx") * 128


def wide(table, width):
    return jnp.concatenate([table] * (width // 128), 1)


def block_of(ref):
    return lambda slot: ref.at[slot // 4, slot // 2 % 2, slot % 2]


def front_kernel(
    tok, wq, wk, wv, router_r, gain_a, gain_m, routes_r, cos_r, sin_r, cot, wo_r,
    w, kv, cot_all, wo, normed_all, q, misc, mask_o, merged_o, mid_o, normed_moe_o, lse_o, own_o, tok_all,
    cos, sin, load, *sems,
):
    own = lax.axis_index("wsh")
    here = pl.ds(pl.multiple_of(own * 64, 64), 64)
    ca, cb = ctx_place()
    rows = pl.ds(pl.multiple_of(ctx_slot(ca, cb) * 128, 128), 128)
    cot_at = block_of(cot_all)
    loads = Loads(
        [wq, wk, wv, tok, cos_r, sin_r, wo_r.at[ca], cot],
        [
            w.at[here, :1024],
            w.at[here, 1024:1536],
            w.at[here, 1536:2048],
            tok_all.at[rows],
            cos,
            sin,
            wo.at[own // 2, own % 2, ca],
            cot_at(own),
        ],
        load,
    )
    expert = lax.broadcasted_iota(jnp.int32, (32, 128), 0)
    named = jnp.zeros((32, 128), F32)
    for k in range(8):
        named = named + jnp.where(routes_r[k : k + 1, :] == expert, 1.0, 0.0)
    own_o[...] = named.T
    small = jnp.concatenate(
        [
            router_r[...].astype(F32),
            named[:, :64],
            named[:, 64:],
            gain_a[...].astype(F32),
            gain_m[...].astype(F32),
            jnp.zeros((30, 64), F32),
        ],
        0,
    )
    w[here, 2048:] = small.T.astype(BF16)
    greet(wsh_peers() + ctx_peers())
    loads.wait(0, 1, 2)
    w_plan = gather_wsh_plan(rows_of(w, 64), sems[:4])
    tok_at = lambda sa, sb: rows_of(tok_all, 128)(ctx_slot(sa, sb))
    tok_plan = gather_plan(tok_at, ctx_device, ca, cb, *sems[4:6])
    next(w_plan)
    loads.wait(3, 6)
    next(tok_plan)
    wo_plan = shared_plan(wo, sems[6:14])
    next(wo_plan)
    loads.wait(4, 5, 7)
    run(w_plan, tok_plan, some(wo_plan, 4))
    next(wo_plan)
    cot_plan = near_plan(cot_at, sems[14:18])
    next(cot_plan)
    misc[...] = w[:, 2048:2176].astype(F32).T
    gain = misc[96:97, :]

    def sequence(i, _):
        at = pl.ds(pl.multiple_of(i * 256, 256), 256)
        x = tok_all[at, :].astype(F32)
        normed = (x * rms_scale(x) * gain).astype(BF16)
        normed_all[at, :] = normed
        c, s = wide(cos[at, :], 512), wide(sin[at, :], 512)
        kv[at, :512] = rotate(dot(normed, w[:, 1024:1536]), c, s).astype(BF16)
        kv[at, 512:] = dot(normed, w[:, 1536:2048]).astype(BF16)
        return _

    lax.fori_loop(0, 4, sequence, 0)
    c, s = wide(cos[rows, :], 1024), wide(sin[rows, :], 1024)
    q[...] = rotate(dot(normed_all[rows, :], w[:, :1024]), c, s).astype(BF16)
    for n in range(16):
        lanes = slice(n * 64, n * 64 + 64)
        mask_o[n] = jnp.concatenate([misc[32:64, lanes], misc[64:96, lanes]], 1)
    visible = visible_mask()
    for g in range(8):
        keys = kv[:, g * 64 : g * 64 + 64]
        values = kv[:, 512 + g * 64 : 512 + g * 64 + 64]
        scores = jnp.where(visible, dot(two_heads(q, g), keys, NT) * DH**-0.5, MASKED)
        top = jnp.max(scores, -1, keepdims=True)
        raised = jnp.exp(scores - top)
        total = jnp.sum(raised, -1, keepdims=True)
        lse_o[g] = top + jnp.log(total)
        probs = (raised * (1.0 / total)).astype(BF16)
        merged_o[:, g * 128 : g * 128 + 128] = side_by_side(dot(probs, values)).astype(BF16)
        if g in (3, 6):
            next(wo_plan)
        if g in (2, 4, 7):
            next(cot_plan)
    run(wo_plan)
    mid = tok_all[rows, :].astype(F32) + dot(merged_o[...], wo[...].reshape(1024, 1024))
    mid_o[...] = mid
    normed_moe_o[...] = (mid * rms_scale(mid) * misc[97:98, :]).astype(BF16)
    run(cot_plan)


def front(*args, cid):
    t, d = 128, 1024
    return talk(
        front_kernel,
        [
            ((d, 2176), BF16), ((d, d), BF16), ((4, 2, 2, t, d), BF16), ((8, 2, 4, 16, d), BF16),
            ((d, d), BF16), ((t, d), BF16), ((128, d), F32), ((16, 32, 128), F32),
            ((t, d), BF16), ((t, d), F32), ((t, d), BF16), ((8, 256, 1), F32), ((t, 32), F32),
        ],
        [
            pltpu.VMEM((d, d), BF16),
            pltpu.VMEM((d, 128), F32),
            pltpu.VMEM((d, 128), F32),
            pltpu.SemaphoreType.DMA((8,)),
        ]
        + WSH_SEMS
        + CTX_SEMS
        + WSH_SEMS
        + X_SEMS
        + WSH_SEMS,
        cid,
        "front",
        [ANY] * 4 + [VMEM] * 4 + [ANY] * 4,
        limit=56,
        flops=60 << 30,
    )(*args)


def several(count, each, body):
    def step(i, _):
        for k in range(each):
            body(i * each + k, None)
        return _

    lax.fori_loop(0, count // each, step, 0)


def parts_of(v):
    high = v.astype(BF16)
    rest = v - high.astype(F32)
    middle = rest.astype(BF16)
    return high, middle, (rest - middle.astype(F32)).astype(BF16)


def experts_kernel(
    x_r, cot, w_in_r, w_out_r, misc_r, mask_r, full, back_o, *rest,
):
    first, second, rest = rest[:3], rest[3:7], rest[7:]
    misc, mask, rest = rest[0], rest[1], rest[2:]
    relay, cotv, w_in, w_out, sel, buf, gbuf, gcol, ggcol, gp, hidden, gact, gcopy, pay, wg = rest[:15]
    land, land_c, load, store, send_x, recv_x, *sems = rest[15:]
    wa, wb, core = wsh_place()
    ca, cb = ctx_place()
    loads = Loads(
        [x_r, misc_r, mask_r, cot.at[:, wb], cot.at[wa, 1 - wb], w_in_r, w_out_r],
        [
            full.at[wsh_slot(wa, wb, core)],
            misc,
            mask,
            cotv.at[:, wb],
            cotv.at[wa, 1 - wb],
            w_in,
            w_out,
        ],
        load,
    )
    own = lax.axis_index("wsh") * 2
    tri = (
        lax.broadcasted_iota(jnp.int32, (128, 128), 0)
        < lax.broadcasted_iota(jnp.int32, (128, 128), 1)
    ).astype(BF16)
    across_x = [ctx_device(around(ca, step), cb) for step in (1, 3, 2)]
    greet(wsh_peers() + across_x)
    loads.wait(0)
    cot_plan = far_plan(block_of(cotv), sems[8:12])
    plan = gather_wsh_plan(lambda slot: full.at[slot], sems[:4], lambda: next(cot_plan))
    next(plan)
    loads.wait(1, 2, 3, 4)
    router = misc[0:32, :].astype(BF16)
    experts = lax.broadcasted_iota(jnp.int32, (32, 128), 0)
    slots = lax.broadcasted_iota(jnp.int32, (64, 128), 0).astype(F32)

    def pick(group):
        def one(i, _):
            sa, sb = lax.rem(wa + i // 2, 4), lax.rem(wb + group, 2)
            s = wsh_slot(sa, sb, i % 2)
            chosen = mask[s]
            x = full[s]
            logits = jnp.where(chosen > 0, dot(router, x, NT), MASKED)
            raised = jnp.exp(logits - jnp.max(logits, 0, keepdims=True)) * chosen
            gates = raised / jnp.sum(raised, 0, keepdims=True)
            earlier = dot(chosen.astype(BF16), tri)
            place, gate = [], []
            for j in range(2):
                is_own = experts == own + j
                row = lambda v: jnp.sum(jnp.where(is_own, v, 0.0), 0, keepdims=True)
                hit = (slots == row(earlier)) & (row(chosen) > 0)
                place.append(hit.astype(F32))
                gate.append(jnp.sum(jnp.where(hit, row(gates), 0.0), 1, keepdims=True))
            both = jnp.concatenate(place, 0).astype(BF16)
            sel[s] = both
            xb = dot(both, x).astype(BF16)
            gb = dot(both, cotv[sa, sb, i % 2]).astype(BF16)
            at = pl.ds(pl.multiple_of(group * 512 + i * 64, 64), 64)
            for j in range(2):
                buf[j, at, :] = xb[j * 64 : j * 64 + 64]
                gbuf[j, at, :] = gb[j * 64 : j * 64 + 64]
                gcol[j, at, :] = gate[j]
            return _

        several(8, 4, one)


    def tile(i, _):
        j = i // 2 % 2
        row = (i // 4) * 512 + (i % 2) * 256
        at = pl.ds(pl.multiple_of(row, 256), 256)
        flat = pl.ds(pl.multiple_of(j * 1024 + row, 256), 256)
        act = dot(buf[j, at, :], w_in[j], NT)
        gate, up = act[:, :512], act[:, 512:]
        s = jax.nn.sigmoid(gate)
        h = (gate * s * up).astype(BF16)
        hidden[j, at, :] = h
        produced = dot(h, w_out[j], NT).astype(BF16).astype(F32)
        gate_col = gcol[j, at, :]
        gr = gbuf[j, at, :].astype(F32)
        ggcol[j, at, :] = jnp.sum(gr * produced, 1, keepdims=True)
        gbuf[j, at, :] = (produced * gate_col).astype(BF16)
        gpt = (gr * gate_col).astype(BF16)
        gp[flat, :] = gpt
        gh = dot(gpt, w_out[j])
        ga_gate = (gh * up * s * (1.0 + gate * (1.0 - s))).astype(BF16)
        ga_up = (gh * gate * s).astype(BF16)
        ga = jnp.concatenate([ga_gate, ga_up], 1)
        gact[j, at, :] = ga
        gcopy[j, at, :] = dot(ga, w_in[j]).astype(BF16)
        return _

    def weights(i, _):
        j, d = i // 4, i % 4
        blocks = [
            pl.ds(pl.multiple_of(ctx_slot(lax.rem(ca + d, 4), lax.rem(cb + e, 2)) * 128, 128), 128)
            for e in range(2)
        ]
        lhs = jnp.concatenate([gact[j, :, blk] for blk in blocks], 1)
        gi = dot(lhs, buf[j], TN).astype(BF16)
        here = pl.ds(pl.multiple_of(j * 1024, 1024), 1024)
        lhs = jnp.concatenate([gp[here, blk] for blk in blocks], 1)
        go = dot(lhs, hidden[j], TN).astype(BF16)
        for e in range(2):
            wg[j, d, e, :, :1024] = gi[e * 128 : e * 128 + 128]
            wg[j, d, e, :, 1024:] = go[e * 128 : e * 128 + 128]
        return _

    for _ in range(3):
        next(plan)
    loads.wait(5, 6)
    pick(0)
    lax.fori_loop(0, 4, tile, 0)
    run(plan, cot_plan)
    pick(1)
    lax.fori_loop(4, 6, tile, 0)
    lax.fori_loop(0, 4, weights, 0)
    stores = [pltpu.make_async_copy(wg.at[0, 0], first[0], store.at[0])]
    stores[0].start()
    sent = []

    def along_x(src, dst, k, step):
        sent.append(remote(src, dst, send_x, recv_x, k, ctx_device(around(ca, step), cb)))
        sent[-1].start()

    along_x(wg.at[0, 2, 0], relay.at[0], 0, 1)
    along_x(wg.at[0, 2, 1], relay.at[1], 1, 3)
    lax.fori_loop(6, 8, tile, 0)
    for e, step in ((0, 1), (1, 3)):
        sent[e].wait_recv()
        mine = wg[0, step, e]
        wg[0, step, e] = (mine.astype(F32) + relay[e].astype(F32)).astype(BF16)
        along_x(wg.at[0, step], first[1 + e], 2 + e, step)
    lane = lax.broadcasted_iota(jnp.int32, (64, 128), 1)

    def place_of(sa, sb, c):
        place = lax.rem(sb + wb, 2) * 8 + lax.rem(sa - wa + 4, 4) * 2 + c
        return pl.ds(pl.multiple_of(place * 64, 64), 64)

    def rows(ref, at):
        return jnp.concatenate([ref[0, at, :], ref[1, at, :]], 0)

    def combine(k, _):
        sa, sb = hand_step(k)
        for c in range(2):
            at = place_of(sa, sb, c)
            both = sel[wsh_slot(sa, sb, c)]
            pay[pair_slot(sa, sb), c, :, :1024] = dot(both, rows(gcopy, at), TN).astype(BF16)
            cells = []
            for j in range(2):
                cell = jnp.zeros((64, 128), F32)
                for n, part in enumerate(parts_of(ggcol[j, at, :])):
                    cell = jnp.where(lane == own + j + 32 * n, part.astype(F32), cell)
                cells.append(cell.astype(BF16))
            pay[pair_slot(sa, sb), c, :, 1024:] = dot(both, jnp.concatenate(cells, 0), TN).astype(
                BF16
            )
        hand_over(pay, land_c, sems[6], sems[7], k).start()
        return _

    several(8, 2, combine)

    def out_rows(s, _):
        at = place_of(s // 4, s // 2 % 2, s % 2)
        full[s] = dot(sel[s], rows(gbuf, at), TN).astype(BF16)
        return _

    steps = scatter_wsh_plan(pay, land, land_c, sems[4:8], handed=True)
    next(steps)
    lax.fori_loop(4, 6, weights, 0)
    next(steps)
    lax.fori_loop(6, 8, weights, 0)
    for d, out in enumerate(second):
        stores.append(pltpu.make_async_copy(wg.at[1, d], out, store.at[1 + d]))
        stores[-1].start()
    next(steps)
    next(steps)
    several(16, 4, out_rows)
    run(steps)
    pair, c = own_pair()
    back_o[...] = pay[pair, c]
    for copy in stores:
        copy.wait()
    for copy in sent:
        copy.wait_send()
    for copy in sent[2:]:
        copy.wait_recv()


def experts(x, cot, w_in, w_out, misc, mask, cid):
    t, d, e = 128, 1024, 1024
    wg = ((2, t, 1536), BF16)
    out = talk(
        experts_kernel,
        [((16, t, d), BF16), ((t, 1152), BF16)] + [wg] * 7,
        [
            pltpu.VMEM((128, d), F32),
            pltpu.VMEM((16, 32, t), F32),
            pltpu.VMEM((2, t, 1536), BF16),
            pltpu.VMEM((4, 2, 2, t, d), BF16),
            pltpu.VMEM((2, e, d), BF16),
            pltpu.VMEM((2, d, 512), BF16),
            pltpu.VMEM((16, 128, 128), BF16),
            pltpu.VMEM((2, e, d), BF16),
            pltpu.VMEM((2, e, d), BF16),
            pltpu.VMEM((2, e, 1), F32),
            pltpu.VMEM((2, e, 1), F32),
            pltpu.VMEM((2 * e, d), BF16),
            pltpu.VMEM((2, e, 512), BF16),
            pltpu.VMEM((2, e, d), BF16),
            pltpu.VMEM((2, e, d), BF16),
            pltpu.VMEM((8, 2, t, 1152), BF16),
            pltpu.VMEM((2, 4, 2, t, 1536), BF16),
        ]
        + wsh_land(t, 1152)
        + [pltpu.SemaphoreType.DMA((n,)) for n in (7, 5, 4, 4)]
        + WSH_SEMS * 3,
        cid,
        "experts",
        [ANY] * 6,
        [VMEM] * 2 + [ANY] * 7,
        limit=63,
        flops=80 << 30,
    )(x, cot, w_in, w_out, misc, mask)
    return out[0], out[1], out[2:5], out[5:]


def split_dot(a, b, dims):
    high = a.astype(BF16)
    rest = (a - high.astype(F32)).astype(BF16)
    return dot(high, b, dims) + dot(rest, b, dims)


BACK_PLACES = [
    pltpu.VMEM((8, 2, 128, 1024), BF16),
    pltpu.VMEM((128, 1152), BF16),
    pltpu.VMEM((128, 1024), F32),
    pltpu.VMEM((128, 1024), BF16),
    pltpu.VMEM((128, 1024), F32),
    pltpu.VMEM((128, 1024), BF16),
    pltpu.VMEM((128, 1024), BF16),
    pltpu.VMEM((1024, 1024), BF16),
    pltpu.VMEM((128, 1024), BF16),
    pltpu.VMEM((1024, 1024), BF16),
    pltpu.VMEM((8, 256, 1), F32),
    pltpu.VMEM((1024, 128), F32),
    pltpu.VMEM((1024, 128), F32),
    pltpu.VMEM((1024, 1024), BF16),
    pltpu.VMEM((128, 1024), BF16),
    pltpu.VMEM((1024, 2176), BF16),
]


def back_kernel(chosen_r, *rest):
    count = len(BACK_PLACES)
    loaded, rest = rest[:count], rest[count:]
    experts, rest = rest[:7], rest[7:]
    out_o, tgrad_o, gwq_o, gwk_o, gwv_o, gwo_o, grouter_o, gga_o, ggm_o, gin_o, gout_o = rest[:11]
    rest = rest[11:]
    places, rest = rest[:count], rest[count:]
    load, gm, dkv, gkv, gall, p1, p2, p3, c1, c2, f1, f2, rest = *rest[:12], rest[12:]
    kland, sland1, sland2, oland, oland_c, land1, land1_c, land2, land2_c, land3, land3_c, *rest = rest
    metx, sendy, landy, eload, send_e, recv_e, send_y, recv_y, *sems = rest
    pay, back, mid_r, cot, misc, normed_moe, merged, wo, q, kv, lse, cos, sin = places[:13]
    normed_all, tok, w = places[13:]
    own = lax.axis_index("ctx")
    own_rows = pl.ds(pl.multiple_of(own * 128, 128), 128)
    loads = Loads(loaded, places, load)
    ea, eb = ctx_place()
    eloads = Loads(experts[:4], [metx.at[0, d] for d in range(3)] + [metx.at[1, 0]], eload)
    greet(wsh_peers() + ctx_others())
    alongx = {
        step: remote(
            experts[3 + step], metx.at[1, step], send_e, recv_e, step - 1,
            ctx_device(around(ea, step), eb),
        )
        for step in (1, 2, 3)
    }
    for step in (1, 3, 2):
        alongx[step].start()
    acrossy = [
        remote(sendy.at[j], landy.at[j], send_y, recv_y, j, ctx_device(ea, 1 - eb)) for j in range(2)
    ]

    def total(j):
        def part(e):
            return sum(metx[j, d, e].astype(F32) for d in range(3 + j))

        sendy[j] = part(1).astype(BF16)
        acrossy[j].start()
        kept = part(0)
        gin_o[j] = kept[:, :1024]
        gout_o[j] = kept[:, 1024:]

    loads.wait(0)
    out_plan = scatter_wsh_plan(pay, oland, oland_c, sems[:4])
    next(out_plan)
    eloads.wait(0, 1, 2)
    total(0)
    loads.wait(1, 2, 3, 4, 5, 6, 7)
    mid = mid_r[...]
    cells = back[:, 1024:].astype(F32)
    ggates = cells[:, :32] + cells[:, 32:64] + cells[:, 64:96]
    router = misc[0:32, :].astype(BF16)
    chosen = chosen_r[...]
    logits = jnp.where(chosen > 0, dot(normed_moe[...], router, NT), MASKED)
    raised = jnp.exp(logits - jnp.max(logits, 1, keepdims=True)) * chosen
    gates = raised / jnp.sum(raised, 1, keepdims=True)
    glogits = gates * (ggates - jnp.sum(gates * ggates, 1, keepdims=True))
    scale = rms_scale(mid)
    gnormed = back[:, :1024].astype(F32) + split_dot(glogits, router, (((1,), (0,)), ((), ())))
    grouter = split_dot(glogits, normed_moe[...], TN)
    ggain = jnp.sum(gnormed * mid * scale, 0, keepdims=True)
    gmid = cot[...].astype(F32) + norm_back(gnormed * misc[97:98, :], mid, scale)
    branch = gmid.astype(BF16)
    blocks = lambda v: v.astype(BF16).reshape(8, 2, 64, v.shape[1])
    spare = jnp.zeros((95, 1024), F32)
    p1[:, :, :, 1024:] = blocks(jnp.concatenate([grouter, ggain, spare], 0).T)
    p1[:, :, :, :1024] = blocks(dot(merged[...], branch, TN))
    plan1 = scatter_wsh_plan(p1, land1, land1_c, sems[6:10], wide=True)
    next(plan1)
    gm[...] = dot(branch, wo[...], NT).astype(BF16)
    loads.wait(*range(8, count))
    visible = visible_mask()
    turned = []
    for g in range(8):
        keys = kv[:, g * 64 : g * 64 + 64]
        values = kv[:, 512 + g * 64 : 512 + g * 64 + 64]
        queries, grads = two_heads(q, g), two_heads(gm, g)
        scores = jnp.where(visible, dot(queries, keys, NT) * DH**-0.5, MASKED)
        probs = jnp.exp(scores - lse[g])
        gprobs = dot(grads, values, NT)
        inner = jnp.sum(probs * gprobs, -1, keepdims=True)
        graw = (probs * (gprobs - inner) * DH**-0.5).astype(BF16)
        turned.append(side_by_side(dot(graw, keys)))
        dkv[g * 64 : g * 64 + 64, :] = dot(queries, graw, TN)
        dkv[512 + g * 64 : 512 + g * 64 + 64, :] = dot(grads, probs.astype(BF16), TN)
        if g in (1, 5):
            next(out_plan)
        if g == 3:
            next(plan1)
    for n in range(8):
        at = slice(n * 128, n * 128 + 128)
        gkeys = dkv[:512, at].T
        gkv[n, :, :512] = unrotate(gkeys, wide(cos[at, :], 512), wide(sin[at, :], 512)).astype(BF16)
        gkv[n, :, 512:] = dkv[512:, at].T.astype(BF16)
    partial = gkv[...].reshape(1024, 1024)
    kv_plan = scatter_ctx_plan(gkv, kland, sems[4:6])
    next(kv_plan)
    p2[:, :, :, 1024:] = blocks(dot(normed_all[...], partial, TN))
    c, s = wide(cos[own_rows, :], 1024), wide(sin[own_rows, :], 1024)
    gall[:, :1024] = unrotate(jnp.concatenate(turned, 1), c, s).astype(BF16)
    p2[:, :, :, :1024] = blocks(dot(normed_all[own_rows, :], gall[:, :1024], TN))
    plan2 = scatter_wsh_plan(p2, land2, land2_c, sems[10:14], wide=True)
    next(plan2)
    run(kv_plan, plan1, some(plan2, 2), out_plan)
    pair, core = own_pair()
    for r in range(4):
        mine = p1[pair, core, r * 16 : r * 16 + 16, :]
        c1[2 * r] = mine[:, :640]
        c1[2 * r + 1, :, :512] = mine[:, 640:]
        c1[2 * r + 1, :, 512:] = jnp.zeros((16, 128), BF16)
    sum1 = sum_ctx_plan(c1, sland1, f1, sems[18:22])
    next(sum1)
    out_o[...] = (mid + pay[pair, core].astype(F32)).astype(BF16)
    gall[:, 1024:] = gkv[own]
    x = tok[...].astype(F32)
    scale = rms_scale(x)
    gnormed = dot(gall[...], w[:, :2048], NT)
    ggain = jnp.sum(gnormed * x * scale, 0, keepdims=True)
    p3[...] = blocks(jnp.concatenate([ggain, jnp.zeros((127, 1024), F32)], 0).T)
    plan3 = scatter_wsh_plan(p3, land3, land3_c, sems[14:18])
    next(plan3)
    tgrad_o[...] = (gmid + norm_back(gnormed * misc[96:97, :], x, scale)).astype(BF16)
    next(sum1)
    eloads.wait(3)
    for step in (1, 3, 2):
        alongx[step].wait()
    total(1)
    run(plan2, plan3)
    for r in range(4):
        at = slice(r * 16, r * 16 + 16)
        c2[2 * r, :, :1024] = p2[pair, core, at, :1024]
        c2[2 * r, :, 1024:] = p3[pair, core, at, :]
        c2[2 * r + 1, :, :1024] = p2[pair, core, at, 1024:]
        c2[2 * r + 1, :, 1024:] = jnp.zeros((16, 128), BF16)
    run(sum_ctx_plan(c2, sland2, f2, sems[22:26]), sum1)
    small, gain = [], []
    for r in range(4):
        at = slice(r * 16, r * 16 + 16)
        gwo_o[at, :640] = f1[2 * r].astype(F32)
        gwo_o[at, 640:] = f1[2 * r + 1, :, :384].astype(F32)
        small.append(f1[2 * r + 1, :, 384:512])
        gwq_o[at, :] = f2[2 * r, :, :1024].astype(F32)
        gain.append(f2[2 * r, :, 1024:])
        gwk_o[at, :] = f2[2 * r + 1, :, :512].astype(F32)
        gwv_o[at, :] = f2[2 * r + 1, :, 512:1024].astype(F32)
    small = jnp.concatenate(small, 0).astype(F32).T
    grouter_o[...] = small[:32]
    ggm_o[...] = small[32:33]
    gga_o[...] = jnp.concatenate(gain, 0).astype(F32).T[:1]
    for j in range(2):
        acrossy[j].wait()
        gin_o[j] += landy[j, :, :1024].astype(F32)
        gout_o[j] += landy[j, :, 1024:].astype(F32)


def back_half(*args, cid):
    t, d = 128, 1024
    return talk(
        back_kernel,
        [
            ((t, d), BF16), ((t, d), BF16), ((64, d), F32), ((64, 512), F32), ((64, 512), F32),
            ((64, d), F32), ((32, 64), F32), ((1, 64), F32), ((1, 64), F32), ((2, t, d), F32), ((2, t, 512), F32),
        ],
        BACK_PLACES
        + [
            pltpu.SemaphoreType.DMA((len(BACK_PLACES),)),
            pltpu.VMEM((t, d), BF16),
            pltpu.VMEM((d, d), F32),
            pltpu.VMEM((8, t, d), BF16),
            pltpu.VMEM((t, 2048), BF16),
            pltpu.VMEM((8, 2, 64, 1152), BF16),
            pltpu.VMEM((8, 2, 64, 2048), BF16),
            pltpu.VMEM((8, 2, 64, 128), BF16),
            pltpu.VMEM((8, 16, 640), BF16),
            pltpu.VMEM((8, 16, 1152), BF16),
            pltpu.VMEM((8, 16, 640), BF16),
            pltpu.VMEM((8, 16, 1152), BF16),
            pltpu.VMEM((7, t, d), BF16),
            pltpu.VMEM((7, 16, 640), BF16),
            pltpu.VMEM((7, 16, 1152), BF16),
        ]
        + wsh_land(t, d)
        + wsh_land(64, 1152)
        + wsh_land(64, 2048)
        + wsh_land(64, 128)
        + [
            pltpu.VMEM((2, 4, 2, t, 1536), BF16),
            pltpu.VMEM((2, t, 1536), BF16),
            pltpu.VMEM((2, t, 1536), BF16),
        ]
        + [pltpu.SemaphoreType.DMA((n,)) for n in (4, 3, 3, 2, 2)]
        + WSH_SEMS
        + CTX_SEMS
        + WSH_SEMS * 3
        + CTX_SEMS * 4,
        cid,
        "back",
        [VMEM] + [ANY] * (len(BACK_PLACES) + 7),
        limit=63,
        flops=80 << 30,
    )(*args)


def settle(arrays):
    count = len(arrays)

    def kernel(*refs):
        sources, places, held = refs[:count], refs[count : 2 * count], refs[2 * count : 3 * count]
        loads = Loads(sources, held, refs[-2])
        stores = []
        for k in range(count):
            loads.wait(k)
            stores.append(pltpu.make_async_copy(held[k], places[k], refs[-1].at[k]))
            stores[k].start()
        for copy in stores:
            copy.wait()

    return pl.pallas_call(
        kernel,
        out_shape=[jax.ShapeDtypeStruct(v.shape, v.dtype) for v in arrays],
        in_specs=[ANY] * count,
        out_specs=[ANY] * count,
        scratch_shapes=[pltpu.VMEM(v.shape, v.dtype) for v in arrays]
        + [pltpu.SemaphoreType.DMA((count,))] * 2,
        compiler_params=pltpu.CompilerParams(vmem_limit_bytes=62 << 20),
        name="settle",
    )(*arrays)


def local(
    tokens, gain_attn, w_query, w_key, w_value, w_output, gain_moe, w_router, w_in, w_out, routes,
    cotangent,
):
    tok = tokens.reshape(128, 1024)
    cot = cotangent.reshape(128, 1024)
    angles = np.arange(1024)[:, None] * ROPE_BASE ** (-np.arange(DH // 2) * 2.0 / DH)[None, :]
    cos = jnp.asarray(np.tile(np.cos(angles), (1, 4)).astype(np.float32))
    sin = jnp.asarray(np.tile(np.sin(angles), (1, 4)).astype(np.float32))
    w, kv, cot_all, wo, normed_all, q, misc, mask, merged, mid, normed_moe, lse, own_mask = front(
        tok, w_query, w_key, w_value, w_router.T, gain_attn.reshape(1, 64),
        gain_moe.reshape(1, 64), routes.reshape(128, 8).T, cos, sin, cot, w_output.reshape(4, 16, 1024), cid=0
    )
    pay, back, first, second = experts(normed_moe, cot_all, w_in, w_out, misc, mask, 1)

    results = back_half(
        own_mask, pay.reshape(8, 2, 128, 1024), back, mid, cot, misc, normed_moe, merged, wo.reshape(1024, 1024), q,
        kv, lse, cos, sin, normed_all, tok, w, *first, *second, cid=2,
    )
    output, tokens_grad, gwq, gwk, gwv, gwo, grouter, gga, ggm, gin, gout = settle(results)
    return (
        output.reshape(1, 128, 1024),
        tokens_grad.reshape(1, 128, 1024),
        gga.reshape(64),
        gwq,
        gwk,
        gwv,
        gwo,
        ggm.reshape(64),
        grouter.T,
        gin,
        gout,
    )


def solution(mesh):
    return jax.shard_map(
        local,
        mesh=mesh,
        in_specs=(
            P("wsh", "ctx", None),
            P("wsh"),
            P("wsh", None),
            P("wsh", None),
            P("wsh", None),
            P("wsh", None),
            P("wsh"),
            P("wsh", None),
            P("wsh", None, None),
            P("wsh", None, None),
            P("wsh", "ctx", None, None),
            P("wsh", "ctx", None),
        ),
        out_specs=(
            P("wsh", "ctx", None),
            P("wsh", "ctx", None),
            P("wsh"),
            P("wsh", None),
            P("wsh", None),
            P("wsh", None),
            P("wsh", None),
            P("wsh"),
            P("wsh", None),
            P("wsh", "ctx", None),
            P("wsh", "ctx", None),
        ),
        check_vma=False,
    )
```

```python
import jax
import jax.numpy as jnp
import numpy as np
from jax import lax
from jax.experimental import pallas as pl
from jax.experimental.pallas import tpu as pltpu
from jax.sharding import PartitionSpec as P

MESH = pl.DeviceIdType.MESH
F32 = jnp.float32
BF16 = jnp.bfloat16
DH = 64
EPS = 1e-05
ROPE_BASE = 10000.0
MASKED = -1e30
VMEM = pl.BlockSpec(memory_space=pltpu.VMEM)
NT = (((1,), (1,)), ((), ()))
TN = (((0,), (0,)), ((), ()))


def dot(a, b, dims=(((1,), (0,)), ((), ()))):
    return lax.dot_general(a, b, dims, preferred_element_type=F32)


def wsh_place():
    w = lax.axis_index("wsh")
    return w // 4, (w // 2) % 2, w % 2


def wsh_slot(a, b, core):
    return (a * 2 + b) * 2 + core


def wsh_device(a, b, core):
    return (lax.axis_index("ctx"), wsh_slot(a, b, core))


def ctx_place():
    c = lax.axis_index("ctx")
    return c % 4, c // 4


def ctx_slot(a, b):
    return b * 4 + a


def ctx_device(a, b):
    return (ctx_slot(a, b), lax.axis_index("wsh"))


def around(a, step):
    return lax.rem(a + step, 4)


def greet(peers):
    barrier = pltpu.get_barrier_semaphore()
    for peer in peers:
        pl.semaphore_signal(barrier, inc=1, device_id=peer, device_id_type=MESH)
    pl.semaphore_wait(barrier, len(peers))


def remote(src, dst, send, recv, k, device):
    return pltpu.make_async_remote_copy(
        src_ref=src,
        dst_ref=dst,
        send_sem=send.at[k],
        recv_sem=recv.at[k],
        device_id=device,
        device_id_type=MESH,
    )


def wsh_peers():
    a, b, core = wsh_place()
    return [
        wsh_device(around(a, 1), b, core),
        wsh_device(around(a, 3), b, core),
        wsh_device(around(a, 2), b, core),
        wsh_device(a, 1 - b, core),
        wsh_device(a, b, 1 - core),
    ]


def ctx_peers():
    a, b = ctx_place()
    return [
        ctx_device(around(a, 1), b),
        ctx_device(around(a, 3), b),
        ctx_device(around(a, 2), b),
        ctx_device(a, 1 - b),
    ]


def run(*plans):
    plans = list(plans)
    while plans:
        plans = [p for p in plans if next(p, "end") != "end"]


def gather_plan(at, device, a, b, send, recv, arrived=lambda *_: None):
    up, down, far = around(a, 1), around(a, 3), around(a, 2)
    other = 1 - b

    def push(k, sa, sb, to):
        copy = remote(at(sa, sb), at(sa, sb), send, recv, k, to)
        copy.start()
        return copy

    def landed(k, sa, sb):
        remote(at(sa, sb), at(sa, sb), send, recv, k, device(a, b)).wait_recv()
        arrived(k, sa, sb)

    sent = [
        push(3, a, b, device(a, other)),
        push(0, a, b, device(up, b)),
        push(1, a, b, device(down, b)),
        push(2, a, b, device(far, b)),
    ]
    yield
    landed(3, a, other)
    sent.append(push(4, a, other, device(up, b)))
    sent.append(push(5, a, other, device(down, b)))
    yield
    landed(0, down, b)
    landed(1, up, b)
    yield
    landed(2, far, b)
    sent.append(push(6, far, b, device(a, other)))
    yield
    landed(4, down, other)
    landed(5, up, other)
    yield
    landed(6, far, other)
    for copy in sent:
        copy.wait_send()


def gather_wsh_plan(at, sems, after_same=lambda: None):
    send, recv, send_c, recv_c = sems
    a, b, core = wsh_place()
    mine = lambda sa, sb: at(wsh_slot(sa, sb, core))
    handed = []

    def hand(k, sa, sb):
        sibling = wsh_device(a, b, 1 - core)
        copy = remote(mine(sa, sb), mine(sa, sb), send_c, recv_c, k, sibling)
        copy.start()
        handed.append((copy, k, sa, sb))

    def take(k, sa, sb):
        block = at(wsh_slot(sa, sb, 1 - core))
        remote(block, block, send_c, recv_c, k, wsh_device(a, b, 1 - core)).wait_recv()

    hand(7, a, b)
    device = lambda sa, sb: wsh_device(sa, sb, core)
    steps = gather_plan(mine, device, a, b, send, recv, hand)
    for count, _ in enumerate(steps):
        if count == 3:
            for _, k, sa, sb in handed:
                if k in (7, 0, 1, 2):
                    take(k, sa, sb)
            after_same()
        yield
    for copy, k, sa, sb in handed:
        if k not in (7, 0, 1, 2):
            take(k, sa, sb)
        copy.wait_send()


def wsh_moves(at, sems):
    send, recv, send_c, recv_c = sems
    a, b, core = wsh_place()
    sibling = wsh_device(a, b, 1 - core)
    mine = lambda sa, sb: at(wsh_slot(sa, sb, core))
    sent = []

    def push(k, sa, sb, to):
        sent.append(remote(mine(sa, sb), mine(sa, sb), send, recv, k, wsh_device(*to, core)))
        sent[-1].start()

    def hand(k, sa, sb):
        sent.append(remote(mine(sa, sb), mine(sa, sb), send_c, recv_c, k, sibling))
        sent[-1].start()

    def landed(k, sa, sb):
        remote(mine(sa, sb), mine(sa, sb), send, recv, k, sibling).wait_recv()
        hand(k, sa, sb)

    def finish(*blocks):
        for k, sa, sb in blocks:
            block = at(wsh_slot(sa, sb, 1 - core))
            remote(block, block, send_c, recv_c, k, sibling).wait_recv()
        for copy in sent:
            copy.wait_send()

    return push, hand, landed, finish


def near_plan(at, sems):
    a, b, _ = wsh_place()
    up, down, far, other = around(a, 1), around(a, 3), around(a, 2), 1 - b
    push, hand, landed, finish = wsh_moves(at, sems)
    hand(7, a, b)
    push(3, a, b, (a, other))
    push(0, a, b, (up, b))
    push(1, a, b, (down, b))
    push(2, a, b, (far, b))
    yield
    landed(3, a, other)
    yield
    landed(0, down, b)
    landed(1, up, b)
    yield
    landed(2, far, b)
    yield
    finish((7, a, b), (3, a, other), (0, down, b), (1, up, b), (2, far, b))


def far_plan(at, sems):
    a, b, _ = wsh_place()
    up, down, far, other = around(a, 1), around(a, 3), around(a, 2), 1 - b
    push, _, landed, finish = wsh_moves(at, sems)
    push(4, a, other, (up, b))
    push(5, a, other, (down, b))
    push(6, far, b, (a, other))
    yield
    landed(4, down, other)
    landed(5, up, other)
    yield
    landed(6, far, other)
    yield
    finish((4, down, other), (5, up, other), (6, far, other))


def shared_plan(ref, sems):
    send, recv, send_c, recv_c = sems[4:]
    a, b, core = wsh_place()
    ca, cb = ctx_place()
    sibling = wsh_device(a, b, 1 - core)
    yield from gather_wsh_plan(lambda slot: ref.at[slot // 2, slot % 2, ca], sems[:4])
    part = lambda c, which: ref.at[:, c, which]
    sent = []

    def move(c, which, sem, k, to):
        sent.append(remote(part(c, which), part(c, which), *sem, k, to))
        sent[-1].start()

    for k, step in ((0, 1), (1, 3), (2, 2)):
        move(core, ca, (send, recv), k, ctx_device(around(ca, step), cb))
    for k, step in ((0, 1), (1, 3), (2, 2)):
        yield
        here = around(ca, 4 - step)
        remote(part(core, here), part(core, here), send, recv, k, sibling).wait_recv()
        move(core, here, (send_c, recv_c), k, sibling)
    for k, step in ((0, 1), (1, 3), (2, 2)):
        here = part(1 - core, around(ca, 4 - step))
        remote(here, here, send_c, recv_c, k, sibling).wait_recv()
    for copy in sent:
        copy.wait_send()


def some(plan, count):
    for _ in range(count):
        next(plan)
        yield


def rows_of(ref, rows):
    return lambda slot: ref.at[pl.ds(pl.multiple_of(slot * rows, rows), rows)]


WSH_SEMS = [pltpu.SemaphoreType.DMA((7,))] * 2 + [pltpu.SemaphoreType.DMA((8,))] * 2
CTX_SEMS = [pltpu.SemaphoreType.DMA((7,))] * 2
X_SEMS = [pltpu.SemaphoreType.DMA((3,))] * 4
ANY = pl.BlockSpec(memory_space=pl.ANY)


def talk(kernel, outs, scratch, cid, name, in_specs, out_specs=None, limit=48, flops=0):
    return pl.pallas_call(
        kernel,
        out_shape=[jax.ShapeDtypeStruct(s, d) for s, d in outs],
        in_specs=in_specs,
        out_specs=out_specs or [VMEM] * len(outs),
        scratch_shapes=list(scratch),
        compiler_params=pltpu.CompilerParams(
            collective_id=cid, has_side_effects=True, vmem_limit_bytes=limit << 20
        ),
        cost_estimate=pl.CostEstimate(
            flops=flops, bytes_accessed=1 << 20, transcendentals=0
        ),
        name=name,
    )


def scatter_plan(at, land, device, a, b, send, recv, ready, add, wide=False):
    up, down, far = around(a, 1), around(a, 3), around(a, 2)
    other = 1 - b

    def push(k, sa, sb, to):
        copy = remote(at(sa, sb), land.at[k], send, recv, k, to)
        copy.start()
        return copy

    def landed(k, sa, sb):
        remote(at(sa, sb), land.at[k], send, recv, k, device(a, b)).wait_recv()
        add(sa, sb, k)

    sent = []
    ready(up, other)
    sent.append(push(1, up, other, device(up, b)))
    ready(far, other)
    sent.append(push(0, far, other, device(far, b) if wide else device(a, other)))
    ready(down, other)
    sent.append(push(2, down, other, device(down, b)))
    ready(a, other)
    ready(up, b)
    sent.append(push(3, up, b, device(up, b)))
    ready(far, b)
    ready(down, b)
    sent.append(push(4, down, b, device(down, b)))
    ready(a, b)
    if wide:
        sent.append(push(5, far, b, device(far, b)))
    yield
    if not wide:
        landed(0, far, b)
        sent.append(push(5, far, b, device(far, b)))
    yield
    landed(1, a, other)
    landed(2, a, other)
    if wide:
        landed(0, a, other)
    sent.append(push(6, a, other, device(a, other)))
    yield
    landed(3, a, b)
    landed(4, a, b)
    yield
    landed(5, a, b)
    landed(6, a, b)
    for copy in sent:
        copy.wait_send()


def pair_slot(sa, sb):
    return sa * 2 + sb


def hand_step(k):
    a, b, _ = wsh_place()
    return lax.rem(a + k + 1, 4), lax.rem(b + 1 + k // 4, 2)


def hand_over(p_ref, land_c, send_c, recv_c, k):
    a, b, core = wsh_place()
    return remote(
        p_ref.at[pair_slot(*hand_step(k)), 1 - core],
        land_c.at[k],
        send_c,
        recv_c,
        k,
        wsh_device(a, b, 1 - core),
    )


def scatter_wsh_plan(p_ref, land, land_c, sems, handed=False, wide=False):
    send, recv, send_c, recv_c = sems
    a, b, core = wsh_place()
    copies = [hand_over(p_ref, land_c, send_c, recv_c, k) for k in range(8)]
    if not handed:
        for copy in copies:
            copy.start()
    count = [0]

    def ready(sa, sb):
        k = count[0]
        count[0] += 1
        copies[k].wait_recv()
        at = pair_slot(sa, sb)
        p_ref[at, core] = (p_ref[at, core].astype(F32) + land_c[k].astype(F32)).astype(BF16)

    def add(sa, sb, k):
        at = pair_slot(sa, sb)
        p_ref[at, core] = (p_ref[at, core].astype(F32) + land[k].astype(F32)).astype(BF16)

    device = lambda sa, sb: wsh_device(sa, sb, core)
    block = lambda sa, sb: p_ref.at[pair_slot(sa, sb), core]
    yield from scatter_plan(block, land, device, a, b, send, recv, ready, add, wide)
    for copy in copies:
        copy.wait_send()


def scatter_ctx_plan(p_ref, land, sems):
    a, b = ctx_place()

    def add(sa, sb, k):
        at = ctx_slot(sa, sb)
        p_ref[at] = (p_ref[at].astype(F32) + land[k].astype(F32)).astype(BF16)

    none = lambda *_: None
    block = lambda sa, sb: p_ref.at[ctx_slot(sa, sb)]
    yield from scatter_plan(block, land, ctx_device, a, b, *sems, none, add)


def sum_ctx_plan(p_ref, land, full, sems):
    send, recv, send_f, recv_f = sems
    me = lax.axis_index("ctx")
    peer = lambda d: lax.rem(me + d, 8)
    device = lambda d: (peer(d), lax.axis_index("wsh"))
    near = (4, 1, 7, 5, 3, 2, 6)
    sent = [
        remote(p_ref.at[peer(d)], land.at[d - 1], send, recv, d - 1, device(d)) for d in near
    ]
    for copy in sent:
        copy.start()
    yield
    total = p_ref[me].astype(F32)
    for d in near:
        remote(p_ref.at[me], land.at[d - 1], send, recv, d - 1, device(d)).wait_recv()
        total = total + land[d - 1].astype(F32)
    full[me] = total.astype(BF16)
    for d in near:
        sent.append(remote(full.at[me], full.at[me], send_f, recv_f, d - 1, device(d)))
        sent[-1].start()
    yield
    for d in near:
        here = full.at[peer(8 - d)]
        remote(here, here, send_f, recv_f, d - 1, device(d)).wait_recv()
    for copy in sent:
        copy.wait_send()


def ctx_others():
    me = lax.axis_index("ctx")
    return [(lax.rem(me + d, 8), lax.axis_index("wsh")) for d in range(1, 8)]


def wsh_land(rows, cols):
    return [pltpu.VMEM((7, rows, cols), BF16), pltpu.VMEM((8, rows, cols), BF16)]


def own_pair():
    a, b, core = wsh_place()
    return pair_slot(a, b), core


class Loads:
    def __init__(self, refs, places, sems):
        self.copies = [
            pltpu.make_async_copy(ref, place, sems.at[k])
            for k, (ref, place) in enumerate(zip(refs, places))
        ]
        for copy in self.copies:
            copy.start()

    def wait(self, *which):
        for k in which:
            self.copies[k].wait()


def rms_scale(x):
    return lax.rsqrt(jnp.mean(x * x, -1, keepdims=True) + EPS)


def norm_back(u, x, scale):
    return scale * u - x * scale * scale * scale * jnp.mean(u * x, -1, keepdims=True)


def low_half(shape):
    return lax.broadcasted_iota(jnp.int32, shape, len(shape) - 1) % DH < DH // 2


def rotate(v, cos, sin):
    width = v.shape[-1]
    turned = jnp.where(
        low_half(v.shape), -pltpu.roll(v, width - DH // 2, 1), pltpu.roll(v, DH // 2, 1)
    )
    return v * cos + turned * sin


def unrotate(v, cos, sin):
    width = v.shape[-1]
    scaled = v * sin
    turned = jnp.where(
        low_half(v.shape), pltpu.roll(scaled, width - DH // 2, 1), -pltpu.roll(scaled, DH // 2, 1)
    )
    return v * cos + turned


def two_heads(ref, g):
    return jnp.concatenate(
        [ref[:, g * 128 : g * 128 + 64], ref[:, g * 128 + 64 : g * 128 + 128]], 0
    )


def side_by_side(rows):
    return jnp.concatenate([rows[:128], rows[128:]], 1)


def visible_mask():
    row = lax.broadcasted_iota(jnp.int32, (256, 1024), 0) % 128
    col = lax.broadcasted_iota(jnp.int32, (256, 1024), 1)
    return col <= row + lax.axis_index("ctx") * 128


def wide(table, width):
    return jnp.concatenate([table] * (width // 128), 1)


def block_of(ref):
    return lambda slot: ref.at[slot // 4, slot // 2 % 2, slot % 2]


def front_kernel(
    tok, wq, wk, wv, router_r, gain_a, gain_m, routes_r, cos_r, sin_r, cot, wo_r,
    w_o, kv_o, cot_o, wo_o, normed_all_o, q, misc, mask_o, merged_o, mid_o, normed_moe_o, lse_o, own_o,
    w, kv, cot_all, wo, normed_all, tok_all, cos, sin, load, store, *sems,
):
    own = lax.axis_index("wsh")
    here = pl.ds(pl.multiple_of(own * 64, 64), 64)
    ca, cb = ctx_place()
    rows = pl.ds(pl.multiple_of(ctx_slot(ca, cb) * 128, 128), 128)
    cot_at = block_of(cot_all)
    loads = Loads(
        [wq, wk, wv, tok, cos_r, sin_r, wo_r.at[ca], cot],
        [
            w.at[here, :1024],
            w.at[here, 1024:1536],
            w.at[here, 1536:2048],
            tok_all.at[rows],
            cos,
            sin,
            wo.at[own // 2, own % 2, ca],
            cot_at(own),
        ],
        load,
    )
    expert = lax.broadcasted_iota(jnp.int32, (32, 128), 0)
    named = jnp.zeros((32, 128), F32)
    for k in range(8):
        named = named + jnp.where(routes_r[k : k + 1, :] == expert, 1.0, 0.0)
    own_o[...] = named.T
    small = jnp.concatenate(
        [
            router_r[...].astype(F32),
            named[:, :64],
            named[:, 64:],
            gain_a[...].astype(F32),
            gain_m[...].astype(F32),
            jnp.zeros((30, 64), F32),
        ],
        0,
    )
    w[here, 2048:] = small.T.astype(BF16)
    greet(wsh_peers() + ctx_peers())
    loads.wait(0, 1, 2)
    w_plan = gather_wsh_plan(rows_of(w, 64), sems[:4])
    tok_at = lambda sa, sb: rows_of(tok_all, 128)(ctx_slot(sa, sb))
    tok_plan = gather_plan(tok_at, ctx_device, ca, cb, *sems[4:6])
    next(w_plan)
    loads.wait(3, 6)
    next(tok_plan)
    wo_plan = shared_plan(wo, sems[6:14])
    next(wo_plan)
    loads.wait(4, 5, 7)
    run(w_plan, tok_plan, some(wo_plan, 4))
    next(wo_plan)
    cot_plan = near_plan(cot_at, sems[14:18])
    next(cot_plan)
    stores = []

    def leave(src, dst):
        stores.append(pltpu.make_async_copy(src, dst, store.at[len(stores)]))
        stores[-1].start()

    leave(w, w_o)
    misc[...] = w[:, 2048:2176].astype(F32).T
    gain = misc[96:97, :]

    def sequence(i, _):
        at = pl.ds(pl.multiple_of(i * 256, 256), 256)
        x = tok_all[at, :].astype(F32)
        normed = (x * rms_scale(x) * gain).astype(BF16)
        normed_all[at, :] = normed
        c, s = wide(cos[at, :], 512), wide(sin[at, :], 512)
        kv[at, :512] = rotate(dot(normed, w[:, 1024:1536]), c, s).astype(BF16)
        kv[at, 512:] = dot(normed, w[:, 1536:2048]).astype(BF16)
        return _

    lax.fori_loop(0, 4, sequence, 0)
    leave(kv, kv_o)
    leave(normed_all, normed_all_o)
    c, s = wide(cos[rows, :], 1024), wide(sin[rows, :], 1024)
    q[...] = rotate(dot(normed_all[rows, :], w[:, :1024]), c, s).astype(BF16)
    for n in range(16):
        lanes = slice(n * 64, n * 64 + 64)
        mask_o[n] = jnp.concatenate([misc[32:64, lanes], misc[64:96, lanes]], 1)
    visible = visible_mask()
    for g in range(8):
        keys = kv[:, g * 64 : g * 64 + 64]
        values = kv[:, 512 + g * 64 : 512 + g * 64 + 64]
        scores = jnp.where(visible, dot(two_heads(q, g), keys, NT) * DH**-0.5, MASKED)
        top = jnp.max(scores, -1, keepdims=True)
        raised = jnp.exp(scores - top)
        total = jnp.sum(raised, -1, keepdims=True)
        lse_o[g] = top + jnp.log(total)
        probs = (raised * (1.0 / total)).astype(BF16)
        merged_o[:, g * 128 : g * 128 + 128] = side_by_side(dot(probs, values)).astype(BF16)
        if g in (3, 6):
            next(wo_plan)
        if g in (2, 4, 7):
            next(cot_plan)
    run(wo_plan)
    leave(wo, wo_o)
    mid = tok_all[rows, :].astype(F32) + dot(merged_o[...], wo[...].reshape(1024, 1024))
    mid_o[...] = mid
    normed_moe_o[...] = (mid * rms_scale(mid) * misc[97:98, :]).astype(BF16)
    run(cot_plan)
    wa, wb, _ = wsh_place()
    leave(cot_all.at[:, wb], cot_o.at[:, wb])
    leave(cot_all.at[wa, 1 - wb], cot_o.at[wa, 1 - wb])
    for copy in stores:
        copy.wait()


def front(*args, cid):
    t, d = 128, 1024
    return talk(
        front_kernel,
        [
            ((d, 2176), BF16), ((d, d), BF16), ((4, 2, 2, t, d), BF16), ((8, 2, 4, 16, d), BF16),
            ((d, d), BF16), ((t, d), BF16), ((128, d), F32), ((16, 32, 128), F32),
            ((t, d), BF16), ((t, d), F32), ((t, d), BF16), ((8, 256, 1), F32), ((t, 32), F32),
        ],
        [
            pltpu.VMEM((d, 2176), BF16),
            pltpu.VMEM((d, d), BF16),
            pltpu.VMEM((4, 2, 2, t, d), BF16),
            pltpu.VMEM((8, 2, 4, 16, d), BF16),
            pltpu.VMEM((d, d), BF16),
            pltpu.VMEM((d, d), BF16),
            pltpu.VMEM((d, 128), F32),
            pltpu.VMEM((d, 128), F32),
            pltpu.SemaphoreType.DMA((8,)),
            pltpu.SemaphoreType.DMA((6,)),
        ]
        + WSH_SEMS
        + CTX_SEMS
        + WSH_SEMS
        + X_SEMS
        + WSH_SEMS,
        cid,
        "front",
        [ANY] * 4 + [VMEM] * 4 + [ANY] * 4,
        [ANY] * 5 + [VMEM] * 8,
        limit=56,
        flops=60 << 30,
    )(*args)


def several(count, each, body):
    def step(i, _):
        for k in range(each):
            body(i * each + k, None)
        return _

    lax.fori_loop(0, count // each, step, 0)


def parts_of(v):
    high = v.astype(BF16)
    rest = v - high.astype(F32)
    middle = rest.astype(BF16)
    return high, middle, (rest - middle.astype(F32)).astype(BF16)


def experts_kernel(
    x_r, cot, w_in_r, w_out_r, misc_r, mask_r, full_o, back_o, *rest,
):
    first, second, rest = rest[:3], rest[3:7], rest[7:]
    misc, mask, rest = rest[0], rest[1], rest[2:]
    full, relay, cotv, w_in, w_out, sel, buf, gbuf, gcol, ggcol, gp, hidden, gact, gcopy, pay, wg = rest[:16]
    land, land_c, load, store, send_x, recv_x, *sems = rest[16:]
    wa, wb, core = wsh_place()
    ca, cb = ctx_place()
    loads = Loads(
        [x_r, misc_r, mask_r, cot.at[:, wb], cot.at[wa, 1 - wb], w_in_r, w_out_r],
        [
            full.at[wsh_slot(wa, wb, core)],
            misc,
            mask,
            cotv.at[:, wb],
            cotv.at[wa, 1 - wb],
            w_in,
            w_out,
        ],
        load,
    )
    own = lax.axis_index("wsh") * 2
    tri = (
        lax.broadcasted_iota(jnp.int32, (128, 128), 0)
        < lax.broadcasted_iota(jnp.int32, (128, 128), 1)
    ).astype(BF16)
    across_x = [ctx_device(around(ca, step), cb) for step in (1, 3, 2)]
    greet(wsh_peers() + across_x)
    loads.wait(0)
    cot_plan = far_plan(block_of(cotv), sems[8:12])
    plan = gather_wsh_plan(lambda slot: full.at[slot], sems[:4], lambda: next(cot_plan))
    next(plan)
    loads.wait(1, 2, 3, 4)
    router = misc[0:32, :].astype(BF16)
    experts = lax.broadcasted_iota(jnp.int32, (32, 128), 0)
    slots = lax.broadcasted_iota(jnp.int32, (64, 128), 0).astype(F32)

    def pick(group):
        def one(i, _):
            sa, sb = lax.rem(wa + i // 2, 4), lax.rem(wb + group, 2)
            s = wsh_slot(sa, sb, i % 2)
            chosen = mask[s]
            x = full[s]
            logits = jnp.where(chosen > 0, dot(router, x, NT), MASKED)
            raised = jnp.exp(logits - jnp.max(logits, 0, keepdims=True)) * chosen
            gates = raised / jnp.sum(raised, 0, keepdims=True)
            earlier = dot(chosen.astype(BF16), tri)
            place, gate = [], []
            for j in range(2):
                is_own = experts == own + j
                row = lambda v: jnp.sum(jnp.where(is_own, v, 0.0), 0, keepdims=True)
                hit = (slots == row(earlier)) & (row(chosen) > 0)
                place.append(hit.astype(F32))
                gate.append(jnp.sum(jnp.where(hit, row(gates), 0.0), 1, keepdims=True))
            both = jnp.concatenate(place, 0).astype(BF16)
            sel[s] = both
            xb = dot(both, x).astype(BF16)
            gb = dot(both, cotv[sa, sb, i % 2]).astype(BF16)
            at = pl.ds(pl.multiple_of(group * 512 + i * 64, 64), 64)
            for j in range(2):
                buf[j, at, :] = xb[j * 64 : j * 64 + 64]
                gbuf[j, at, :] = gb[j * 64 : j * 64 + 64]
                gcol[j, at, :] = gate[j]
            return _

        several(8, 4, one)


    def tile(i, _):
        j = i // 2 % 2
        row = (i // 4) * 512 + (i % 2) * 256
        at = pl.ds(pl.multiple_of(row, 256), 256)
        flat = pl.ds(pl.multiple_of(j * 1024 + row, 256), 256)
        act = dot(buf[j, at, :], w_in[j], NT)
        gate, up = act[:, :512], act[:, 512:]
        s = jax.nn.sigmoid(gate)
        h = (gate * s * up).astype(BF16)
        hidden[j, at, :] = h
        produced = dot(h, w_out[j], NT).astype(BF16).astype(F32)
        gate_col = gcol[j, at, :]
        gr = gbuf[j, at, :].astype(F32)
        ggcol[j, at, :] = jnp.sum(gr * produced, 1, keepdims=True)
        gbuf[j, at, :] = (produced * gate_col).astype(BF16)
        gpt = (gr * gate_col).astype(BF16)
        gp[flat, :] = gpt
        gh = dot(gpt, w_out[j])
        ga_gate = (gh * up * s * (1.0 + gate * (1.0 - s))).astype(BF16)
        ga_up = (gh * gate * s).astype(BF16)
        ga = jnp.concatenate([ga_gate, ga_up], 1)
        gact[j, at, :] = ga
        gcopy[j, at, :] = dot(ga, w_in[j]).astype(BF16)
        return _

    def weights(i, _):
        j, d = i // 4, i % 4
        blocks = [
            pl.ds(pl.multiple_of(ctx_slot(lax.rem(ca + d, 4), lax.rem(cb + e, 2)) * 128, 128), 128)
            for e in range(2)
        ]
        lhs = jnp.concatenate([gact[j, :, blk] for blk in blocks], 1)
        gi = dot(lhs, buf[j], TN).astype(BF16)
        here = pl.ds(pl.multiple_of(j * 1024, 1024), 1024)
        lhs = jnp.concatenate([gp[here, blk] for blk in blocks], 1)
        go = dot(lhs, hidden[j], TN).astype(BF16)
        for e in range(2):
            wg[j, d, e, :, :1024] = gi[e * 128 : e * 128 + 128]
            wg[j, d, e, :, 1024:] = go[e * 128 : e * 128 + 128]
        return _

    for _ in range(3):
        next(plan)
    loads.wait(5, 6)
    pick(0)
    lax.fori_loop(0, 4, tile, 0)
    run(plan, cot_plan)
    pick(1)
    lax.fori_loop(4, 6, tile, 0)
    lax.fori_loop(0, 4, weights, 0)
    stores = [pltpu.make_async_copy(wg.at[0, 0], first[0], store.at[0])]
    stores[0].start()
    sent = []

    def along_x(src, dst, k, step):
        sent.append(remote(src, dst, send_x, recv_x, k, ctx_device(around(ca, step), cb)))
        sent[-1].start()

    along_x(wg.at[0, 2, 0], relay.at[0], 0, 1)
    along_x(wg.at[0, 2, 1], relay.at[1], 1, 3)
    lax.fori_loop(6, 8, tile, 0)
    lane = lax.broadcasted_iota(jnp.int32, (64, 128), 1)

    def place_of(sa, sb, c):
        place = lax.rem(sb + wb, 2) * 8 + lax.rem(sa - wa + 4, 4) * 2 + c
        return pl.ds(pl.multiple_of(place * 64, 64), 64)

    def rows(ref, at):
        return jnp.concatenate([ref[0, at, :], ref[1, at, :]], 0)

    def combine(k, _):
        sa, sb = hand_step(k)
        for c in range(2):
            at = place_of(sa, sb, c)
            both = sel[wsh_slot(sa, sb, c)]
            pay[pair_slot(sa, sb), c, :, :1024] = dot(both, rows(gcopy, at), TN).astype(BF16)
            cells = []
            for j in range(2):
                cell = jnp.zeros((64, 128), F32)
                for n, part in enumerate(parts_of(ggcol[j, at, :])):
                    cell = jnp.where(lane == own + j + 32 * n, part.astype(F32), cell)
                cells.append(cell.astype(BF16))
            pay[pair_slot(sa, sb), c, :, 1024:] = dot(both, jnp.concatenate(cells, 0), TN).astype(
                BF16
            )
        hand_over(pay, land_c, sems[6], sems[7], k).start()
        return _

    several(8, 2, combine)

    def out_rows(s, _):
        at = place_of(s // 4, s // 2 % 2, s % 2)
        full[s] = dot(sel[s], rows(gbuf, at), TN).astype(BF16)
        return _

    steps = scatter_wsh_plan(pay, land, land_c, sems[4:8], handed=True)
    next(steps)
    for e, step in ((0, 1), (1, 3)):
        sent[e].wait_recv()
        mine = wg[0, step, e]
        wg[0, step, e] = (mine.astype(F32) + relay[e].astype(F32)).astype(BF16)
        along_x(wg.at[0, step], first[1 + e], 2 + e, step)
    lax.fori_loop(4, 6, weights, 0)
    next(steps)
    lax.fori_loop(6, 8, weights, 0)
    for d, out in enumerate(second):
        stores.append(pltpu.make_async_copy(wg.at[1, d], out, store.at[1 + d]))
        stores[-1].start()
    next(steps)
    next(steps)
    several(16, 4, out_rows)
    stores.append(pltpu.make_async_copy(full, full_o, store.at[5]))
    stores[-1].start()
    run(steps)
    pair, c = own_pair()
    back_o[...] = pay[pair, c]
    for copy in stores:
        copy.wait()
    for copy in sent:
        copy.wait_send()
    for copy in sent[2:]:
        copy.wait_recv()


def experts(x, cot, w_in, w_out, misc, mask, cid):
    t, d, e = 128, 1024, 1024
    wg = ((2, t, 1536), BF16)
    out = talk(
        experts_kernel,
        [((16, t, d), BF16), ((t, 1152), BF16)] + [wg] * 7,
        [
            pltpu.VMEM((128, d), F32),
            pltpu.VMEM((16, 32, t), F32),
            pltpu.VMEM((16, t, d), BF16),
            pltpu.VMEM((2, t, 1536), BF16),
            pltpu.VMEM((4, 2, 2, t, d), BF16),
            pltpu.VMEM((2, e, d), BF16),
            pltpu.VMEM((2, d, 512), BF16),
            pltpu.VMEM((16, 128, 128), BF16),
            pltpu.VMEM((2, e, d), BF16),
            pltpu.VMEM((2, e, d), BF16),
            pltpu.VMEM((2, e, 1), F32),
            pltpu.VMEM((2, e, 1), F32),
            pltpu.VMEM((2 * e, d), BF16),
            pltpu.VMEM((2, e, 512), BF16),
            pltpu.VMEM((2, e, d), BF16),
            pltpu.VMEM((2, e, d), BF16),
            pltpu.VMEM((8, 2, t, 1152), BF16),
            pltpu.VMEM((2, 4, 2, t, 1536), BF16),
        ]
        + wsh_land(t, 1152)
        + [pltpu.SemaphoreType.DMA((n,)) for n in (7, 6, 4, 4)]
        + WSH_SEMS * 3,
        cid,
        "experts",
        [ANY] * 6,
        [ANY, VMEM] + [ANY] * 7,
        limit=63,
        flops=80 << 30,
    )(x, cot, w_in, w_out, misc, mask)
    return out[0], out[1], out[2:5], out[5:]


def split_dot(a, b, dims):
    high = a.astype(BF16)
    rest = (a - high.astype(F32)).astype(BF16)
    return dot(high, b, dims) + dot(rest, b, dims)


BACK_PLACES = [
    pltpu.VMEM((8, 2, 128, 1024), BF16),
    pltpu.VMEM((128, 1152), BF16),
    pltpu.VMEM((128, 1024), F32),
    pltpu.VMEM((128, 1024), BF16),
    pltpu.VMEM((128, 1024), F32),
    pltpu.VMEM((128, 1024), BF16),
    pltpu.VMEM((128, 1024), BF16),
    pltpu.VMEM((1024, 1024), BF16),
    pltpu.VMEM((128, 1024), BF16),
    pltpu.VMEM((1024, 1024), BF16),
    pltpu.VMEM((8, 256, 1), F32),
    pltpu.VMEM((1024, 128), F32),
    pltpu.VMEM((1024, 128), F32),
    pltpu.VMEM((1024, 1024), BF16),
    pltpu.VMEM((128, 1024), BF16),
    pltpu.VMEM((1024, 2176), BF16),
]


def back_kernel(chosen_r, *rest):
    count = len(BACK_PLACES)
    loaded, rest = rest[:count], rest[count:]
    experts, rest = rest[:7], rest[7:]
    out_o, tgrad_o, gwq_o, gwk_o, gwv_o, gwo_o, grouter_o, gga_o, ggm_o, gin_o, gout_o = rest[:11]
    rest = rest[11:]
    places, rest = rest[:count], rest[count:]
    load, gm, dkv, gkv, gall, p1, p2, p3, c1, c2, f1, f2, rest = *rest[:12], rest[12:]
    kland, sland1, sland2, oland, oland_c, land1, land1_c, land2, land2_c, land3, land3_c, *rest = rest
    metx, sendy, landy, eload, send_e, recv_e, send_y, recv_y, *sems = rest
    pay, back, mid_r, cot, misc, normed_moe, merged, wo, q, kv, lse, cos, sin = places[:13]
    normed_all, tok, w = places[13:]
    own = lax.axis_index("ctx")
    own_rows = pl.ds(pl.multiple_of(own * 128, 128), 128)
    loads = Loads(loaded, places, load)
    ea, eb = ctx_place()
    eloads = Loads(experts[:4], [metx.at[0, d] for d in range(3)] + [metx.at[1, 0]], eload)
    greet(wsh_peers() + ctx_others())
    alongx = {
        step: remote(
            experts[3 + step], metx.at[1, step], send_e, recv_e, step - 1,
            ctx_device(around(ea, step), eb),
        )
        for step in (1, 2, 3)
    }
    for step in (1, 3, 2):
        alongx[step].start()
    acrossy = [
        remote(sendy.at[j], landy.at[j], send_y, recv_y, j, ctx_device(ea, 1 - eb)) for j in range(2)
    ]

    def total(j):
        def part(e):
            return sum(metx[j, d, e].astype(F32) for d in range(3 + j))

        sendy[j] = part(1).astype(BF16)
        acrossy[j].start()
        kept = part(0)
        gin_o[j] = kept[:, :1024]
        gout_o[j] = kept[:, 1024:]

    loads.wait(0)
    out_plan = scatter_wsh_plan(pay, oland, oland_c, sems[:4])
    next(out_plan)
    loads.wait(1, 2, 3, 4, 5, 6, 7)
    mid = mid_r[...]
    cells = back[:, 1024:].astype(F32)
    ggates = cells[:, :32] + cells[:, 32:64] + cells[:, 64:96]
    router = misc[0:32, :].astype(BF16)
    chosen = chosen_r[...]
    logits = jnp.where(chosen > 0, dot(normed_moe[...], router, NT), MASKED)
    raised = jnp.exp(logits - jnp.max(logits, 1, keepdims=True)) * chosen
    gates = raised / jnp.sum(raised, 1, keepdims=True)
    glogits = gates * (ggates - jnp.sum(gates * ggates, 1, keepdims=True))
    scale = rms_scale(mid)
    gnormed = back[:, :1024].astype(F32) + split_dot(glogits, router, (((1,), (0,)), ((), ())))
    grouter = split_dot(glogits, normed_moe[...], TN)
    ggain = jnp.sum(gnormed * mid * scale, 0, keepdims=True)
    gmid = cot[...].astype(F32) + norm_back(gnormed * misc[97:98, :], mid, scale)
    branch = gmid.astype(BF16)
    blocks = lambda v: v.astype(BF16).reshape(8, 2, 64, v.shape[1])
    spare = jnp.zeros((95, 1024), F32)
    p1[:, :, :, 1024:] = blocks(jnp.concatenate([grouter, ggain, spare], 0).T)
    p1[:, :, :, :1024] = blocks(dot(merged[...], branch, TN))
    plan1 = scatter_wsh_plan(p1, land1, land1_c, sems[6:10], wide=True)
    next(plan1)
    gm[...] = dot(branch, wo[...], NT).astype(BF16)
    loads.wait(*range(8, count))
    visible = visible_mask()
    turned = []
    for g in range(8):
        keys = kv[:, g * 64 : g * 64 + 64]
        values = kv[:, 512 + g * 64 : 512 + g * 64 + 64]
        queries, grads = two_heads(q, g), two_heads(gm, g)
        scores = jnp.where(visible, dot(queries, keys, NT) * DH**-0.5, MASKED)
        probs = jnp.exp(scores - lse[g])
        gprobs = dot(grads, values, NT)
        inner = jnp.sum(probs * gprobs, -1, keepdims=True)
        graw = (probs * (gprobs - inner) * DH**-0.5).astype(BF16)
        turned.append(side_by_side(dot(graw, keys)))
        dkv[g * 64 : g * 64 + 64, :] = dot(queries, graw, TN)
        dkv[512 + g * 64 : 512 + g * 64 + 64, :] = dot(grads, probs.astype(BF16), TN)
        if g in (1, 5):
            next(out_plan)
        if g == 3:
            next(plan1)
    for n in range(8):
        at = slice(n * 128, n * 128 + 128)
        gkeys = dkv[:512, at].T
        gkv[n, :, :512] = unrotate(gkeys, wide(cos[at, :], 512), wide(sin[at, :], 512)).astype(BF16)
        gkv[n, :, 512:] = dkv[512:, at].T.astype(BF16)
    partial = gkv[...].reshape(1024, 1024)
    kv_plan = scatter_ctx_plan(gkv, kland, sems[4:6])
    next(kv_plan)
    p2[:, :, :, 1024:] = blocks(dot(normed_all[...], partial, TN))
    c, s = wide(cos[own_rows, :], 1024), wide(sin[own_rows, :], 1024)
    gall[:, :1024] = unrotate(jnp.concatenate(turned, 1), c, s).astype(BF16)
    p2[:, :, :, :1024] = blocks(dot(normed_all[own_rows, :], gall[:, :1024], TN))
    plan2 = scatter_wsh_plan(p2, land2, land2_c, sems[10:14], wide=True)
    next(plan2)
    eloads.wait(0, 1, 2)
    total(0)
    run(kv_plan, plan1, some(plan2, 2), out_plan)
    pair, core = own_pair()
    for r in range(4):
        mine = p1[pair, core, r * 16 : r * 16 + 16, :]
        c1[2 * r] = mine[:, :640]
        c1[2 * r + 1, :, :512] = mine[:, 640:]
        c1[2 * r + 1, :, 512:] = jnp.zeros((16, 128), BF16)
    sum1 = sum_ctx_plan(c1, sland1, f1, sems[18:22])
    next(sum1)
    out_o[...] = (mid + pay[pair, core].astype(F32)).astype(BF16)
    gall[:, 1024:] = gkv[own]
    x = tok[...].astype(F32)
    scale = rms_scale(x)
    gnormed = dot(gall[...], w[:, :2048], NT)
    ggain = jnp.sum(gnormed * x * scale, 0, keepdims=True)
    p3[...] = blocks(jnp.concatenate([ggain, jnp.zeros((127, 1024), F32)], 0).T)
    plan3 = scatter_wsh_plan(p3, land3, land3_c, sems[14:18])
    next(plan3)
    tgrad_o[...] = (gmid + norm_back(gnormed * misc[96:97, :], x, scale)).astype(BF16)
    next(sum1)
    eloads.wait(3)
    for step in (1, 3, 2):
        alongx[step].wait()
    total(1)
    run(plan2, plan3)
    for r in range(4):
        at = slice(r * 16, r * 16 + 16)
        c2[2 * r, :, :1024] = p2[pair, core, at, :1024]
        c2[2 * r, :, 1024:] = p3[pair, core, at, :]
        c2[2 * r + 1, :, :1024] = p2[pair, core, at, 1024:]
        c2[2 * r + 1, :, 1024:] = jnp.zeros((16, 128), BF16)
    run(sum_ctx_plan(c2, sland2, f2, sems[22:26]), sum1)
    small, gain = [], []
    for r in range(4):
        at = slice(r * 16, r * 16 + 16)
        gwo_o[at, :640] = f1[2 * r].astype(F32)
        gwo_o[at, 640:] = f1[2 * r + 1, :, :384].astype(F32)
        small.append(f1[2 * r + 1, :, 384:512])
        gwq_o[at, :] = f2[2 * r, :, :1024].astype(F32)
        gain.append(f2[2 * r, :, 1024:])
        gwk_o[at, :] = f2[2 * r + 1, :, :512].astype(F32)
        gwv_o[at, :] = f2[2 * r + 1, :, 512:1024].astype(F32)
    small = jnp.concatenate(small, 0).astype(F32).T
    grouter_o[...] = small[:32]
    ggm_o[...] = small[32:33]
    gga_o[...] = jnp.concatenate(gain, 0).astype(F32).T[:1]
    for j in range(2):
        acrossy[j].wait()
        gin_o[j] += landy[j, :, :1024].astype(F32)
        gout_o[j] += landy[j, :, 1024:].astype(F32)


def back_half(*args, cid):
    t, d = 128, 1024
    return talk(
        back_kernel,
        [
            ((t, d), BF16), ((t, d), BF16), ((64, d), F32), ((64, 512), F32), ((64, 512), F32),
            ((64, d), F32), ((32, 64), F32), ((1, 64), F32), ((1, 64), F32), ((2, t, d), F32), ((2, t, 512), F32),
        ],
        BACK_PLACES
        + [
            pltpu.SemaphoreType.DMA((len(BACK_PLACES),)),
            pltpu.VMEM((t, d), BF16),
            pltpu.VMEM((d, d), F32),
            pltpu.VMEM((8, t, d), BF16),
            pltpu.VMEM((t, 2048), BF16),
            pltpu.VMEM((8, 2, 64, 1152), BF16),
            pltpu.VMEM((8, 2, 64, 2048), BF16),
            pltpu.VMEM((8, 2, 64, 128), BF16),
            pltpu.VMEM((8, 16, 640), BF16),
            pltpu.VMEM((8, 16, 1152), BF16),
            pltpu.VMEM((8, 16, 640), BF16),
            pltpu.VMEM((8, 16, 1152), BF16),
            pltpu.VMEM((7, t, d), BF16),
            pltpu.VMEM((7, 16, 640), BF16),
            pltpu.VMEM((7, 16, 1152), BF16),
        ]
        + wsh_land(t, d)
        + wsh_land(64, 1152)
        + wsh_land(64, 2048)
        + wsh_land(64, 128)
        + [
            pltpu.VMEM((2, 4, 2, t, 1536), BF16),
            pltpu.VMEM((2, t, 1536), BF16),
            pltpu.VMEM((2, t, 1536), BF16),
        ]
        + [pltpu.SemaphoreType.DMA((n,)) for n in (4, 3, 3, 2, 2)]
        + WSH_SEMS
        + CTX_SEMS
        + WSH_SEMS * 3
        + CTX_SEMS * 4,
        cid,
        "back",
        [VMEM] + [ANY] * (len(BACK_PLACES) + 7),
        limit=63,
        flops=80 << 30,
    )(*args)


def settle(arrays):
    count = len(arrays)

    def kernel(*refs):
        sources, places, held = refs[:count], refs[count : 2 * count], refs[2 * count : 3 * count]
        loads = Loads(sources, held, refs[-2])
        stores = []
        for k in range(count):
            loads.wait(k)
            stores.append(pltpu.make_async_copy(held[k], places[k], refs[-1].at[k]))
            stores[k].start()
        for copy in stores:
            copy.wait()

    return pl.pallas_call(
        kernel,
        out_shape=[jax.ShapeDtypeStruct(v.shape, v.dtype) for v in arrays],
        in_specs=[ANY] * count,
        out_specs=[ANY] * count,
        scratch_shapes=[pltpu.VMEM(v.shape, v.dtype) for v in arrays]
        + [pltpu.SemaphoreType.DMA((count,))] * 2,
        compiler_params=pltpu.CompilerParams(vmem_limit_bytes=62 << 20),
        name="settle",
    )(*arrays)


def local(
    tokens, gain_attn, w_query, w_key, w_value, w_output, gain_moe, w_router, w_in, w_out, routes,
    cotangent,
):
    tok = tokens.reshape(128, 1024)
    cot = cotangent.reshape(128, 1024)
    angles = np.arange(1024)[:, None] * ROPE_BASE ** (-np.arange(DH // 2) * 2.0 / DH)[None, :]
    cos = jnp.asarray(np.tile(np.cos(angles), (1, 4)).astype(np.float32))
    sin = jnp.asarray(np.tile(np.sin(angles), (1, 4)).astype(np.float32))
    w, kv, cot_all, wo, normed_all, q, misc, mask, merged, mid, normed_moe, lse, own_mask = front(
        tok, w_query, w_key, w_value, w_router.T, gain_attn.reshape(1, 64),
        gain_moe.reshape(1, 64), routes.reshape(128, 8).T, cos, sin, cot, w_output.reshape(4, 16, 1024), cid=0
    )
    pay, back, first, second = experts(normed_moe, cot_all, w_in, w_out, misc, mask, 1)

    results = back_half(
        own_mask, pay.reshape(8, 2, 128, 1024), back, mid, cot, misc, normed_moe, merged, wo.reshape(1024, 1024), q,
        kv, lse, cos, sin, normed_all, tok, w, *first, *second, cid=2,
    )
    output, tokens_grad, gwq, gwk, gwv, gwo, grouter, gga, ggm, gin, gout = settle(results)
    return (
        output.reshape(1, 128, 1024),
        tokens_grad.reshape(1, 128, 1024),
        gga.reshape(64),
        gwq,
        gwk,
        gwv,
        gwo,
        ggm.reshape(64),
        grouter.T,
        gin,
        gout,
    )


def solution(mesh):
    return jax.shard_map(
        local,
        mesh=mesh,
        in_specs=(
            P("wsh", "ctx", None),
            P("wsh"),
            P("wsh", None),
            P("wsh", None),
            P("wsh", None),
            P("wsh", None),
            P("wsh"),
            P("wsh", None),
            P("wsh", None, None),
            P("wsh", None, None),
            P("wsh", "ctx", None, None),
            P("wsh", "ctx", None),
        ),
        out_specs=(
            P("wsh", "ctx", None),
            P("wsh", "ctx", None),
            P("wsh"),
            P("wsh", None),
            P("wsh", None),
            P("wsh", None),
            P("wsh", None),
            P("wsh"),
            P("wsh", None),
            P("wsh", "ctx", None),
            P("wsh", "ctx", None),
        ),
        check_vma=False,
    )
```

```python
import jax
import jax.numpy as jnp
import numpy as np
from jax import lax
from jax.experimental import pallas as pl
from jax.experimental.pallas import tpu as pltpu
from jax.sharding import PartitionSpec as P

MESH = pl.DeviceIdType.MESH
F32 = jnp.float32
BF16 = jnp.bfloat16
DH = 64
EPS = 1e-05
ROPE_BASE = 10000.0
MASKED = -1e30
VMEM = pl.BlockSpec(memory_space=pltpu.VMEM)
NT = (((1,), (1,)), ((), ()))
TN = (((0,), (0,)), ((), ()))


def dot(a, b, dims=(((1,), (0,)), ((), ()))):
    return lax.dot_general(a, b, dims, preferred_element_type=F32)


def wsh_place():
    w = lax.axis_index("wsh")
    return w // 4, (w // 2) % 2, w % 2


def wsh_slot(a, b, core):
    return (a * 2 + b) * 2 + core


def wsh_device(a, b, core):
    return (lax.axis_index("ctx"), wsh_slot(a, b, core))


def ctx_place():
    c = lax.axis_index("ctx")
    return c % 4, c // 4


def ctx_slot(a, b):
    return b * 4 + a


def ctx_device(a, b):
    return (ctx_slot(a, b), lax.axis_index("wsh"))


def around(a, step):
    return lax.rem(a + step, 4)


def greet(peers):
    barrier = pltpu.get_barrier_semaphore()
    for peer in peers:
        pl.semaphore_signal(barrier, inc=1, device_id=peer, device_id_type=MESH)
    pl.semaphore_wait(barrier, len(peers))


def remote(src, dst, send, recv, k, device):
    return pltpu.make_async_remote_copy(
        src_ref=src,
        dst_ref=dst,
        send_sem=send.at[k],
        recv_sem=recv.at[k],
        device_id=device,
        device_id_type=MESH,
    )


def wsh_peers():
    a, b, core = wsh_place()
    return [
        wsh_device(around(a, 1), b, core),
        wsh_device(around(a, 3), b, core),
        wsh_device(around(a, 2), b, core),
        wsh_device(a, 1 - b, core),
        wsh_device(a, b, 1 - core),
    ]


def ctx_peers():
    a, b = ctx_place()
    return [
        ctx_device(around(a, 1), b),
        ctx_device(around(a, 3), b),
        ctx_device(around(a, 2), b),
        ctx_device(a, 1 - b),
    ]


def run(*plans):
    plans = list(plans)
    while plans:
        plans = [p for p in plans if next(p, "end") != "end"]


def gather_plan(at, device, a, b, send, recv, arrived=lambda *_: None):
    up, down, far = around(a, 1), around(a, 3), around(a, 2)
    other = 1 - b

    def push(k, sa, sb, to):
        copy = remote(at(sa, sb), at(sa, sb), send, recv, k, to)
        copy.start()
        return copy

    def landed(k, sa, sb):
        remote(at(sa, sb), at(sa, sb), send, recv, k, device(a, b)).wait_recv()
        arrived(k, sa, sb)

    sent = [
        push(3, a, b, device(a, other)),
        push(0, a, b, device(up, b)),
        push(1, a, b, device(down, b)),
        push(2, a, b, device(far, b)),
    ]
    yield
    landed(3, a, other)
    sent.append(push(4, a, other, device(up, b)))
    sent.append(push(5, a, other, device(down, b)))
    yield
    landed(0, down, b)
    landed(1, up, b)
    yield
    landed(2, far, b)
    sent.append(push(6, far, b, device(a, other)))
    yield
    landed(4, down, other)
    landed(5, up, other)
    yield
    landed(6, far, other)
    for copy in sent:
        copy.wait_send()


def gather_wsh_plan(at, sems, after_same=lambda: None):
    send, recv, send_c, recv_c = sems
    a, b, core = wsh_place()
    mine = lambda sa, sb: at(wsh_slot(sa, sb, core))
    handed = []

    def hand(k, sa, sb):
        sibling = wsh_device(a, b, 1 - core)
        copy = remote(mine(sa, sb), mine(sa, sb), send_c, recv_c, k, sibling)
        copy.start()
        handed.append((copy, k, sa, sb))

    def take(k, sa, sb):
        block = at(wsh_slot(sa, sb, 1 - core))
        remote(block, block, send_c, recv_c, k, wsh_device(a, b, 1 - core)).wait_recv()

    hand(7, a, b)
    device = lambda sa, sb: wsh_device(sa, sb, core)
    steps = gather_plan(mine, device, a, b, send, recv, hand)
    for count, _ in enumerate(steps):
        if count == 3:
            for _, k, sa, sb in handed:
                if k in (7, 0, 1, 2):
                    take(k, sa, sb)
            after_same()
        yield
    for copy, k, sa, sb in handed:
        if k not in (7, 0, 1, 2):
            take(k, sa, sb)
        copy.wait_send()


def wsh_moves(at, sems):
    send, recv, send_c, recv_c = sems
    a, b, core = wsh_place()
    sibling = wsh_device(a, b, 1 - core)
    mine = lambda sa, sb: at(wsh_slot(sa, sb, core))
    sent = []

    def push(k, sa, sb, to):
        sent.append(remote(mine(sa, sb), mine(sa, sb), send, recv, k, wsh_device(*to, core)))
        sent[-1].start()

    def hand(k, sa, sb):
        sent.append(remote(mine(sa, sb), mine(sa, sb), send_c, recv_c, k, sibling))
        sent[-1].start()

    def landed(k, sa, sb):
        remote(mine(sa, sb), mine(sa, sb), send, recv, k, sibling).wait_recv()
        hand(k, sa, sb)

    def finish(*blocks):
        for k, sa, sb in blocks:
            block = at(wsh_slot(sa, sb, 1 - core))
            remote(block, block, send_c, recv_c, k, sibling).wait_recv()
        for copy in sent:
            copy.wait_send()

    return push, hand, landed, finish


def near_plan(at, sems):
    a, b, _ = wsh_place()
    up, down, far, other = around(a, 1), around(a, 3), around(a, 2), 1 - b
    push, hand, landed, finish = wsh_moves(at, sems)
    hand(7, a, b)
    push(3, a, b, (a, other))
    push(0, a, b, (up, b))
    push(1, a, b, (down, b))
    push(2, a, b, (far, b))
    yield
    landed(3, a, other)
    yield
    landed(0, down, b)
    landed(1, up, b)
    yield
    landed(2, far, b)
    yield
    finish((7, a, b), (3, a, other), (0, down, b), (1, up, b), (2, far, b))


def far_plan(at, sems):
    a, b, _ = wsh_place()
    up, down, far, other = around(a, 1), around(a, 3), around(a, 2), 1 - b
    push, _, landed, finish = wsh_moves(at, sems)
    push(4, a, other, (up, b))
    push(5, a, other, (down, b))
    push(6, far, b, (a, other))
    yield
    landed(4, down, other)
    landed(5, up, other)
    yield
    landed(6, far, other)
    yield
    finish((4, down, other), (5, up, other), (6, far, other))


def shared_plan(ref, sems):
    send, recv, send_c, recv_c = sems[4:]
    a, b, core = wsh_place()
    ca, cb = ctx_place()
    sibling = wsh_device(a, b, 1 - core)
    yield from gather_wsh_plan(lambda slot: ref.at[slot // 2, slot % 2, ca], sems[:4])
    part = lambda c, which: ref.at[:, c, which]
    sent = []

    def move(c, which, sem, k, to):
        sent.append(remote(part(c, which), part(c, which), *sem, k, to))
        sent[-1].start()

    for k, step in ((0, 1), (1, 3), (2, 2)):
        move(core, ca, (send, recv), k, ctx_device(around(ca, step), cb))
    for k, step in ((0, 1), (1, 3), (2, 2)):
        yield
        here = around(ca, 4 - step)
        remote(part(core, here), part(core, here), send, recv, k, sibling).wait_recv()
        move(core, here, (send_c, recv_c), k, sibling)
    for k, step in ((0, 1), (1, 3), (2, 2)):
        here = part(1 - core, around(ca, 4 - step))
        remote(here, here, send_c, recv_c, k, sibling).wait_recv()
    for copy in sent:
        copy.wait_send()


def some(plan, count):
    for _ in range(count):
        next(plan)
        yield


def rows_of(ref, rows):
    return lambda slot: ref.at[pl.ds(pl.multiple_of(slot * rows, rows), rows)]


WSH_SEMS = [pltpu.SemaphoreType.DMA((7,))] * 2 + [pltpu.SemaphoreType.DMA((8,))] * 2
CTX_SEMS = [pltpu.SemaphoreType.DMA((7,))] * 2
X_SEMS = [pltpu.SemaphoreType.DMA((3,))] * 4
ANY = pl.BlockSpec(memory_space=pl.ANY)


def talk(kernel, outs, scratch, cid, name, in_specs, out_specs=None, limit=48, flops=0):
    return pl.pallas_call(
        kernel,
        out_shape=[jax.ShapeDtypeStruct(s, d) for s, d in outs],
        in_specs=in_specs,
        out_specs=out_specs or [VMEM] * len(outs),
        scratch_shapes=list(scratch),
        compiler_params=pltpu.CompilerParams(
            collective_id=cid, has_side_effects=True, vmem_limit_bytes=limit << 20
        ),
        cost_estimate=pl.CostEstimate(
            flops=flops, bytes_accessed=1 << 20, transcendentals=0
        ),
        name=name,
    )


def scatter_plan(at, land, device, a, b, send, recv, ready, add, wide=False):
    up, down, far = around(a, 1), around(a, 3), around(a, 2)
    other = 1 - b

    def push(k, sa, sb, to):
        copy = remote(at(sa, sb), land.at[k], send, recv, k, to)
        copy.start()
        return copy

    def landed(k, sa, sb):
        remote(at(sa, sb), land.at[k], send, recv, k, device(a, b)).wait_recv()
        add(sa, sb, k)

    sent = []
    ready(up, other)
    sent.append(push(1, up, other, device(up, b)))
    ready(far, other)
    sent.append(push(0, far, other, device(far, b) if wide else device(a, other)))
    ready(down, other)
    sent.append(push(2, down, other, device(down, b)))
    ready(a, other)
    ready(up, b)
    sent.append(push(3, up, b, device(up, b)))
    ready(far, b)
    ready(down, b)
    sent.append(push(4, down, b, device(down, b)))
    ready(a, b)
    if wide:
        sent.append(push(5, far, b, device(far, b)))
    yield
    if not wide:
        landed(0, far, b)
        sent.append(push(5, far, b, device(far, b)))
    yield
    landed(1, a, other)
    landed(2, a, other)
    if wide:
        landed(0, a, other)
    sent.append(push(6, a, other, device(a, other)))
    yield
    landed(3, a, b)
    landed(4, a, b)
    yield
    landed(5, a, b)
    landed(6, a, b)
    for copy in sent:
        copy.wait_send()


def pair_slot(sa, sb):
    return sa * 2 + sb


def hand_step(k):
    a, b, _ = wsh_place()
    return lax.rem(a + k + 1, 4), lax.rem(b + 1 + k // 4, 2)


def hand_over(p_ref, land_c, send_c, recv_c, k):
    a, b, core = wsh_place()
    return remote(
        p_ref.at[pair_slot(*hand_step(k)), 1 - core],
        land_c.at[k],
        send_c,
        recv_c,
        k,
        wsh_device(a, b, 1 - core),
    )


def scatter_wsh_plan(p_ref, land, land_c, sems, handed=False, wide=False):
    send, recv, send_c, recv_c = sems
    a, b, core = wsh_place()
    copies = [hand_over(p_ref, land_c, send_c, recv_c, k) for k in range(8)]
    if not handed:
        for copy in copies:
            copy.start()
    count = [0]

    def ready(sa, sb):
        k = count[0]
        count[0] += 1
        copies[k].wait_recv()
        at = pair_slot(sa, sb)
        p_ref[at, core] = (p_ref[at, core].astype(F32) + land_c[k].astype(F32)).astype(BF16)

    def add(sa, sb, k):
        at = pair_slot(sa, sb)
        p_ref[at, core] = (p_ref[at, core].astype(F32) + land[k].astype(F32)).astype(BF16)

    device = lambda sa, sb: wsh_device(sa, sb, core)
    block = lambda sa, sb: p_ref.at[pair_slot(sa, sb), core]
    yield from scatter_plan(block, land, device, a, b, send, recv, ready, add, wide)
    for copy in copies:
        copy.wait_send()


def scatter_ctx_plan(p_ref, land, sems):
    a, b = ctx_place()

    def add(sa, sb, k):
        at = ctx_slot(sa, sb)
        p_ref[at] = (p_ref[at].astype(F32) + land[k].astype(F32)).astype(BF16)

    none = lambda *_: None
    block = lambda sa, sb: p_ref.at[ctx_slot(sa, sb)]
    yield from scatter_plan(block, land, ctx_device, a, b, *sems, none, add)


def sum_ctx_plan(p_ref, land, full, sems):
    send, recv, send_f, recv_f = sems
    me = lax.axis_index("ctx")
    peer = lambda d: lax.rem(me + d, 8)
    device = lambda d: (peer(d), lax.axis_index("wsh"))
    near = (4, 1, 7, 5, 3, 2, 6)
    sent = [
        remote(p_ref.at[peer(d)], land.at[d - 1], send, recv, d - 1, device(d)) for d in near
    ]
    for copy in sent:
        copy.start()
    yield
    total = p_ref[me].astype(F32)
    for d in near:
        remote(p_ref.at[me], land.at[d - 1], send, recv, d - 1, device(d)).wait_recv()
        total = total + land[d - 1].astype(F32)
    full[me] = total.astype(BF16)
    for d in near:
        sent.append(remote(full.at[me], full.at[me], send_f, recv_f, d - 1, device(d)))
        sent[-1].start()
    yield
    for d in near:
        here = full.at[peer(8 - d)]
        remote(here, here, send_f, recv_f, d - 1, device(d)).wait_recv()
    for copy in sent:
        copy.wait_send()


def ctx_others():
    me = lax.axis_index("ctx")
    return [(lax.rem(me + d, 8), lax.axis_index("wsh")) for d in range(1, 8)]


def wsh_land(rows, cols):
    return [pltpu.VMEM((7, rows, cols), BF16), pltpu.VMEM((8, rows, cols), BF16)]


def own_pair():
    a, b, core = wsh_place()
    return pair_slot(a, b), core


class Loads:
    def __init__(self, refs, places, sems, later=()):
        self.copies = [
            pltpu.make_async_copy(ref, place, sems.at[k])
            for k, (ref, place) in enumerate(zip(refs, places))
        ]
        self.start(*(k for k in range(len(refs)) if k not in later))

    def start(self, *which):
        for k in which:
            self.copies[k].start()

    def wait(self, *which):
        for k in which:
            self.copies[k].wait()


def rms_scale(x):
    return lax.rsqrt(jnp.mean(x * x, -1, keepdims=True) + EPS)


def norm_back(u, x, scale):
    return scale * u - x * scale * scale * scale * jnp.mean(u * x, -1, keepdims=True)


def low_half(shape):
    return lax.broadcasted_iota(jnp.int32, shape, len(shape) - 1) % DH < DH // 2


def rotate(v, cos, sin):
    width = v.shape[-1]
    turned = jnp.where(
        low_half(v.shape), -pltpu.roll(v, width - DH // 2, 1), pltpu.roll(v, DH // 2, 1)
    )
    return v * cos + turned * sin


def unrotate(v, cos, sin):
    width = v.shape[-1]
    scaled = v * sin
    turned = jnp.where(
        low_half(v.shape), pltpu.roll(scaled, width - DH // 2, 1), -pltpu.roll(scaled, DH // 2, 1)
    )
    return v * cos + turned


def two_heads(ref, g):
    return jnp.concatenate(
        [ref[:, g * 128 : g * 128 + 64], ref[:, g * 128 + 64 : g * 128 + 128]], 0
    )


def side_by_side(rows):
    return jnp.concatenate([rows[:128], rows[128:]], 1)


def visible_mask():
    row = lax.broadcasted_iota(jnp.int32, (256, 1024), 0) % 128
    col = lax.broadcasted_iota(jnp.int32, (256, 1024), 1)
    return col <= row + lax.axis_index("ctx") * 128


def wide(table, width):
    return jnp.concatenate([table] * (width // 128), 1)


def block_of(ref):
    return lambda slot: ref.at[slot // 4, slot // 2 % 2, slot % 2]


def front_kernel(
    tok, wq, wk, wv, router_r, gain_a, gain_m, routes_r, cos_r, sin_r, cot, wo_r,
    w_o, kv_o, cot_o, wo_o, normed_all_o, q, misc, mask_o, merged_o, mid_o, normed_moe_o, lse_o, own_o,
    w, kv, cot_all, wo, normed_all, tok_all, cos, sin, load, store, *sems,
):
    own = lax.axis_index("wsh")
    here = pl.ds(pl.multiple_of(own * 64, 64), 64)
    ca, cb = ctx_place()
    rows = pl.ds(pl.multiple_of(ctx_slot(ca, cb) * 128, 128), 128)
    cot_at = block_of(cot_all)
    loads = Loads(
        [wq, wk, wv, tok, cos_r, sin_r, wo_r.at[ca], cot],
        [
            w.at[here, :1024],
            w.at[here, 1024:1536],
            w.at[here, 1536:2048],
            tok_all.at[rows],
            cos,
            sin,
            wo.at[own // 2, own % 2, ca],
            cot_at(own),
        ],
        load,
    )
    expert = lax.broadcasted_iota(jnp.int32, (32, 128), 0)
    named = jnp.zeros((32, 128), F32)
    for k in range(8):
        named = named + jnp.where(routes_r[k : k + 1, :] == expert, 1.0, 0.0)
    own_o[...] = named.T
    small = jnp.concatenate(
        [
            router_r[...].astype(F32),
            named[:, :64],
            named[:, 64:],
            gain_a[...].astype(F32),
            gain_m[...].astype(F32),
            jnp.zeros((30, 64), F32),
        ],
        0,
    )
    w[here, 2048:] = small.T.astype(BF16)
    greet(wsh_peers() + ctx_peers())
    loads.wait(0, 1, 2)
    w_plan = gather_wsh_plan(rows_of(w, 64), sems[:4])
    tok_at = lambda sa, sb: rows_of(tok_all, 128)(ctx_slot(sa, sb))
    tok_plan = gather_plan(tok_at, ctx_device, ca, cb, *sems[4:6])
    next(w_plan)
    loads.wait(3, 6)
    next(tok_plan)
    wo_plan = shared_plan(wo, sems[6:14])
    next(wo_plan)
    loads.wait(4, 5, 7)
    run(w_plan, tok_plan, some(wo_plan, 4))
    next(wo_plan)
    cot_plan = near_plan(cot_at, sems[14:18])
    next(cot_plan)
    stores = []

    def leave(src, dst):
        stores.append(pltpu.make_async_copy(src, dst, store.at[len(stores)]))
        stores[-1].start()

    leave(w, w_o)
    misc[...] = w[:, 2048:2176].astype(F32).T
    gain = misc[96:97, :]

    def sequence(i, _):
        at = pl.ds(pl.multiple_of(i * 256, 256), 256)
        x = tok_all[at, :].astype(F32)
        normed = (x * rms_scale(x) * gain).astype(BF16)
        normed_all[at, :] = normed
        c, s = wide(cos[at, :], 512), wide(sin[at, :], 512)
        kv[at, :512] = rotate(dot(normed, w[:, 1024:1536]), c, s).astype(BF16)
        kv[at, 512:] = dot(normed, w[:, 1536:2048]).astype(BF16)
        return _

    lax.fori_loop(0, 4, sequence, 0)
    leave(kv, kv_o)
    leave(normed_all, normed_all_o)
    c, s = wide(cos[rows, :], 1024), wide(sin[rows, :], 1024)
    q[...] = rotate(dot(normed_all[rows, :], w[:, :1024]), c, s).astype(BF16)
    for n in range(16):
        lanes = slice(n * 64, n * 64 + 64)
        mask_o[n] = jnp.concatenate([misc[32:64, lanes], misc[64:96, lanes]], 1)
    visible = visible_mask()
    for g in range(8):
        keys = kv[:, g * 64 : g * 64 + 64]
        values = kv[:, 512 + g * 64 : 512 + g * 64 + 64]
        scores = jnp.where(visible, dot(two_heads(q, g), keys, NT) * DH**-0.5, MASKED)
        top = jnp.max(scores, -1, keepdims=True)
        raised = jnp.exp(scores - top)
        total = jnp.sum(raised, -1, keepdims=True)
        lse_o[g] = top + jnp.log(total)
        probs = (raised * (1.0 / total)).astype(BF16)
        merged_o[:, g * 128 : g * 128 + 128] = side_by_side(dot(probs, values)).astype(BF16)
        if g in (3, 6):
            next(wo_plan)
        if g in (2, 4, 7):
            next(cot_plan)
    run(wo_plan)
    leave(wo, wo_o)
    mid = tok_all[rows, :].astype(F32) + dot(merged_o[...], wo[...].reshape(1024, 1024))
    mid_o[...] = mid
    normed_moe_o[...] = (mid * rms_scale(mid) * misc[97:98, :]).astype(BF16)
    run(cot_plan)
    wa, wb, _ = wsh_place()
    leave(cot_all.at[:, wb], cot_o.at[:, wb])
    leave(cot_all.at[wa, 1 - wb], cot_o.at[wa, 1 - wb])
    for copy in stores:
        copy.wait()


def front(*args, cid):
    t, d = 128, 1024
    return talk(
        front_kernel,
        [
            ((d, 2176), BF16), ((d, d), BF16), ((4, 2, 2, t, d), BF16), ((8, 2, 4, 16, d), BF16),
            ((d, d), BF16), ((t, d), BF16), ((128, d), F32), ((16, 32, 128), F32),
            ((t, d), BF16), ((t, d), F32), ((t, d), BF16), ((8, 256, 1), F32), ((t, 32), F32),
        ],
        [
            pltpu.VMEM((d, 2176), BF16),
            pltpu.VMEM((d, d), BF16),
            pltpu.VMEM((4, 2, 2, t, d), BF16),
            pltpu.VMEM((8, 2, 4, 16, d), BF16),
            pltpu.VMEM((d, d), BF16),
            pltpu.VMEM((d, d), BF16),
            pltpu.VMEM((d, 128), F32),
            pltpu.VMEM((d, 128), F32),
            pltpu.SemaphoreType.DMA((8,)),
            pltpu.SemaphoreType.DMA((6,)),
        ]
        + WSH_SEMS
        + CTX_SEMS
        + WSH_SEMS
        + X_SEMS
        + WSH_SEMS,
        cid,
        "front",
        [ANY] * 4 + [VMEM] * 4 + [ANY] * 4,
        [ANY] * 5 + [VMEM] * 8,
        limit=56,
        flops=60 << 30,
    )(*args)


def several(count, each, body):
    def step(i, _):
        for k in range(each):
            body(i * each + k, None)
        return _

    lax.fori_loop(0, count // each, step, 0)


def parts_of(v):
    high = v.astype(BF16)
    rest = v - high.astype(F32)
    middle = rest.astype(BF16)
    return high, middle, (rest - middle.astype(F32)).astype(BF16)


def experts_kernel(
    x_r, cot, w_in_r, w_out_r, misc_r, mask_r, full_o, back_o, *rest,
):
    first, second, rest = rest[:3], rest[3:7], rest[7:]
    misc, mask, rest = rest[0], rest[1], rest[2:]
    full, relay, cotv, w_in, w_out, sel, buf, gbuf, gcol, ggcol, gp, hidden, gact, gcopy, pay, wg = rest[:16]
    land, land_c, load, store, send_x, recv_x, *sems = rest[16:]
    wa, wb, core = wsh_place()
    ca, cb = ctx_place()
    loads = Loads(
        [x_r, misc_r, mask_r, cot.at[:, wb], cot.at[wa, 1 - wb], w_in_r, w_out_r],
        [
            full.at[wsh_slot(wa, wb, core)],
            misc,
            mask,
            cotv.at[:, wb],
            cotv.at[wa, 1 - wb],
            w_in,
            w_out,
        ],
        load,
        later=(5, 6),
    )
    own = lax.axis_index("wsh") * 2
    tri = (
        lax.broadcasted_iota(jnp.int32, (128, 128), 0)
        < lax.broadcasted_iota(jnp.int32, (128, 128), 1)
    ).astype(BF16)
    across_x = [ctx_device(around(ca, step), cb) for step in (1, 3, 2)]
    greet(wsh_peers() + across_x)
    loads.wait(0)
    cot_plan = far_plan(block_of(cotv), sems[8:12])
    plan = gather_wsh_plan(lambda slot: full.at[slot], sems[:4], lambda: next(cot_plan))
    next(plan)
    loads.wait(1, 2, 3, 4)
    loads.start(5, 6)
    router = misc[0:32, :].astype(BF16)
    experts = lax.broadcasted_iota(jnp.int32, (32, 128), 0)
    slots = lax.broadcasted_iota(jnp.int32, (64, 128), 0).astype(F32)

    def pick(group):
        def one(i, _):
            sa, sb = lax.rem(wa + i // 2, 4), lax.rem(wb + group, 2)
            s = wsh_slot(sa, sb, i % 2)
            chosen = mask[s]
            x = full[s]
            logits = jnp.where(chosen > 0, dot(router, x, NT), MASKED)
            raised = jnp.exp(logits - jnp.max(logits, 0, keepdims=True)) * chosen
            gates = raised / jnp.sum(raised, 0, keepdims=True)
            earlier = dot(chosen.astype(BF16), tri)
            place, gate = [], []
            for j in range(2):
                is_own = experts == own + j
                row = lambda v: jnp.sum(jnp.where(is_own, v, 0.0), 0, keepdims=True)
                hit = (slots == row(earlier)) & (row(chosen) > 0)
                place.append(hit.astype(F32))
                gate.append(jnp.sum(jnp.where(hit, row(gates), 0.0), 1, keepdims=True))
            both = jnp.concatenate(place, 0).astype(BF16)
            sel[s] = both
            xb = dot(both, x).astype(BF16)
            gb = dot(both, cotv[sa, sb, i % 2]).astype(BF16)
            at = pl.ds(pl.multiple_of(group * 512 + i * 64, 64), 64)
            for j in range(2):
                buf[j, at, :] = xb[j * 64 : j * 64 + 64]
                gbuf[j, at, :] = gb[j * 64 : j * 64 + 64]
                gcol[j, at, :] = gate[j]
            return _

        several(8, 4, one)


    def tile(i, _):
        j = i // 2 % 2
        row = (i // 4) * 512 + (i % 2) * 256
        at = pl.ds(pl.multiple_of(row, 256), 256)
        flat = pl.ds(pl.multiple_of(j * 1024 + row, 256), 256)
        act = dot(buf[j, at, :], w_in[j], NT)
        gate, up = act[:, :512], act[:, 512:]
        s = jax.nn.sigmoid(gate)
        h = (gate * s * up).astype(BF16)
        hidden[j, at, :] = h
        produced = dot(h, w_out[j], NT).astype(BF16).astype(F32)
        gate_col = gcol[j, at, :]
        gr = gbuf[j, at, :].astype(F32)
        ggcol[j, at, :] = jnp.sum(gr * produced, 1, keepdims=True)
        gbuf[j, at, :] = (produced * gate_col).astype(BF16)
        gpt = (gr * gate_col).astype(BF16)
        gp[flat, :] = gpt
        gh = dot(gpt, w_out[j])
        ga_gate = (gh * up * s * (1.0 + gate * (1.0 - s))).astype(BF16)
        ga_up = (gh * gate * s).astype(BF16)
        ga = jnp.concatenate([ga_gate, ga_up], 1)
        gact[j, at, :] = ga
        gcopy[j, at, :] = dot(ga, w_in[j]).astype(BF16)
        return _

    def weights(i, _):
        j, d = i // 4, i % 4
        blocks = [
            pl.ds(pl.multiple_of(ctx_slot(lax.rem(ca + d, 4), lax.rem(cb + e, 2)) * 128, 128), 128)
            for e in range(2)
        ]
        lhs = jnp.concatenate([gact[j, :, blk] for blk in blocks], 1)
        gi = dot(lhs, buf[j], TN).astype(BF16)
        here = pl.ds(pl.multiple_of(j * 1024, 1024), 1024)
        lhs = jnp.concatenate([gp[here, blk] for blk in blocks], 1)
        go = dot(lhs, hidden[j], TN).astype(BF16)
        for e in range(2):
            wg[j, d, e, :, :1024] = gi[e * 128 : e * 128 + 128]
            wg[j, d, e, :, 1024:] = go[e * 128 : e * 128 + 128]
        return _

    for _ in range(3):
        next(plan)
    loads.wait(5, 6)
    pick(0)
    several(4, 2, tile)
    run(plan, cot_plan)
    pick(1)
    lax.fori_loop(4, 6, tile, 0)
    lax.fori_loop(0, 4, weights, 0)
    stores = [pltpu.make_async_copy(wg.at[0, 0], first[0], store.at[0])]
    stores[0].start()
    sent = []

    def along_x(src, dst, k, step):
        sent.append(remote(src, dst, send_x, recv_x, k, ctx_device(around(ca, step), cb)))
        sent[-1].start()

    along_x(wg.at[0, 2, 0], relay.at[0], 0, 1)
    along_x(wg.at[0, 2, 1], relay.at[1], 1, 3)
    lax.fori_loop(6, 8, tile, 0)
    lane = lax.broadcasted_iota(jnp.int32, (64, 128), 1)

    def place_of(sa, sb, c):
        place = lax.rem(sb + wb, 2) * 8 + lax.rem(sa - wa + 4, 4) * 2 + c
        return pl.ds(pl.multiple_of(place * 64, 64), 64)

    def rows(ref, at):
        return jnp.concatenate([ref[0, at, :], ref[1, at, :]], 0)

    def combine(k, _):
        sa, sb = hand_step(k)
        for c in range(2):
            at = place_of(sa, sb, c)
            both = sel[wsh_slot(sa, sb, c)]
            pay[pair_slot(sa, sb), c, :, :1024] = dot(both, rows(gcopy, at), TN).astype(BF16)
            cells = []
            for j in range(2):
                cell = jnp.zeros((64, 128), F32)
                for n, part in enumerate(parts_of(ggcol[j, at, :])):
                    cell = jnp.where(lane == own + j + 32 * n, part.astype(F32), cell)
                cells.append(cell.astype(BF16))
            pay[pair_slot(sa, sb), c, :, 1024:] = dot(both, jnp.concatenate(cells, 0), TN).astype(
                BF16
            )
        hand_over(pay, land_c, sems[6], sems[7], k).start()
        return _

    several(8, 2, combine)

    def out_rows(s, _):
        at = place_of(s // 4, s // 2 % 2, s % 2)
        full[s] = dot(sel[s], rows(gbuf, at), TN).astype(BF16)
        return _

    steps = scatter_wsh_plan(pay, land, land_c, sems[4:8], handed=True)
    next(steps)
    for e, step in ((0, 1), (1, 3)):
        sent[e].wait_recv()
        mine = wg[0, step, e]
        wg[0, step, e] = (mine.astype(F32) + relay[e].astype(F32)).astype(BF16)
        along_x(wg.at[0, step], first[1 + e], 2 + e, step)
    lax.fori_loop(4, 6, weights, 0)
    next(steps)
    lax.fori_loop(6, 8, weights, 0)
    for d, out in enumerate(second):
        stores.append(pltpu.make_async_copy(wg.at[1, d], out, store.at[1 + d]))
        stores[-1].start()
    next(steps)
    next(steps)
    several(16, 4, out_rows)
    stores.append(pltpu.make_async_copy(full, full_o, store.at[5]))
    stores[-1].start()
    run(steps)
    pair, c = own_pair()
    back_o[...] = pay[pair, c]
    for copy in stores:
        copy.wait()
    for copy in sent:
        copy.wait_send()
    for copy in sent[2:]:
        copy.wait_recv()


def experts(x, cot, w_in, w_out, misc, mask, cid):
    t, d, e = 128, 1024, 1024
    wg = ((2, t, 1536), BF16)
    out = talk(
        experts_kernel,
        [((16, t, d), BF16), ((t, 1152), BF16)] + [wg] * 7,
        [
            pltpu.VMEM((128, d), F32),
            pltpu.VMEM((16, 32, t), F32),
            pltpu.VMEM((16, t, d), BF16),
            pltpu.VMEM((2, t, 1536), BF16),
            pltpu.VMEM((4, 2, 2, t, d), BF16),
            pltpu.VMEM((2, e, d), BF16),
            pltpu.VMEM((2, d, 512), BF16),
            pltpu.VMEM((16, 128, 128), BF16),
            pltpu.VMEM((2, e, d), BF16),
            pltpu.VMEM((2, e, d), BF16),
            pltpu.VMEM((2, e, 1), F32),
            pltpu.VMEM((2, e, 1), F32),
            pltpu.VMEM((2 * e, d), BF16),
            pltpu.VMEM((2, e, 512), BF16),
            pltpu.VMEM((2, e, d), BF16),
            pltpu.VMEM((2, e, d), BF16),
            pltpu.VMEM((8, 2, t, 1152), BF16),
            pltpu.VMEM((2, 4, 2, t, 1536), BF16),
        ]
        + wsh_land(t, 1152)
        + [pltpu.SemaphoreType.DMA((n,)) for n in (7, 6, 4, 4)]
        + WSH_SEMS * 3,
        cid,
        "experts",
        [ANY] * 6,
        [ANY, VMEM] + [ANY] * 7,
        limit=63,
        flops=80 << 30,
    )(x, cot, w_in, w_out, misc, mask)
    return out[0], out[1], out[2:5], out[5:]


def split_dot(a, b, dims):
    high = a.astype(BF16)
    rest = (a - high.astype(F32)).astype(BF16)
    return dot(high, b, dims) + dot(rest, b, dims)


BACK_PLACES = [
    pltpu.VMEM((8, 2, 128, 1024), BF16),
    pltpu.VMEM((128, 1152), BF16),
    pltpu.VMEM((128, 1024), F32),
    pltpu.VMEM((128, 1024), BF16),
    pltpu.VMEM((128, 1024), F32),
    pltpu.VMEM((128, 1024), BF16),
    pltpu.VMEM((128, 1024), BF16),
    pltpu.VMEM((1024, 1024), BF16),
    pltpu.VMEM((128, 1024), BF16),
    pltpu.VMEM((1024, 1024), BF16),
    pltpu.VMEM((8, 256, 1), F32),
    pltpu.VMEM((1024, 128), F32),
    pltpu.VMEM((1024, 128), F32),
    pltpu.VMEM((1024, 1024), BF16),
    pltpu.VMEM((128, 1024), BF16),
    pltpu.VMEM((1024, 2176), BF16),
]


def back_kernel(chosen_r, *rest):
    count = len(BACK_PLACES)
    loaded, rest = rest[:count], rest[count:]
    experts, rest = rest[:7], rest[7:]
    out_o, tgrad_o, gwq_o, gwk_o, gwv_o, gwo_o, grouter_o, gga_o, ggm_o, gin_o, gout_o = rest[:11]
    rest = rest[11:]
    places, rest = rest[:count], rest[count:]
    load, gm, dkv, gkv, gall, p1, p2, p3, c1, c2, f1, f2, rest = *rest[:12], rest[12:]
    kland, sland1, sland2, oland, oland_c, land1, land1_c, land2, land2_c, land3, land3_c, *rest = rest
    metx, sendy, landy, eload, send_e, recv_e, send_y, recv_y, *sems = rest
    pay, back, mid_r, cot, misc, normed_moe, merged, wo, q, kv, lse, cos, sin = places[:13]
    normed_all, tok, w = places[13:]
    own = lax.axis_index("ctx")
    own_rows = pl.ds(pl.multiple_of(own * 128, 128), 128)
    loads = Loads(loaded, places, load, later=range(8, count))
    ea, eb = ctx_place()
    eloads = Loads(experts[:4], [metx.at[0, d] for d in range(3)] + [metx.at[1, 0]], eload, range(4))
    greet(wsh_peers() + ctx_others())
    alongx = {
        step: remote(
            experts[3 + step], metx.at[1, step], send_e, recv_e, step - 1,
            ctx_device(around(ea, step), eb),
        )
        for step in (1, 2, 3)
    }
    for step in (1, 3, 2):
        alongx[step].start()
    acrossy = [
        remote(sendy.at[j], landy.at[j], send_y, recv_y, j, ctx_device(ea, 1 - eb)) for j in range(2)
    ]

    def total(j):
        def part(e):
            return sum(metx[j, d, e].astype(F32) for d in range(3 + j))

        sendy[j] = part(1).astype(BF16)
        acrossy[j].start()
        kept = part(0)
        gin_o[j] = kept[:, :1024]
        gout_o[j] = kept[:, 1024:]

    loads.wait(0)
    out_plan = scatter_wsh_plan(pay, oland, oland_c, sems[:4], wide=True)
    next(out_plan)
    loads.wait(1, 2, 3, 4, 5, 6, 7)
    loads.start(*range(8, 13))
    mid = mid_r[...]
    cells = back[:, 1024:].astype(F32)
    ggates = cells[:, :32] + cells[:, 32:64] + cells[:, 64:96]
    router = misc[0:32, :].astype(BF16)
    chosen = chosen_r[...]
    logits = jnp.where(chosen > 0, dot(normed_moe[...], router, NT), MASKED)
    raised = jnp.exp(logits - jnp.max(logits, 1, keepdims=True)) * chosen
    gates = raised / jnp.sum(raised, 1, keepdims=True)
    glogits = gates * (ggates - jnp.sum(gates * ggates, 1, keepdims=True))
    scale = rms_scale(mid)
    gnormed = back[:, :1024].astype(F32) + split_dot(glogits, router, (((1,), (0,)), ((), ())))
    grouter = split_dot(glogits, normed_moe[...], TN)
    ggain = jnp.sum(gnormed * mid * scale, 0, keepdims=True)
    gmid = cot[...].astype(F32) + norm_back(gnormed * misc[97:98, :], mid, scale)
    branch = gmid.astype(BF16)
    blocks = lambda v: v.astype(BF16).reshape(8, 2, 64, v.shape[1])
    spare = jnp.zeros((95, 1024), F32)
    p1[:, :, :, 1024:] = blocks(jnp.concatenate([grouter, ggain, spare], 0).T)
    p1[:, :, :, :1024] = blocks(dot(merged[...], branch, TN))
    plan1 = scatter_wsh_plan(p1, land1, land1_c, sems[6:10], wide=True)
    next(plan1)
    gm[...] = dot(branch, wo[...], NT).astype(BF16)
    loads.wait(*range(8, 13))
    loads.start(*range(13, count))
    eloads.start(0, 1, 2, 3)
    visible = visible_mask()
    turned = []
    for g in range(8):
        keys = kv[:, g * 64 : g * 64 + 64]
        values = kv[:, 512 + g * 64 : 512 + g * 64 + 64]
        queries, grads = two_heads(q, g), two_heads(gm, g)
        scores = jnp.where(visible, dot(queries, keys, NT) * DH**-0.5, MASKED)
        probs = jnp.exp(scores - lse[g])
        gprobs = dot(grads, values, NT)
        inner = jnp.sum(probs * gprobs, -1, keepdims=True)
        graw = (probs * (gprobs - inner) * DH**-0.5).astype(BF16)
        turned.append(side_by_side(dot(graw, keys)))
        dkv[g * 64 : g * 64 + 64, :] = dot(queries, graw, TN)
        dkv[512 + g * 64 : 512 + g * 64 + 64, :] = dot(grads, probs.astype(BF16), TN)
        if g in (1, 5):
            next(out_plan)
        if g == 3:
            next(plan1)
    for n in range(8):
        at = slice(n * 128, n * 128 + 128)
        gkeys = dkv[:512, at].T
        gkv[n, :, :512] = unrotate(gkeys, wide(cos[at, :], 512), wide(sin[at, :], 512)).astype(BF16)
        gkv[n, :, 512:] = dkv[512:, at].T.astype(BF16)
    partial = gkv[...].reshape(1024, 1024)
    kv_plan = scatter_ctx_plan(gkv, kland, sems[4:6])
    next(kv_plan)
    loads.wait(*range(13, count))
    p2[:, :, :, 1024:] = blocks(dot(normed_all[...], partial, TN))
    c, s = wide(cos[own_rows, :], 1024), wide(sin[own_rows, :], 1024)
    gall[:, :1024] = unrotate(jnp.concatenate(turned, 1), c, s).astype(BF16)
    p2[:, :, :, :1024] = blocks(dot(normed_all[own_rows, :], gall[:, :1024], TN))
    plan2 = scatter_wsh_plan(p2, land2, land2_c, sems[10:14], wide=True)
    next(plan2)
    eloads.wait(0, 1, 2)
    total(0)
    run(kv_plan, plan1, some(plan2, 2), out_plan)
    pair, core = own_pair()
    for r in range(4):
        mine = p1[pair, core, r * 16 : r * 16 + 16, :]
        c1[2 * r] = mine[:, :640]
        c1[2 * r + 1, :, :512] = mine[:, 640:]
        c1[2 * r + 1, :, 512:] = jnp.zeros((16, 128), BF16)
    sum1 = sum_ctx_plan(c1, sland1, f1, sems[18:22])
    next(sum1)
    out_o[...] = (mid + pay[pair, core].astype(F32)).astype(BF16)
    gall[:, 1024:] = gkv[own]
    x = tok[...].astype(F32)
    scale = rms_scale(x)
    gnormed = dot(gall[...], w[:, :2048], NT)
    ggain = jnp.sum(gnormed * x * scale, 0, keepdims=True)
    p3[...] = blocks(jnp.concatenate([ggain, jnp.zeros((127, 1024), F32)], 0).T)
    plan3 = scatter_wsh_plan(p3, land3, land3_c, sems[14:18])
    next(plan3)
    tgrad_o[...] = (gmid + norm_back(gnormed * misc[96:97, :], x, scale)).astype(BF16)
    next(sum1)
    eloads.wait(3)
    for step in (1, 3, 2):
        alongx[step].wait()
    total(1)
    run(plan2, plan3)
    for r in range(4):
        at = slice(r * 16, r * 16 + 16)
        c2[2 * r, :, :1024] = p2[pair, core, at, :1024]
        c2[2 * r, :, 1024:] = p3[pair, core, at, :]
        c2[2 * r + 1, :, :1024] = p2[pair, core, at, 1024:]
        c2[2 * r + 1, :, 1024:] = jnp.zeros((16, 128), BF16)
    run(sum_ctx_plan(c2, sland2, f2, sems[22:26]), sum1)
    small, gain = [], []
    for r in range(4):
        at = slice(r * 16, r * 16 + 16)
        gwo_o[at, :640] = f1[2 * r].astype(F32)
        gwo_o[at, 640:] = f1[2 * r + 1, :, :384].astype(F32)
        small.append(f1[2 * r + 1, :, 384:512])
        gwq_o[at, :] = f2[2 * r, :, :1024].astype(F32)
        gain.append(f2[2 * r, :, 1024:])
        gwk_o[at, :] = f2[2 * r + 1, :, :512].astype(F32)
        gwv_o[at, :] = f2[2 * r + 1, :, 512:1024].astype(F32)
    small = jnp.concatenate(small, 0).astype(F32).T
    grouter_o[...] = small[:32]
    ggm_o[...] = small[32:33]
    gga_o[...] = jnp.concatenate(gain, 0).astype(F32).T[:1]
    for j in range(2):
        acrossy[j].wait()
        gin_o[j] += landy[j, :, :1024].astype(F32)
        gout_o[j] += landy[j, :, 1024:].astype(F32)


def back_half(*args, cid):
    t, d = 128, 1024
    return talk(
        back_kernel,
        [
            ((t, d), BF16), ((t, d), BF16), ((64, d), F32), ((64, 512), F32), ((64, 512), F32),
            ((64, d), F32), ((32, 64), F32), ((1, 64), F32), ((1, 64), F32), ((2, t, d), F32), ((2, t, 512), F32),
        ],
        BACK_PLACES
        + [
            pltpu.SemaphoreType.DMA((len(BACK_PLACES),)),
            pltpu.VMEM((t, d), BF16),
            pltpu.VMEM((d, d), F32),
            pltpu.VMEM((8, t, d), BF16),
            pltpu.VMEM((t, 2048), BF16),
            pltpu.VMEM((8, 2, 64, 1152), BF16),
            pltpu.VMEM((8, 2, 64, 2048), BF16),
            pltpu.VMEM((8, 2, 64, 128), BF16),
            pltpu.VMEM((8, 16, 640), BF16),
            pltpu.VMEM((8, 16, 1152), BF16),
            pltpu.VMEM((8, 16, 640), BF16),
            pltpu.VMEM((8, 16, 1152), BF16),
            pltpu.VMEM((7, t, d), BF16),
            pltpu.VMEM((7, 16, 640), BF16),
            pltpu.VMEM((7, 16, 1152), BF16),
        ]
        + wsh_land(t, d)
        + wsh_land(64, 1152)
        + wsh_land(64, 2048)
        + wsh_land(64, 128)
        + [
            pltpu.VMEM((2, 4, 2, t, 1536), BF16),
            pltpu.VMEM((2, t, 1536), BF16),
            pltpu.VMEM((2, t, 1536), BF16),
        ]
        + [pltpu.SemaphoreType.DMA((n,)) for n in (4, 3, 3, 2, 2)]
        + WSH_SEMS
        + CTX_SEMS
        + WSH_SEMS * 3
        + CTX_SEMS * 4,
        cid,
        "back",
        [VMEM] + [ANY] * (len(BACK_PLACES) + 7),
        limit=63,
        flops=80 << 30,
    )(*args)


def settle(arrays):
    count = len(arrays)

    def kernel(*refs):
        sources, places, held = refs[:count], refs[count : 2 * count], refs[2 * count : 3 * count]
        loads = Loads(sources, held, refs[-2])
        stores = []
        for k in range(count):
            loads.wait(k)
            stores.append(pltpu.make_async_copy(held[k], places[k], refs[-1].at[k]))
            stores[k].start()
        for copy in stores:
            copy.wait()

    return pl.pallas_call(
        kernel,
        out_shape=[jax.ShapeDtypeStruct(v.shape, v.dtype) for v in arrays],
        in_specs=[ANY] * count,
        out_specs=[ANY] * count,
        scratch_shapes=[pltpu.VMEM(v.shape, v.dtype) for v in arrays]
        + [pltpu.SemaphoreType.DMA((count,))] * 2,
        compiler_params=pltpu.CompilerParams(vmem_limit_bytes=62 << 20),
        name="settle",
    )(*arrays)


def local(
    tokens, gain_attn, w_query, w_key, w_value, w_output, gain_moe, w_router, w_in, w_out, routes,
    cotangent,
):
    tok = tokens.reshape(128, 1024)
    cot = cotangent.reshape(128, 1024)
    angles = np.arange(1024)[:, None] * ROPE_BASE ** (-np.arange(DH // 2) * 2.0 / DH)[None, :]
    cos = jnp.asarray(np.tile(np.cos(angles), (1, 4)).astype(np.float32))
    sin = jnp.asarray(np.tile(np.sin(angles), (1, 4)).astype(np.float32))
    w, kv, cot_all, wo, normed_all, q, misc, mask, merged, mid, normed_moe, lse, own_mask = front(
        tok, w_query, w_key, w_value, w_router.T, gain_attn.reshape(1, 64),
        gain_moe.reshape(1, 64), routes.reshape(128, 8).T, cos, sin, cot, w_output.reshape(4, 16, 1024), cid=0
    )
    pay, back, first, second = experts(normed_moe, cot_all, w_in, w_out, misc, mask, 1)

    results = back_half(
        own_mask, pay.reshape(8, 2, 128, 1024), back, mid, cot, misc, normed_moe, merged, wo.reshape(1024, 1024), q,
        kv, lse, cos, sin, normed_all, tok, w, *first, *second, cid=2,
    )
    output, tokens_grad, gwq, gwk, gwv, gwo, grouter, gga, ggm, gin, gout = settle(results)
    return (
        output.reshape(1, 128, 1024),
        tokens_grad.reshape(1, 128, 1024),
        gga.reshape(64),
        gwq,
        gwk,
        gwv,
        gwo,
        ggm.reshape(64),
        grouter.T,
        gin,
        gout,
    )


def solution(mesh):
    return jax.shard_map(
        local,
        mesh=mesh,
        in_specs=(
            P("wsh", "ctx", None),
            P("wsh"),
            P("wsh", None),
            P("wsh", None),
            P("wsh", None),
            P("wsh", None),
            P("wsh"),
            P("wsh", None),
            P("wsh", None, None),
            P("wsh", None, None),
            P("wsh", "ctx", None, None),
            P("wsh", "ctx", None),
        ),
        out_specs=(
            P("wsh", "ctx", None),
            P("wsh", "ctx", None),
            P("wsh"),
            P("wsh", None),
            P("wsh", None),
            P("wsh", None),
            P("wsh", None),
            P("wsh"),
            P("wsh", None),
            P("wsh", "ctx", None),
            P("wsh", "ctx", None),
        ),
        check_vma=False,
    )
```
